32 devices in a mesh: parts: 2 (over y), slab: 16 (over z, x, core).
Axes of the slice: x: 2, y: 2, z: 4, core: 2. Of those that a mesh axis runs over, the one named last changes fastest.
Arguments:
- volume: bfloat16 [32, 32, 512], P(('parts', 'slab')), parts along dimension 0, may hold values from -6 to 6
- tiles: bfloat16 [8, 512, 256], replicated, may hold values from -0.09375 to 0.09375
- slab_ids: int32 [512, 8], P(('parts', 'slab')), parts along dimension 0, may hold values from 0 to 15, all different within a row; in each aligned block of 16 rows (0 to 15, 16 to 31, ...) at most 16 rows name the same one
- tile_ids: int32 [512, 8], P(('parts', 'slab')), parts along dimension 0, may hold values from 0 to 7
- batch_block: int32 [512], P(('parts', 'slab')), parts along dimension 0, may hold values from 0 to 15
- images: bfloat16 [4096, 32, 256], P(('parts', 'slab')), parts along dimension 0, may hold values from -6 to 6
- defocus: float32 [4096], P(('parts', 'slab')), parts along dimension 0, may hold values from 2 to 12
- inv_sigma2: float32 [64, 256], P('parts'), parts along dimension 0, may hold values from 0.3 to 3
Outputs:
- scores: float32 [4096], P(('parts', 'slab')), parts along dimension 0
- data_volume: float32 [32, 32, 512], P(('parts', 'slab')), parts along dimension 0
- weight_volume: float32 [32, 32, 512], P(('parts', 'slab')), parts along dimension 0
The draws below stay inside these ranges and needn't reach their ends.
There are 2 independent parts, one for each index of `parts`. The reference program is written for one: setup_inputs(seed, part) draws one part's arguments, and reference() takes and returns one part's arrays. A program takes and returns all parts, laid end to end along the dimension named above; an argument that names none is the same for every part. Nothing has to cross between parts.
Inputs may be any that keep to these rules, and one draw needn't show every extreme that they name: `slab_ids`: each orientation block names 8 different slabs; among the blocks of one device no slab is named more than 16 times, a bound that some block reaches.
All inputs are finite; a program needn't handle non-finite values.
Results may differ from the reference program's by a relative error of at most 0.0041.
Values may be sent and summed in bfloat16 or wider, within the bound.
No kernel may reach another device: no remote copies, remote signals or barrier semaphores. Data moves between devices by JAX's collectives and lax.ppermute only.
A program may use at most 128 MiB of HBM per device.

```python
import math
import jax
import jax.numpy as jnp
import numpy as np
from jax import lax

L = 512
PX = 256
C = 32
R = 8
NT = 8
BATCH = 8
OB_DEV = 16
IMG_DEV = 128
VSLABS = 16
BLOCKS = 256
IMAGES = 2048
BATCHES = 256
CAP = 16
N_SLAB = 16


def touch_ends(values, key, smallest, high):
    extent = values.shape
    place = [jax.random.randint(jax.random.fold_in(key, axis), (), 0, extent[axis]) for axis in range(len(extent))]
    values = values.at[tuple(place)].set(smallest)
    longest = extent.index(max(extent))
    place[longest] = (place[longest] + 1) % extent[longest]
    return values.at[tuple(place)].set(high)


def block_scale(stream_key, shape, cuts, least, top_value):
    gain, own = 1.0, jax.random.fold_in(stream_key, 6)
    for axis_at, parts in cuts:
        steps = jnp.exp(jax.random.uniform(jax.random.fold_in(own, axis_at), (parts,), jnp.float32, least / len(cuts), top_value / len(cuts)))
        gain = gain * jnp.repeat(steps, shape[axis_at] // parts).reshape([-1 if axis == axis_at else 1 for axis in range(len(shape))])
    return gain


def assign_block(key, own, number, rows, number_of, top, reach, skew):
    order = jax.random.permutation(key, number_of)
    crowded, ordinary = shares(number_of, rows * top, reach, skew, True), shares(number_of, rows * top, reach, skew, False)
    places = jnp.arange(number_of)

    def named(lengths, offset_by):
        used = int((lengths > 0).sum())
        fixed = max(1, used // 4)
        passed = fixed + (places - fixed + offset_by * (used - fixed)) % max(1, number_of - fixed)
        return jnp.zeros((number_of,), jnp.int32).at[order[jnp.where(places < fixed, places, passed)]].set(jnp.asarray(lengths, jnp.int32))

    lengths = jnp.where(number % 4 == 0, named(crowded, number // 4), named(ordinary, number - number // 4 - 1))
    mixed = jax.random.permutation(jax.random.fold_in(own, 3), number_of)
    source_of, taker = mixed[0:number_of // 2 * 2:2], mixed[1:number_of // 2 * 2:2]
    room = jnp.minimum(lengths[source_of] - 1, reach - lengths[taker]) // 2
    room = jnp.where((source_of == order[0]) | (taker == order[0]) | (lengths[taker] == 0), 0, jnp.maximum(room, 0))
    passed = jax.random.randint(jax.random.fold_in(own, 4), (number_of // 2,), 0, 1 << 20) % (room + 1)
    lengths = lengths.at[source_of].add(-passed).at[taker].add(passed)
    items = jnp.searchsorted(jnp.cumsum(lengths), jnp.arange(rows * top), side="right").astype(jnp.int32)
    table = items.reshape(top, rows).T
    table = table[jax.random.permutation(jax.random.fold_in(own, 1), rows)]
    offset_by = jax.random.randint(jax.random.fold_in(own, 2), (rows, 1), 0, top)
    return jnp.take_along_axis(table, (jnp.arange(top)[None, :] + offset_by) % top, axis=1)


def shares(amount, total, reach, skew, full):
    weights = [(1 << 20) // math.isqrt(rank ** skew) + 1 for rank in range(1, amount + 1)]
    largest = reach if full else min(reach, max(-(-total // amount), total * weights[0] // sum(weights)))
    least = 1 if total - largest >= amount - 1 else 0
    given, rest = [largest] + [least] * (amount - 1), total - largest - least * (amount - 1)
    while rest > 0:
        free = [i for i in range(1, amount) if given[i] < largest] or [i for i in range(1, amount) if given[i] < reach]
        mass, budget = sum([weights[i] for i in free]), rest
        for i in free:
            extra = min(reach - given[i], max(1, budget * weights[i] // mass), rest)
            given[i] = given[i] + extra
            rest = rest - extra
    return np.array(given)


def bell_draw(key, dims, spread, bound, cuts=(), dtype=jnp.bfloat16):
    result = jax.random.normal(key, dims, jnp.float32) * spread
    if len(cuts) > 0:
        result = block_scale(key, dims, cuts, -0.22, 0.18) * result
    return jnp.clip(result, min=-bound, max=bound).astype(dtype)


def setup_inputs(seed: int = 0, part: int = 0) -> dict:
    key_of = jax.random.split(jax.random.key(seed), 9)
    part_splits = jax.random.split(jax.random.fold_in(key_of[8], part), 9)
    volume = bell_draw(part_splits[0], (VSLABS, C, L), 1.0, 6.0, ((0, 16),))
    tiles = bell_draw(key_of[1], (NT, L, PX), (R * L) ** -0.5, 0.09375)
    slab_ids_keys = jax.random.split(jax.random.fold_in(part_splits[2], 1), BLOCKS // OB_DEV)
    slab_ids_turns = jax.random.permutation(jax.random.fold_in(part_splits[2], 3), BLOCKS // OB_DEV)
    slab_ids = jax.vmap(lambda own, number: assign_block(jax.random.fold_in(part_splits[2], 2), own, number, OB_DEV, VSLABS, R, CAP, 2))(slab_ids_keys, slab_ids_turns).reshape((BLOCKS, R))
    tile_ids = touch_ends(jax.random.randint(part_splits[3], (BLOCKS, R), 0, NT), jax.random.fold_in(part_splits[3], 1), 0, NT - 1).astype(jnp.int32)
    batch_block = touch_ends(jax.random.randint(part_splits[4], (BATCHES,), 0, OB_DEV), jax.random.fold_in(part_splits[4], 1), 0, OB_DEV - 1).astype(jnp.int32)
    images = bell_draw(part_splits[5], (IMAGES, C, PX), 1.0, 6.0, ((0, 16),))
    defocus = jnp.clip(2.0 + 10.0 * jax.random.uniform(part_splits[6], (IMAGES,), jnp.float32) ** block_scale(part_splits[6], (IMAGES,), ((0, 16),), -0.2, 0.2), 2.0, 12.0)
    inv_sigma2 = jnp.clip(jnp.exp(jax.random.uniform(part_splits[7], (C, PX), jnp.float32, math.log(0.3), math.log(3.0))), 0.3, 3.0)
    return {"volume": volume, "tiles": tiles, "slab_ids": slab_ids, "tile_ids": tile_ids, "batch_block": batch_block, "images": images, "defocus": defocus, "inv_sigma2": inv_sigma2}


def wave_factor(defocus_row, height, pixels):
    line_pos = (jnp.arange(height) // 2 + 1).astype(jnp.float32) / (height // 2)
    pixel_pos = (jnp.arange(pixels) + 1).astype(jnp.float32) / pixels
    radius = line_pos[:, None] ** 2 + pixel_pos[None, :] ** 2
    return jnp.sin(defocus_row[:, None, None] * radius[None] + 0.3)


def reference(volume, tiles, slab_ids, tile_ids, batch_block, images, defocus, inv_sigma2):
    slab_rows = slab_ids.reshape(N_SLAB, OB_DEV * R)
    tile_rows = tile_ids.reshape(N_SLAB, OB_DEV * R)
    block_rows = batch_block.reshape(N_SLAB, IMG_DEV // BATCH)
    image_rows = images.reshape(N_SLAB, IMG_DEV, C, PX)
    defocus_rows = defocus.reshape(N_SLAB, IMG_DEV)

    def device_step(buffer, inputs):
        data_acc, weight_acc = buffer
        slab_list, tile_list, block_list, pictures, defocus_row = inputs
        chosen = volume[slab_list].astype(jnp.float32)
        kernels = tiles[tile_list].astype(jnp.float32)
        projection = jnp.einsum('icl,ilp->icp', chosen, kernels).reshape(OB_DEV, R, C, PX).sum(axis=1)
        contrast = wave_factor(defocus_row, C, PX)
        owners = jnp.repeat(block_list, BATCH)
        pictures32 = pictures.astype(jnp.float32)
        residual = pictures32 - contrast * projection[owners]
        scores = jnp.mean(residual * residual * inv_sigma2, axis=(1, 2))
        member = (owners[:, None] == jnp.arange(OB_DEV)[None, :]).astype(jnp.float32)
        data_sums = jnp.einsum('io,icp->ocp', member, contrast * pictures32 * inv_sigma2,
                               precision=lax.Precision.HIGHEST).astype(jnp.bfloat16)
        weight_sums = jnp.einsum('io,icp->ocp', member, contrast * contrast * inv_sigma2,
                                 precision=lax.Precision.HIGHEST).astype(jnp.bfloat16)
        stacked = jnp.stack([data_sums, weight_sums]).astype(jnp.float32)
        per_item = jnp.repeat(stacked, R, axis=1)
        partials = jnp.einsum('kicp,ilp->kicl', per_item, kernels)
        partials = lax.optimization_barrier(partials.astype(jnp.bfloat16)).astype(jnp.float32)
        data_acc = data_acc.at[slab_list].add(partials[0])
        weight_acc = weight_acc.at[slab_list].add(partials[1])
        return (data_acc, weight_acc), scores

    start_acc = (jnp.zeros((VSLABS, C, L), jnp.float32), jnp.zeros((VSLABS, C, L), jnp.float32))
    (data_volume, weight_volume), scores = lax.scan(
        device_step, start_acc, (slab_rows, tile_rows, block_rows, image_rows, defocus_rows))
    return scores.reshape(IMAGES), data_volume, weight_volume
```

```python
import functools

import jax
import jax.numpy as jnp
from jax import lax
from jax.experimental import pallas as pl
from jax.experimental.pallas import tpu as pltpu
from jax.sharding import PartitionSpec as P

LANES = 128
CHUNKS = 4
VMEM_BYTES = 48 * 1024 * 1024


def grid_of(devices):
    cores = 2 if devices % 2 == 0 else 1
    chips = devices // cores
    wide = 1
    while (2 * wide) ** 3 <= chips:
        wide *= 2
    return chips // wide, wide, cores


def sin_cos(angle):
    turns = jnp.floor(angle * 0.3183098861837907 + 0.5)
    rest = angle - turns * 3.140625
    rest = rest - turns * 9.675025939941406e-4
    rest = rest - turns * 1.5099580252808664e-7
    half = turns * 0.5
    sign = 1.0 - 4.0 * (half - jnp.floor(half))
    sq = rest * rest
    sin = rest * (1.0 + sq * (-1.0 / 6 + sq * (1.0 / 120 + sq * (-1.0 / 5040 + sq * (1.0 / 362880 + sq * (-1.0 / 39916800))))))
    cos = 1.0 + sq * (-0.5 + sq * (1.0 / 24 + sq * (-1.0 / 720 + sq * (1.0 / 40320 + sq * (-1.0 / 3628800 + sq * (1.0 / 479001600))))))
    return sign * sin, sign * cos


def tables(defocus_ref, height, repeat, pixels, line_ref, pixel_ref):
    images = defocus_ref.shape[1]
    defocus = defocus_ref[...]
    rows = lax.broadcasted_iota(jnp.int32, (height * repeat, images), 0)
    line = ((rows // repeat + 1).astype(jnp.float32) / height) ** 2
    line_ref[0], line_ref[1] = sin_cos(defocus * line + 0.3)
    column = jnp.transpose(jnp.broadcast_to(defocus, (LANES, images)))
    column = jnp.concatenate([column] * (pixels // LANES), axis=1)
    lanes = lax.broadcasted_iota(jnp.int32, (images, pixels), 1)
    pixel = ((lanes + 1).astype(jnp.float32) / pixels) ** 2
    pixel_ref[0], pixel_ref[1] = sin_cos(column * pixel)


def lines_of(line_ref, batch, size):
    images = line_ref.shape[2]
    shift = lax.rem(images - batch * size, images)
    return pltpu.roll(line_ref[0], shift, 1), pltpu.roll(line_ref[1], shift, 1)


def contrast_of(lines, pixel_ref, batch, size, j):
    sin_line, cos_line = lines
    row = pl.ds(batch * size + j, 1)
    return sin_line[:, j : j + 1] * pixel_ref[1, row, :] + cos_line[:, j : j + 1] * pixel_ref[0, row, :]


def clear_lists(count_ref):
    def clear(s, carry):
        count_ref[s] = 0
        return carry

    lax.fori_loop(0, count_ref.shape[0], clear, 0)


def list_block(k, slab_ref, tile_ref, count_ref, list_ref):
    crossed, blocks = slab_ref.shape
    for r in range(crossed):
        s = slab_ref[r, k]
        at = count_ref[s]
        list_ref[s * blocks + at] = k * 256 + tile_ref[r, k]
        count_ref[s] = at + 1


def insert(sums, tiles_ref, parts_ref, count_ref, list_ref, keep_ref, send_ref, height, shape):
    far, wide, cores = shape
    blocks = sums.shape[0] // height
    devices = count_ref.shape[0]
    for t in range(tiles_ref.shape[0]):
        parts_ref[t] = lax.dot_general(
            sums, tiles_ref[t], (((1,), (1,)), ((), ())), preferred_element_type=jnp.float32
        ).astype(jnp.bfloat16)
    me = lax.axis_index("slab")

    def total(slot, core):
        x, z = slot // far, lax.rem(slot, far)
        s = me ^ ((z * wide + x) * cores + core)

        def add(m, acc):
            item = list_ref[s * blocks + m]
            k, t = item // 256, lax.rem(item, 256)
            rows = pl.ds(pl.multiple_of(k * height, height), height)
            return acc + parts_ref[t, rows, :].astype(jnp.float32)

        zero = jnp.zeros((height, parts_ref.shape[2]), jnp.float32)
        return lax.fori_loop(0, count_ref[s], add, zero)

    def send(slot, carry):
        send_ref[slot] = total(slot, 1).astype(jnp.bfloat16)
        return carry

    def keep(slot, carry):
        keep_ref[slot] = total(slot, 0)
        return carry

    half = devices // 2
    lax.fori_loop(0, half, send, 0)
    lax.fori_loop(0, half, keep, 0)


def weight_kernel(shape, slab_ref, tile_ref, block_ref, defocus_ref, noise_ref, tiles_hbm, keep_ref, send_ref,
                  tiles_ref, line_ref, pixel_ref, sums_ref, wide_ref, parts_ref, count_ref, list_ref, sem):
    copy = pltpu.make_async_copy(tiles_hbm, tiles_ref, sem)
    copy.start()
    height, pixels = noise_ref.shape
    blocks = sums_ref.shape[0]
    batches = block_ref.shape[0]
    size = defocus_ref.shape[1] // batches
    tables(defocus_ref, height // 2, 1, pixels, line_ref, pixel_ref)
    sums_ref[...] = jnp.zeros_like(sums_ref)
    clear_lists(count_ref)

    def batch_step(b, carry):
        lines = lines_of(line_ref, b, size)
        acc = jnp.zeros((height // 2, pixels), jnp.float32)
        for j in range(size):
            wave = contrast_of(lines, pixel_ref, b, size, j)
            acc = acc + wave * wave
        k = block_ref[b]
        sums_ref[k] = sums_ref[k] + acc
        return carry

    def list_step(k, carry):
        list_block(k, slab_ref, tile_ref, count_ref, list_ref)
        return carry

    if blocks == batches:
        lax.fori_loop(0, batches, lambda b, c: list_step(b, batch_step(b, c)), 0)
    else:
        lax.fori_loop(0, batches, batch_step, 0)
        lax.fori_loop(0, blocks, list_step, 0)

    noise = noise_ref[...]
    for k in range(blocks):
        block = sums_ref[k]
        for n in range(pixels // LANES):
            for odd in range(2):
                wide_ref[k, n, pl.ds(odd, height // 2, 2), :] = block[:, n * LANES : (n + 1) * LANES]
    sums = jnp.concatenate([wide_ref[:, n] for n in range(pixels // LANES)], axis=2) * noise[None]
    sums = sums.astype(jnp.bfloat16).reshape(blocks * height, pixels)
    copy.wait()
    insert(sums, tiles_ref, parts_ref, count_ref, list_ref, keep_ref, send_ref, height, shape)


def data_kernel(shape, slab_ref, tile_ref, block_ref, defocus_ref, noise_ref, images_hbm, tiles_hbm, keep_ref, send_ref,
                images_ref, tiles_ref, line_ref, pixel_ref, sums_ref, parts_ref, count_ref, list_ref, sem, chunk_sem):
    height, pixels = noise_ref.shape
    blocks = sums_ref.shape[0]
    batches = block_ref.shape[0]
    size = defocus_ref.shape[1] // batches
    part = images_ref.shape[0] // CHUNKS
    chunk = [
        pltpu.make_async_copy(images_hbm.at[pl.ds(n * part, part)], images_ref.at[pl.ds(n * part, part)], chunk_sem.at[n])
        for n in range(CHUNKS)
    ]
    for c in chunk:
        c.start()
    copy = pltpu.make_async_copy(tiles_hbm, tiles_ref, sem)
    copy.start()
    tables(defocus_ref, height // 2, 2, pixels, line_ref, pixel_ref)
    sums_ref[...] = jnp.zeros_like(sums_ref)
    clear_lists(count_ref)

    def batch_step(b, carry):
        lines = lines_of(line_ref, b, size)
        acc = jnp.zeros((height, pixels), jnp.float32)
        for j in range(size):
            wave = contrast_of(lines, pixel_ref, b, size, j)
            acc = acc + wave * images_ref[b * size + j].astype(jnp.float32)
        k = block_ref[b]
        sums_ref[k] = sums_ref[k] + acc
        return carry

    def list_step(k, carry):
        list_block(k, slab_ref, tile_ref, count_ref, list_ref)
        return carry

    each = batches // CHUNKS
    for n in range(CHUNKS):
        chunk[n].wait()
        if blocks == batches:
            lax.fori_loop(n * each, (n + 1) * each, lambda b, c: list_step(b, batch_step(b, c)), 0)
        else:
            lax.fori_loop(n * each, (n + 1) * each, batch_step, 0)
    if blocks != batches:
        lax.fori_loop(0, blocks, list_step, 0)

    sums = (sums_ref[...] * noise_ref[...][None]).astype(jnp.bfloat16).reshape(blocks * height, pixels)
    copy.wait()
    insert(sums, tiles_ref, parts_ref, count_ref, list_ref, keep_ref, send_ref, height, shape)


def score_kernel(shape, slab_ref, tile_ref, block_ref, defocus_ref, noise_ref, near_ref, other_ref, images_hbm, tiles_hbm,
                 score_ref, images_ref, tiles_ref, line_ref, pixel_ref, flat_ref, proj_ref, part_ref, sem, chunk_sem):
    far, wide, cores = shape
    height, pixels = noise_ref.shape
    crossed, blocks = slab_ref.shape
    batches = block_ref.shape[0]
    size = defocus_ref.shape[1] // batches
    half = near_ref.shape[0]
    copy = pltpu.make_async_copy(tiles_hbm, tiles_ref, sem)
    copy.start()
    load = pltpu.make_async_copy(images_hbm, images_ref, chunk_sem)
    load.start()
    tables(defocus_ref, height // 2, 2, pixels, line_ref, pixel_ref)
    me = lax.axis_index("slab")
    copy.wait()
    dense = 2 * half * tiles_ref.shape[0] <= crossed * blocks

    def slot_of(s):
        away = me ^ s
        core, chip = lax.rem(away, cores), away // cores
        return core * half + lax.rem(chip, wide) * far + chip // wide

    if dense:
        for n, ref in enumerate((near_ref, other_ref)):
            lines = ref[...].reshape(half * height, ref.shape[2])
            for t in range(tiles_ref.shape[0]):
                flat_ref[t, n * half * height : (n + 1) * half * height, :] = jnp.dot(
                    lines, tiles_ref[t], preferred_element_type=jnp.float32
                )
    else:
        flat_ref[0:half] = near_ref[...]
        flat_ref[half : 2 * half] = other_ref[...]

    def project(k, carry):
        acc = jnp.zeros((height, pixels), jnp.float32)
        for r in range(crossed):
            slot, t = slot_of(slab_ref[r, k]), tile_ref[r, k]
            if dense:
                acc = acc + flat_ref[t, pl.ds(pl.multiple_of(slot * height, height), height), :]
            else:
                acc = acc + jnp.dot(flat_ref[slot], tiles_ref[t], preferred_element_type=jnp.float32)
        proj_ref[k] = acc
        return carry

    lax.fori_loop(0, blocks, project, 0)
    load.wait()

    def batch_step(b, carry):
        lines = lines_of(line_ref, b, size)
        k = block_ref[b]
        for j in range(size):
            wave = contrast_of(lines, pixel_ref, b, size, j)
            residual = images_ref[b * size + j].astype(jnp.float32) - wave * proj_ref[k]
            power = jnp.sum(residual * residual * noise_ref[...], axis=0, keepdims=True)
            part_ref[pl.ds(b * size + j, 1), :] = sum(
                power[:, n * LANES : (n + 1) * LANES] for n in range(pixels // LANES)
            )
        return carry

    lax.fori_loop(0, batches, batch_step, 0)
    total = jnp.sum(jnp.transpose(part_ref[...]), axis=0, keepdims=True)
    score_ref[...] = total * (1.0 / (height * pixels))


def on_device(volume, tiles, slab_ids, tile_ids, batch_block, images, defocus, inv_sigma2):
    blocks, crossed = slab_ids.shape
    height, length = volume.shape[1:]
    count, _, pixels = images.shape
    kinds = tiles.shape[0]
    devices = lax.axis_size("slab")
    shape = far, wide, cores = grid_of(devices)
    half = devices // 2
    slabs, kind_rows, row = slab_ids.T, tile_ids.T, defocus.reshape(1, count)

    def swap(array, offset):
        return lax.ppermute(array, "slab", [(i, i ^ offset) for i in range(devices)])

    smem = pl.BlockSpec(memory_space=pltpu.SMEM)
    vmem = pl.BlockSpec(memory_space=pltpu.VMEM)
    hbm = pl.BlockSpec(memory_space=pl.ANY)
    params = pltpu.CompilerParams(vmem_limit_bytes=VMEM_BYTES)
    tiles_scratch = pltpu.VMEM(tiles.shape, jnp.bfloat16)
    pixel_scratch = pltpu.VMEM((2, count, pixels), jnp.float32)
    parts_scratch = pltpu.VMEM((kinds, blocks * height, length), jnp.bfloat16)
    lists = [pltpu.SMEM((devices,), jnp.int32), pltpu.SMEM((devices * blocks,), jnp.int32)]
    sums_out = (
        jax.ShapeDtypeStruct((half, height, length), jnp.float32),
        jax.ShapeDtypeStruct((half, height, length), jnp.bfloat16),
    )
    insert_flops = 2 * blocks * height * pixels * kinds * length

    weight_keep, weight_send = pl.pallas_call(
        functools.partial(weight_kernel, shape),
        out_shape=sums_out,
        in_specs=[smem, smem, smem, vmem, vmem, hbm],
        out_specs=(vmem, vmem),
        scratch_shapes=[
            tiles_scratch,
            pltpu.VMEM((2, height // 2, count), jnp.float32),
            pixel_scratch,
            pltpu.VMEM((blocks, height // 2, pixels), jnp.float32),
            pltpu.VMEM((blocks, pixels // LANES, height, LANES), jnp.float32),
            parts_scratch,
            *lists,
            pltpu.SemaphoreType.DMA,
        ],
        compiler_params=params,
        cost_estimate=pl.CostEstimate(flops=insert_flops, bytes_accessed=4 << 20, transcendentals=0),
        name="weights",
    )(slabs, kind_rows, batch_block, row, inv_sigma2, tiles)

    data_keep, data_send = pl.pallas_call(
        functools.partial(data_kernel, shape),
        out_shape=sums_out,
        in_specs=[smem, smem, smem, vmem, vmem, hbm, hbm],
        out_specs=(vmem, vmem),
        scratch_shapes=[
            pltpu.VMEM(images.shape, jnp.bfloat16),
            tiles_scratch,
            pltpu.VMEM((2, height, count), jnp.float32),
            pixel_scratch,
            pltpu.VMEM((blocks, height, pixels), jnp.float32),
            parts_scratch,
            *lists,
            pltpu.SemaphoreType.DMA,
            pltpu.SemaphoreType.DMA((CHUNKS,)),
        ],
        compiler_params=params,
        cost_estimate=pl.CostEstimate(flops=insert_flops, bytes_accessed=6 << 20, transcendentals=0),
        name="data",
    )(slabs, kind_rows, batch_block, row, inv_sigma2, images, tiles)

    def reduce(keep, send):
        if cores == 2:
            other = swap(send, 1).astype(jnp.float32)
        else:
            other = send.astype(jnp.float32)
        sums = (keep + other).reshape(wide, far, height, length)
        outgoing = (keep + other).reshape(wide, far, height, length)[1:].astype(jnp.bfloat16)
        line = sums[0]
        for x in range(1, wide):
            line = line + swap(outgoing[x - 1], x * cores).astype(jnp.float32)
        total = line[0]
        for z in range(1, far):
            total = total + swap(line[z].astype(jnp.bfloat16), z * wide * cores).astype(jnp.float32)
        return total[None]

    column = jnp.concatenate([volume] + [swap(volume, z * wide * cores) for z in range(1, far)], axis=0)
    near = jnp.concatenate([column] + [swap(column, x * cores) for x in range(1, wide)], axis=0)
    other = swap(near, 1)

    if devices * kinds <= blocks * crossed:
        flat = pltpu.VMEM((kinds, devices * height, pixels), jnp.float32)
    else:
        flat = pltpu.VMEM((devices, height, length), jnp.bfloat16)
    scores = pl.pallas_call(
        functools.partial(score_kernel, shape),
        out_shape=jax.ShapeDtypeStruct((1, count), jnp.float32),
        in_specs=[smem, smem, smem, vmem, vmem, vmem, vmem, hbm, hbm],
        out_specs=vmem,
        scratch_shapes=[
            pltpu.VMEM(images.shape, jnp.bfloat16),
            tiles_scratch,
            pltpu.VMEM((2, height, count), jnp.float32),
            pixel_scratch,
            flat,
            pltpu.VMEM((blocks, height, pixels), jnp.float32),
            pltpu.VMEM((count, LANES), jnp.float32),
            pltpu.SemaphoreType.DMA,
            pltpu.SemaphoreType.DMA,
        ],
        compiler_params=params,
        cost_estimate=pl.CostEstimate(flops=insert_flops // 2, bytes_accessed=5 << 20, transcendentals=0),
        name="scores",
    )(slabs, kind_rows, batch_block, row, inv_sigma2, near, other, images, tiles)

    weight_volume = reduce(weight_keep, weight_send)
    data_volume = reduce(data_keep, data_send)
    return scores.reshape(count), data_volume, weight_volume


def solution(mesh):
    placed = (
        P(("parts", "slab"), None, None),
        P(),
        P(("parts", "slab"), None),
        P(("parts", "slab"), None),
        P(("parts", "slab")),
        P(("parts", "slab"), None, None),
        P(("parts", "slab")),
        P("parts", None),
    )
    return jax.shard_map(
        on_device,
        mesh=mesh,
        in_specs=placed,
        out_specs=(
            P(("parts", "slab")),
            P(("parts", "slab"), None, None),
            P(("parts", "slab"), None, None),
        ),
        check_vma=False,
    )
```

```python
import functools

import jax
import jax.numpy as jnp
from jax import lax
from jax.experimental import pallas as pl
from jax.experimental.pallas import tpu as pltpu
from jax.sharding import PartitionSpec as P

LANES = 128
CHUNKS = 4
VMEM_BYTES = 62 * 1024 * 1024


def grid_of(devices):
    cores = 2 if devices % 2 == 0 else 1
    chips = devices // cores
    wide = 1
    while (2 * wide) ** 3 <= chips:
        wide *= 2
    return chips // wide, wide, cores


def sin_cos(angle):
    turns = jnp.floor(angle * 0.3183098861837907 + 0.5)
    rest = angle - turns * 3.140625
    rest = rest - turns * 9.675025939941406e-4
    rest = rest - turns * 1.5099580252808664e-7
    half = turns * 0.5
    sign = 1.0 - 4.0 * (half - jnp.floor(half))
    sq = rest * rest
    sin = rest * (1.0 + sq * (-1.0 / 6 + sq * (1.0 / 120 + sq * (-1.0 / 5040 + sq * (1.0 / 362880 + sq * (-1.0 / 39916800))))))
    cos = 1.0 + sq * (-0.5 + sq * (1.0 / 24 + sq * (-1.0 / 720 + sq * (1.0 / 40320 + sq * (-1.0 / 3628800 + sq * (1.0 / 479001600))))))
    return sign * sin, sign * cos


def tables(defocus_ref, height, pixels, line_ref, pixel_ref):
    images = defocus_ref.shape[1]
    defocus = defocus_ref[...]
    rows = lax.broadcasted_iota(jnp.int32, (height, images), 0)
    line = ((rows // 2 + 1).astype(jnp.float32) / (height // 2)) ** 2
    line_ref[0], line_ref[1] = sin_cos(defocus * line + 0.3)
    column = jnp.transpose(jnp.broadcast_to(defocus, (LANES, images)))
    part = 32
    lanes = lax.broadcasted_iota(jnp.int32, (part, LANES), 1)
    for n in range(images // part):
        rows = slice(n * part, (n + 1) * part)
        for m in range(pixels // LANES):
            pixel = ((lanes + (m * LANES + 1)).astype(jnp.float32) / pixels) ** 2
            at = slice(m * LANES, (m + 1) * LANES)
            pixel_ref[0, rows, at], pixel_ref[1, rows, at] = sin_cos(column[rows] * pixel)


def contrast_of(line_ref, pixel_ref, i):
    sin_line, cos_line = line_ref[0, :, i : i + 1], line_ref[1, :, i : i + 1]
    return sin_line * pixel_ref[1, i : i + 1, :] + cos_line * pixel_ref[0, i : i + 1, :]


def copies(pairs, sems):
    started = [pltpu.make_async_copy(source, target, sems.at[n]) for n, (source, target) in enumerate(pairs)]
    for copy in started:
        copy.start()
    return started


def image_parts(images_hbm, images_ref):
    part = images_ref.shape[0] // CHUNKS
    return [(images_hbm.at[pl.ds(n * part, part)], images_ref.at[pl.ds(n * part, part)]) for n in range(CHUNKS)]


def insert_kernel(shape, slab_hbm, tile_hbm, block_hbm, defocus_hbm, noise_hbm, tiles_hbm, images_hbm,
                  send_ref, keep_ref, line_ref, pixel_ref,
                  slab_ref, tile_ref, block_ref, defocus_ref, noise_ref, tiles_ref, images_ref,
                  sums_ref, parts_ref, place_ref, sems):
    far, wide, cores = shape
    small = [(defocus_hbm, defocus_ref), (block_hbm, block_ref), (noise_hbm, noise_ref), (slab_hbm, slab_ref), (tile_hbm, tile_ref)]
    started = copies(small + image_parts(images_hbm, images_ref) + [(tiles_hbm, tiles_ref)], sems)
    height, pixels = noise_ref.shape
    crossed, blocks = slab_ref.shape
    kinds = tiles_ref.shape[0]
    rows = blocks * 2 * height
    devices = place_ref.shape[0] // blocks
    batches = block_ref.shape[0]
    size = images_ref.shape[0] // batches
    for copy in started[: len(small)]:
        copy.wait()
    tables(defocus_ref, height, pixels, line_ref, pixel_ref)

    def clear(n, carry):
        for m in range(blocks):
            place_ref[n * blocks + m] = kinds * rows
        return carry

    lax.fori_loop(0, devices, clear, 0, unroll=devices <= 16)
    for k in range(blocks):
        for r in range(crossed):
            place_ref[slab_ref[r, k] * blocks + k] = tile_ref[r, k] * rows + k * 2 * height
    parts_ref[pl.ds(kinds * rows, 2 * height), :] = jnp.zeros((2 * height, parts_ref.shape[1]), jnp.float32)
    sums_ref[...] = jnp.zeros_like(sums_ref)

    for b in range(batches):
        if b % (batches // CHUNKS) == 0:
            started[len(small) + b // (batches // CHUNKS)].wait()
        data = jnp.zeros((height, pixels), jnp.float32)
        weight = jnp.zeros((height, pixels), jnp.float32)
        for j in range(size):
            wave = contrast_of(line_ref, pixel_ref, b * size + j)
            data = data + wave * images_ref[b * size + j].astype(jnp.float32)
            weight = weight + wave * wave
        k = block_ref[b]
        sums_ref[k, 0] = sums_ref[k, 0] + data
        sums_ref[k, 1] = sums_ref[k, 1] + weight

    sums = (sums_ref[...] * noise_ref[...][None, None]).astype(jnp.bfloat16).reshape(rows, pixels)
    started[-1].wait()
    for t in range(kinds):
        parts_ref[t * rows : (t + 1) * rows, :] = lax.dot_general(
            sums, tiles_ref[t], (((1,), (1,)), ((), ())), preferred_element_type=jnp.float32
        )
    me = lax.axis_index("slab")

    def total(slot, core, kind):
        x, z = slot // far, lax.rem(slot, far)
        s = me ^ ((z * wide + x) * cores + core)
        acc = None
        for k in range(blocks):
            at = pl.multiple_of(place_ref[s * blocks + k] + kind * height, height)
            part = parts_ref[pl.ds(at, height), :]
            acc = part if acc is None else acc + part
        return acc

    def send(slot, carry):
        for kind in range(2):
            send_ref[slot, kind] = total(slot, 1, kind).astype(jnp.bfloat16)
        return carry

    def keep(slot, carry):
        for kind in range(2):
            keep_ref[slot, kind] = total(slot, 0, kind)
        return carry

    half = devices // 2
    lax.fori_loop(0, half, send, 0)
    lax.fori_loop(0, half, keep, 0)


def score_kernel(shape, slab_hbm, tile_hbm, block_hbm, noise_hbm, line_hbm, pixel_hbm, near_hbm, other_hbm, images_hbm, tiles_hbm,
                 score_ref,
                 slab_ref, tile_ref, block_ref, noise_ref, line_ref, pixel_ref, slabs_ref, tiles_ref, images_ref,
                 flat_ref, proj_ref, part_ref, sems):
    far, wide, cores = shape
    height, pixels = noise_ref.shape
    crossed, blocks = slab_ref.shape
    batches = block_ref.shape[0]
    size = images_ref.shape[0] // batches
    half = near_hbm.shape[0]
    first = [(near_hbm, slabs_ref.at[pl.ds(0, half)]), (tiles_hbm, tiles_ref), (other_hbm, slabs_ref.at[pl.ds(half, half)]),
             (slab_hbm, slab_ref), (tile_hbm, tile_ref)]
    last = [(block_hbm, block_ref), (noise_hbm, noise_ref), (line_hbm, line_ref), (pixel_hbm, pixel_ref), (images_hbm, images_ref)]
    started = copies(first + last, sems)
    me = lax.axis_index("slab")
    dense = 2 * half * tiles_ref.shape[0] <= crossed * blocks
    for copy in started[: len(first)]:
        copy.wait()

    def slot_of(s):
        away = me ^ s
        core, chip = lax.rem(away, cores), away // cores
        return core * half + lax.rem(chip, wide) * far + chip // wide

    if dense:
        lines = slabs_ref[...].reshape(2 * half * height, slabs_ref.shape[2])
        for t in range(tiles_ref.shape[0]):
            flat_ref[t] = jnp.dot(lines, tiles_ref[t], preferred_element_type=jnp.float32)

    def project(k, carry):
        acc = None
        for r in range(crossed):
            slot, t = slot_of(slab_ref[r, k]), tile_ref[r, k]
            if dense:
                part = flat_ref[t, pl.ds(pl.multiple_of(slot * height, height), height), :]
            else:
                part = jnp.dot(slabs_ref[slot], tiles_ref[t], preferred_element_type=jnp.float32)
            acc = part if acc is None else acc + part
        proj_ref[k] = acc
        return carry

    lax.fori_loop(0, blocks, project, 0, unroll=dense)
    for copy in started[len(first) :]:
        copy.wait()

    for b in range(batches):
        k = block_ref[b]
        for j in range(size):
            i = b * size + j
            residual = images_ref[i].astype(jnp.float32) - contrast_of(line_ref, pixel_ref, i) * proj_ref[k]
            power = jnp.sum(residual * residual * noise_ref[...], axis=0, keepdims=True)
            part_ref[i : i + 1, :] = sum(power[:, n * LANES : (n + 1) * LANES] for n in range(pixels // LANES))
    total = jnp.sum(jnp.transpose(part_ref[...]), axis=0, keepdims=True)
    score_ref[...] = total * (1.0 / (height * pixels))


def on_device(volume, tiles, slab_ids, tile_ids, batch_block, images, defocus, inv_sigma2):
    blocks, crossed = slab_ids.shape
    height, length = volume.shape[1:]
    count, _, pixels = images.shape
    kinds = tiles.shape[0]
    devices = lax.axis_size("slab")
    shape = far, wide, cores = grid_of(devices)
    half = devices // 2
    slabs, kind_rows, row = slab_ids.T, tile_ids.T, defocus.reshape(1, count)

    def swap(array, offset):
        return lax.ppermute(array, "slab", [(i, i ^ offset) for i in range(devices)])

    vmem = pl.BlockSpec(memory_space=pltpu.VMEM)
    hbm = pl.BlockSpec(memory_space=pl.ANY)
    params = pltpu.CompilerParams(vmem_limit_bytes=VMEM_BYTES)
    line_shape, pixel_shape = (2, height, count), (2, count, pixels)
    index_scratch = [pltpu.SMEM((crossed, blocks), jnp.int32), pltpu.SMEM((crossed, blocks), jnp.int32), pltpu.SMEM(batch_block.shape, jnp.int32)]
    noise_scratch = pltpu.VMEM((height, pixels), jnp.float32)
    tiles_scratch = pltpu.VMEM(tiles.shape, jnp.bfloat16)
    images_scratch = pltpu.VMEM(images.shape, jnp.bfloat16)
    insert_flops = 4 * blocks * height * pixels * kinds * length

    send, keep, line, pixel = pl.pallas_call(
        functools.partial(insert_kernel, shape),
        out_shape=(
            jax.ShapeDtypeStruct((half, 2, height, length), jnp.bfloat16),
            jax.ShapeDtypeStruct((half, 2, height, length), jnp.float32),
            jax.ShapeDtypeStruct(line_shape, jnp.float32),
            jax.ShapeDtypeStruct(pixel_shape, jnp.float32),
        ),
        in_specs=[hbm] * 7,
        out_specs=(vmem, vmem, vmem, vmem),
        scratch_shapes=[
            *index_scratch,
            pltpu.VMEM((1, count), jnp.float32),
            noise_scratch,
            tiles_scratch,
            images_scratch,
            pltpu.VMEM((blocks, 2, height, pixels), jnp.float32),
            pltpu.VMEM((kinds * blocks * 2 * height + 2 * height, length), jnp.float32),
            pltpu.SMEM((devices * blocks,), jnp.int32),
            pltpu.SemaphoreType.DMA((CHUNKS + 6,)),
        ],
        compiler_params=params,
        cost_estimate=pl.CostEstimate(flops=insert_flops, bytes_accessed=6 << 20, transcendentals=0),
        name="insert",
    )(slabs, kind_rows, batch_block, row, inv_sigma2, tiles, images)

    column = jnp.concatenate([volume] + [swap(volume, z * wide * cores) for z in range(1, far)], axis=0)
    near = jnp.concatenate([column] + [swap(column, x * cores) for x in range(1, wide)], axis=0)
    other = swap(near, 1)

    if devices * kinds <= blocks * crossed:
        flat = pltpu.VMEM((kinds, devices * height, pixels), jnp.float32)
    else:
        flat = pltpu.VMEM((8, LANES), jnp.float32)
    scores = pl.pallas_call(
        functools.partial(score_kernel, shape),
        out_shape=jax.ShapeDtypeStruct((1, count), jnp.float32),
        in_specs=[hbm] * 10,
        out_specs=vmem,
        scratch_shapes=[
            *index_scratch,
            noise_scratch,
            pltpu.VMEM(line_shape, jnp.float32),
            pltpu.VMEM(pixel_shape, jnp.float32),
            pltpu.VMEM((devices, height, length), jnp.bfloat16),
            tiles_scratch,
            images_scratch,
            flat,
            pltpu.VMEM((blocks, height, pixels), jnp.float32),
            pltpu.VMEM((count, LANES), jnp.float32),
            pltpu.SemaphoreType.DMA((10,)),
        ],
        compiler_params=params,
        cost_estimate=pl.CostEstimate(flops=insert_flops // 4, bytes_accessed=5 << 20, transcendentals=0),
        name="scores",
    )(slabs, kind_rows, batch_block, inv_sigma2, line, pixel, near, other, images, tiles)

    sums = (keep + swap(send, 1).astype(jnp.float32)).reshape(wide, far, 2, height, length)
    mine = sums[0]
    for x in range(1, wide):
        mine = mine + swap(sums[x].astype(jnp.bfloat16), x * cores).astype(jnp.float32)
    total = mine[0]
    for z in range(1, far):
        total = total + swap(mine[z].astype(jnp.bfloat16), z * wide * cores).astype(jnp.float32)
    return scores.reshape(count), total[0:1], total[1:2]


def solution(mesh):
    placed = (
        P(("parts", "slab"), None, None),
        P(),
        P(("parts", "slab"), None),
        P(("parts", "slab"), None),
        P(("parts", "slab")),
        P(("parts", "slab"), None, None),
        P(("parts", "slab")),
        P("parts", None),
    )
    return jax.shard_map(
        on_device,
        mesh=mesh,
        in_specs=placed,
        out_specs=(
            P(("parts", "slab")),
            P(("parts", "slab"), None, None),
            P(("parts", "slab"), None, None),
        ),
        check_vma=False,
    )
```

```python
import functools

import jax
import jax.numpy as jnp
from jax import lax
from jax.experimental import pallas as pl
from jax.experimental.pallas import tpu as pltpu
from jax.sharding import PartitionSpec as P

LANES = 128
CHUNKS = 4
VMEM_BYTES = 32 * 1024 * 1024


def grid_of(devices):
    cores = 2 if devices % 2 == 0 else 1
    chips = devices // cores
    wide = 1
    while (2 * wide) ** 3 <= chips:
        wide *= 2
    return chips // wide, wide, cores


def sin_cos(angle):
    turns = jnp.floor(angle * 0.3183098861837907 + 0.5)
    rest = angle - turns * 3.140625
    rest = rest - turns * 9.675025939941406e-4
    rest = rest - turns * 1.5099580252808664e-7
    half = turns * 0.5
    sign = 1.0 - 4.0 * (half - jnp.floor(half))
    sq = rest * rest
    sin = rest * (1.0 + sq * (-1.0 / 6 + sq * (1.0 / 120 + sq * (-1.0 / 5040 + sq * (1.0 / 362880 + sq * (-1.0 / 39916800))))))
    cos = 1.0 + sq * (-0.5 + sq * (1.0 / 24 + sq * (-1.0 / 720 + sq * (1.0 / 40320 + sq * (-1.0 / 3628800 + sq * (1.0 / 479001600))))))
    return sign * sin, sign * cos


def tables(defocus_ref, height, pixels, line_ref, pixel_ref):
    images = defocus_ref.shape[1]
    defocus = defocus_ref[...]
    rows = lax.broadcasted_iota(jnp.int32, (height, images), 0)
    line = ((rows // 2 + 1).astype(jnp.float32) / (height // 2)) ** 2
    line_ref[0], line_ref[1] = sin_cos(defocus * line + 0.3)
    column = jnp.transpose(jnp.broadcast_to(defocus, (LANES, images)))
    part = 32
    lanes = lax.broadcasted_iota(jnp.int32, (part, LANES), 1)
    for n in range(images // part):
        rows = slice(n * part, (n + 1) * part)
        for m in range(pixels // LANES):
            pixel = ((lanes + (m * LANES + 1)).astype(jnp.float32) / pixels) ** 2
            at = slice(m * LANES, (m + 1) * LANES)
            pixel_ref[0, rows, at], pixel_ref[1, rows, at] = sin_cos(column[rows] * pixel)


def contrast_of(line_ref, pixel_ref, i):
    sin_line, cos_line = line_ref[0, :, i : i + 1], line_ref[1, :, i : i + 1]
    return sin_line * pixel_ref[1, i : i + 1, :] + cos_line * pixel_ref[0, i : i + 1, :]


def copies(pairs, sems):
    started = [pltpu.make_async_copy(source, target, sems.at[n]) for n, (source, target) in enumerate(pairs)]
    for copy in started:
        copy.start()
    return started


def sum_kernel(block_hbm, defocus_hbm, noise_hbm, tiles_hbm, images_hbm,
               sums_ref, wave_ref, tiles_ref, images_ref,
               block_ref, defocus_ref, noise_ref, line_ref, pixel_ref, acc_ref, sems):
    count = images_ref.shape[0]
    part = count // CHUNKS
    small = [(defocus_hbm, defocus_ref), (block_hbm, block_ref), (noise_hbm, noise_ref)]
    large = [(images_hbm.at[pl.ds(n * part, part)], images_ref.at[pl.ds(n * part, part)]) for n in range(CHUNKS)]
    started = copies(small + large + [(tiles_hbm, tiles_ref)], sems)
    height, pixels = noise_ref.shape
    batches = block_ref.shape[0]
    size = count // batches
    acc_ref[...] = jnp.zeros_like(acc_ref)
    for copy in started[: len(small)]:
        copy.wait()
    tables(defocus_ref, height, pixels, line_ref, pixel_ref)
    for b in range(batches):
        if b % (batches // CHUNKS) == 0:
            started[len(small) + b // (batches // CHUNKS)].wait()
        data = jnp.zeros((height, pixels), jnp.float32)
        weight = jnp.zeros((height, pixels), jnp.float32)
        for j in range(size):
            i = b * size + j
            wave = contrast_of(line_ref, pixel_ref, i)
            wave_ref[i] = wave
            data = data + wave * images_ref[i].astype(jnp.float32)
            weight = weight + wave * wave
        k = block_ref[b]
        acc_ref[k, 0] = acc_ref[k, 0] + data
        acc_ref[k, 1] = acc_ref[k, 1] + weight
    sums = (acc_ref[...] * noise_ref[...][None, None]).astype(jnp.bfloat16)
    sums_ref[...] = sums.reshape(sums_ref.shape)
    started[-1].wait()


def insert_kernel(shape, slab_hbm, tile_hbm, sums_ref, tiles_ref, send_ref, far_ref, near_ref,
                  slab_ref, tile_ref, parts_ref, place_ref, sems):
    far, wide, cores = shape
    started = copies([(slab_hbm, slab_ref), (tile_hbm, tile_ref)], sems)
    crossed, blocks = slab_ref.shape
    kinds = tiles_ref.shape[0]
    rows = sums_ref.shape[0]
    height = rows // (2 * blocks)
    devices = place_ref.shape[0] // blocks

    def clear(n, carry):
        for m in range(blocks):
            place_ref[n * blocks + m] = kinds * rows
        return carry

    lax.fori_loop(0, devices, clear, 0, unroll=devices <= 16)
    for copy in started:
        copy.wait()
    for k in range(blocks):
        for r in range(crossed):
            place_ref[slab_ref[r, k] * blocks + k] = tile_ref[r, k] * rows + k * 2 * height
    parts_ref[pl.ds(kinds * rows, 2 * height), :] = jnp.zeros((2 * height, parts_ref.shape[1]), jnp.float32)
    for t in range(kinds):
        parts_ref[t * rows : (t + 1) * rows, :] = lax.dot_general(
            sums_ref[...], tiles_ref[t], (((1,), (1,)), ((), ())), preferred_element_type=jnp.float32
        )
    me = lax.axis_index("slab")

    def total(x, z, core, kind):
        s = me ^ ((z * wide + x) * cores + core)
        acc = None
        for k in range(blocks):
            at = pl.multiple_of(place_ref[s * blocks + k] + kind * height, height)
            part = parts_ref[pl.ds(at, height), :]
            acc = part if acc is None else acc + part
        return acc

    def fill(ref, start, core):
        def step(slot, carry):
            x, z = start + slot // far, lax.rem(slot, far)
            for kind in range(2):
                ref[slot, kind] = total(x, z, core, kind).astype(ref.dtype)
            return carry

        lax.fori_loop(0, ref.shape[0], step, 0)

    fill(send_ref, 0, 1)
    fill(far_ref, 1, 0)
    fill(near_ref, 0, 0)


def score_kernel(shape, slab_hbm, tile_hbm, block_hbm, noise_hbm, wave_ref, near_ref, other_ref, images_ref, tiles_ref,
                 score_ref, slab_ref, tile_ref, block_ref, noise_ref, flat_ref, proj_ref, part_ref, sems):
    far, wide, cores = shape
    started = copies([(slab_hbm, slab_ref), (tile_hbm, tile_ref), (block_hbm, block_ref), (noise_hbm, noise_ref)], sems)
    height, pixels = noise_ref.shape
    crossed, blocks = slab_ref.shape
    batches = block_ref.shape[0]
    count = images_ref.shape[0]
    size = count // batches
    half = near_ref.shape[0]
    me = lax.axis_index("slab")
    dense = 2 * half * tiles_ref.shape[0] <= crossed * blocks

    def slot_of(s):
        away = me ^ s
        core, chip = lax.rem(away, cores), away // cores
        return core * half + lax.rem(chip, wide) * far + chip // wide

    for n, ref in enumerate((near_ref, other_ref)):
        lines = ref[...].reshape(half * height, ref.shape[2])
        if dense:
            for t in range(tiles_ref.shape[0]):
                flat_ref[t, n * half * height : (n + 1) * half * height, :] = jnp.dot(
                    lines, tiles_ref[t], preferred_element_type=jnp.float32
                )
        else:
            flat_ref[n * half * height : (n + 1) * half * height, :] = lines
    for copy in started:
        copy.wait()

    def project(k, carry):
        acc = None
        for r in range(crossed):
            t = tile_ref[r, k]
            rows = pl.ds(pl.multiple_of(slot_of(slab_ref[r, k]) * height, height), height)
            if dense:
                part = flat_ref[t, rows, :]
            else:
                part = jnp.dot(flat_ref[rows, :], tiles_ref[t], preferred_element_type=jnp.float32)
            acc = part if acc is None else acc + part
        proj_ref[k] = acc
        return carry

    lax.fori_loop(0, blocks, project, 0, unroll=dense)
    for b in range(batches):
        k = block_ref[b]
        for j in range(size):
            i = b * size + j
            residual = images_ref[i].astype(jnp.float32) - wave_ref[i] * proj_ref[k]
            power = residual * residual * noise_ref[...]
            power = sum(power[n * 8 : (n + 1) * 8] for n in range(height // 8))
            part_ref[i * 8 : (i + 1) * 8, :] = sum(power[:, n * LANES : (n + 1) * LANES] for n in range(pixels // LANES))
    total = sum(part_ref[pl.ds(n, count, 8), :] for n in range(8))
    total = jnp.sum(jnp.transpose(total), axis=0, keepdims=True)
    score_ref[...] = total * (1.0 / (height * pixels))


def on_device(volume, tiles, slab_ids, tile_ids, batch_block, images, defocus, inv_sigma2):
    blocks, crossed = slab_ids.shape
    height, length = volume.shape[1:]
    count, _, pixels = images.shape
    kinds = tiles.shape[0]
    devices = lax.axis_size("slab")
    shape = far, wide, cores = grid_of(devices)
    half = devices // 2
    rows = blocks * 2 * height
    slabs, kind_rows, row = slab_ids.T, tile_ids.T, defocus.reshape(1, count)

    def swap(array, offset):
        return lax.ppermute(array, "slab", [(i, i ^ offset) for i in range(devices)])

    vmem = pl.BlockSpec(memory_space=pltpu.VMEM)
    hbm = pl.BlockSpec(memory_space=pltpu.HBM)
    params = pltpu.CompilerParams(vmem_limit_bytes=VMEM_BYTES)
    f32, bf16 = jnp.float32, jnp.bfloat16
    pairs_scratch = [pltpu.SMEM((crossed, blocks), jnp.int32), pltpu.SMEM((crossed, blocks), jnp.int32)]
    block_scratch = pltpu.SMEM(batch_block.shape, jnp.int32)
    noise_scratch = pltpu.VMEM((height, pixels), f32)

    def call(kernel, outs, inputs, operands, scratch, flops, moved, name):
        operands = [
            pltpu.with_memory_space_constraint(x, pltpu.HBM) if spec is hbm else x for x, spec in zip(operands, inputs)
        ]
        return pl.pallas_call(
            kernel,
            out_shape=tuple(jax.ShapeDtypeStruct(s, t) for s, t in outs),
            in_specs=inputs,
            out_specs=(vmem,) * len(outs),
            scratch_shapes=scratch,
            compiler_params=params,
            cost_estimate=pl.CostEstimate(flops=flops, bytes_accessed=moved, transcendentals=0),
            name=name,
        )(*operands)

    column = jnp.concatenate([volume] + [swap(volume, z * wide * cores) for z in range(1, far)], axis=0)

    sums, wave, tiles_near, images_near = call(
        sum_kernel,
        [((rows, pixels), bf16), (images.shape, f32), (tiles.shape, bf16), (images.shape, bf16)],
        [hbm] * 5,
        (batch_block, row, inv_sigma2, tiles, images),
        [
            block_scratch,
            pltpu.VMEM((1, count), f32),
            noise_scratch,
            pltpu.VMEM((2, height, count), f32),
            pltpu.VMEM((2, count, pixels), f32),
            pltpu.VMEM((blocks, 2, height, pixels), f32),
            pltpu.SemaphoreType.DMA((CHUNKS + 4,)),
        ],
        0,
        10 << 20,
        "sums",
    )
    sums, column = lax.optimization_barrier((sums, column))
    near = jnp.concatenate([column] + [swap(column, x * cores) for x in range(1, wide)], axis=0)

    place = (2, height, length)
    send, keep_far, keep_near = call(
        functools.partial(insert_kernel, shape),
        [((half, *place), bf16), (((wide - 1) * far, *place), f32), ((far, *place), f32)],
        [hbm, hbm, vmem, vmem],
        (slabs, kind_rows, sums, tiles_near),
        [
            *pairs_scratch,
            pltpu.VMEM((kinds * rows + 2 * height, length), f32),
            pltpu.SMEM((devices * blocks,), jnp.int32),
            pltpu.SemaphoreType.DMA((2,)),
        ],
        2 * rows * pixels * kinds * length,
        8 << 20,
        "insert",
    )
    send, near = lax.optimization_barrier((send, near))
    other = swap(near, 1)
    mate = swap(send, 1)
    beyond = (keep_far + mate[far:].astype(f32)).astype(bf16)
    other, beyond = lax.optimization_barrier((other, beyond))

    if devices * kinds <= blocks * crossed:
        flat = pltpu.VMEM((kinds, devices * height, pixels), f32)
    else:
        flat = pltpu.VMEM((devices * height, length), bf16)
    (scores,) = call(
        functools.partial(score_kernel, shape),
        [((1, count), f32)],
        [hbm] * 4 + [vmem] * 5,
        (slabs, kind_rows, batch_block, inv_sigma2, wave, near, other, images_near, tiles_near),
        [
            *pairs_scratch,
            block_scratch,
            noise_scratch,
            flat,
            pltpu.VMEM((blocks, height, pixels), f32),
            pltpu.VMEM((count * 8, LANES), f32),
            pltpu.SemaphoreType.DMA((4,)),
        ],
        2 * devices * height * length * kinds * pixels,
        8 << 20,
        "scores",
    )

    mine = keep_near + mate[:far].astype(f32)
    for x in range(1, wide):
        came, scores = lax.optimization_barrier((swap(beyond[(x - 1) * far : x * far], x * cores), scores))
        mine = mine + came.astype(f32)
    total = mine[0]
    for z in range(1, far):
        total = total + swap(mine[z].astype(bf16), z * wide * cores).astype(f32)
    return scores.reshape(count), total[0:1], total[1:2]


def solution(mesh):
    placed = (
        P(("parts", "slab"), None, None),
        P(),
        P(("parts", "slab"), None),
        P(("parts", "slab"), None),
        P(("parts", "slab")),
        P(("parts", "slab"), None, None),
        P(("parts", "slab")),
        P("parts", None),
    )
    return jax.shard_map(
        on_device,
        mesh=mesh,
        in_specs=placed,
        out_specs=(
            P(("parts", "slab")),
            P(("parts", "slab"), None, None),
            P(("parts", "slab"), None, None),
        ),
        check_vma=False,
    )
```

```python
import functools

import jax
import jax.numpy as jnp
from jax import lax
from jax.experimental import pallas as pl
from jax.experimental.pallas import tpu as pltpu
from jax.sharding import PartitionSpec as P

LANES = 128
CHUNKS = 4
VMEM_BYTES = 32 * 1024 * 1024


def grid_of(devices):
    cores = 2 if devices % 2 == 0 else 1
    chips = devices // cores
    wide = 1
    while (2 * wide) ** 3 <= chips:
        wide *= 2
    return chips // wide, wide, cores


def powers(size):
    return [1 << n for n in range(size.bit_length() - 1)]


def sin_cos(angle):
    turns = jnp.floor(angle * 0.3183098861837907 + 0.5)
    rest = angle - turns * 3.140625
    rest = rest - turns * 9.675025939941406e-4
    rest = rest - turns * 1.5099580252808664e-7
    half = turns * 0.5
    sign = 1.0 - 4.0 * (half - jnp.floor(half))
    sq = rest * rest
    sin = rest * (1.0 + sq * (-1.0 / 6 + sq * (1.0 / 120 + sq * (-1.0 / 5040 + sq * (1.0 / 362880 + sq * (-1.0 / 39916800))))))
    cos = 1.0 + sq * (-0.5 + sq * (1.0 / 24 + sq * (-1.0 / 720 + sq * (1.0 / 40320 + sq * (-1.0 / 3628800 + sq * (1.0 / 479001600))))))
    return sign * sin, sign * cos


def tables(defocus_ref, height, pixels, line_ref, pixel_ref):
    images = defocus_ref.shape[1]
    defocus = defocus_ref[...]
    rows = lax.broadcasted_iota(jnp.int32, (height, images), 0)
    line = ((rows // 2 + 1).astype(jnp.float32) / (height // 2)) ** 2
    line_ref[0], line_ref[1] = sin_cos(defocus * line + 0.3)
    column = jnp.transpose(jnp.broadcast_to(defocus, (LANES, images)))
    part = 32
    lanes = lax.broadcasted_iota(jnp.int32, (part, LANES), 1)
    for n in range(images // part):
        rows = slice(n * part, (n + 1) * part)
        for m in range(pixels // LANES):
            pixel = ((lanes + (m * LANES + 1)).astype(jnp.float32) / pixels) ** 2
            at = slice(m * LANES, (m + 1) * LANES)
            pixel_ref[0, rows, at], pixel_ref[1, rows, at] = sin_cos(column[rows] * pixel)


def contrast_of(line_ref, pixel_ref, i):
    sin_line, cos_line = line_ref[0, :, i : i + 1], line_ref[1, :, i : i + 1]
    return sin_line * pixel_ref[1, i : i + 1, :] + cos_line * pixel_ref[0, i : i + 1, :]


def copies(pairs, sems):
    started = [pltpu.make_async_copy(source, target, sems.at[n]) for n, (source, target) in enumerate(pairs)]
    for copy in started:
        copy.start()
    return started


def sum_kernel(block_hbm, defocus_hbm, noise_hbm, tiles_hbm, images_hbm,
               sums_ref, wave_ref, tiles_ref, images_ref,
               block_ref, defocus_ref, noise_ref, line_ref, pixel_ref, acc_ref, sems):
    count = images_ref.shape[0]
    part = count // CHUNKS
    small = [(defocus_hbm, defocus_ref), (block_hbm, block_ref), (noise_hbm, noise_ref)]
    large = [(images_hbm.at[pl.ds(n * part, part)], images_ref.at[pl.ds(n * part, part)]) for n in range(CHUNKS)]
    started = copies(small + large + [(tiles_hbm, tiles_ref)], sems)
    height, pixels = noise_ref.shape
    batches = block_ref.shape[0]
    size = count // batches
    acc_ref[...] = jnp.zeros_like(acc_ref)
    for copy in started[: len(small)]:
        copy.wait()
    tables(defocus_ref, height, pixels, line_ref, pixel_ref)
    for b in range(batches):
        if b % (batches // CHUNKS) == 0:
            started[len(small) + b // (batches // CHUNKS)].wait()
        data = jnp.zeros((height, pixels), jnp.float32)
        weight = jnp.zeros((height, pixels), jnp.float32)
        for j in range(size):
            i = b * size + j
            wave = contrast_of(line_ref, pixel_ref, i)
            wave_ref[i] = wave
            data = data + wave * images_ref[i].astype(jnp.float32)
            weight = weight + wave * wave
        k = block_ref[b]
        acc_ref[0, k] = acc_ref[0, k] + data
        acc_ref[1, k] = acc_ref[1, k] + weight
    sums = (acc_ref[...] * noise_ref[...][None, None]).astype(jnp.bfloat16)
    sums_ref[...] = sums.reshape(sums_ref.shape)
    started[-1].wait()


def insert_kernel(shape, slab_hbm, tile_hbm, sums_ref, tiles_ref, send_ref, far_ref, near_ref,
                  slab_ref, tile_ref, parts_ref, place_ref, sems):
    far, wide, cores = shape
    started = copies([(slab_hbm, slab_ref), (tile_hbm, tile_ref)], sems)
    crossed, blocks = slab_ref.shape
    kinds, length, _ = tiles_ref.shape
    rows = sums_ref.shape[1]
    height = rows // blocks
    devices = place_ref.shape[0] // blocks
    columns = parts_ref.shape[2]
    per_kind = length // columns
    pieces = [(kind, n * columns) for kind in range(sums_ref.shape[0]) for n in range(per_kind)]
    each = devices // kinds

    def multiply(piece, t):
        kind, start = pieces[piece]
        at = pl.multiple_of(t * rows, rows)
        parts_ref[piece % 2, pl.ds(at, rows), :] = lax.dot_general(
            sums_ref[kind], tiles_ref[t, start : start + columns, :], (((1,), (1,)), ((), ())), preferred_element_type=jnp.float32
        )

    for n in range(2):
        parts_ref[n, pl.ds(kinds * rows, height), :] = jnp.zeros((height, columns), jnp.float32)
    for t in range(kinds // 2):
        multiply(0, t)

    for copy in started:
        copy.wait()

    def clear(n, carry):
        for m in range(blocks):
            place_ref[n * blocks + m] = kinds * rows
        return carry

    lax.fori_loop(0, devices, clear, 0, unroll=devices <= 16)
    for k in range(blocks):
        for r in range(crossed):
            place_ref[slab_ref[r, k] * blocks + k] = tile_ref[r, k] * rows + k * height
    for t in range(kinds // 2, kinds):
        multiply(0, t)

    low = lax.rem(lax.axis_index("slab"), wide * cores)

    def total(piece, x, z, core):
        s = z * wide * cores + (low ^ (x * cores + core))
        acc = None
        for k in range(blocks):
            at = pl.multiple_of(place_ref[s * blocks + k], height)
            part = parts_ref[piece % 2, pl.ds(at, height), :]
            acc = part if acc is None else acc + part
        return acc

    for piece, (kind, start) in enumerate(pieces):
        done = 0
        for ref, first, core in ((send_ref, 0, 1), (far_ref, 1, 0), (near_ref, 0, 0)):

            def step(n, carry, ref=ref, first=first, core=core, done=done, piece=piece, kind=kind, start=start):
                if piece + 1 < len(pieces):
                    multiply(piece + 1, done + n)
                for m in range(each):
                    slot = n * each + m
                    x, z = first + slot // far, lax.rem(slot, far)
                    ref[slot, kind, :, start : start + columns] = total(piece, x, z, core).astype(ref.dtype)
                return carry

            steps = ref.shape[0] // each
            lax.fori_loop(0, steps, step, 0)
            done += steps


def score_kernel(shape, slab_hbm, tile_hbm, block_hbm, noise_hbm, wave_ref, near_ref, other_ref, images_ref, tiles_ref,
                 score_ref, slab_ref, tile_ref, block_ref, noise_ref, flat_ref, proj_ref, part_ref, sems):
    far, wide, cores = shape
    started = copies([(slab_hbm, slab_ref), (tile_hbm, tile_ref), (block_hbm, block_ref), (noise_hbm, noise_ref)], sems)
    height, pixels = noise_ref.shape
    crossed, blocks = slab_ref.shape
    batches = block_ref.shape[0]
    count = images_ref.shape[0]
    size = count // batches
    half = near_ref.shape[0]
    me = lax.axis_index("slab")
    dense = 2 * half * tiles_ref.shape[0] <= crossed * blocks

    def slot_of(s):
        away = me ^ s
        core, chip = lax.rem(away, cores), away // cores
        return core * half + lax.rem(chip, wide) * far + chip // wide

    for n, ref in enumerate((near_ref, other_ref)):
        lines = ref[...].reshape(half * height, ref.shape[2])
        if dense:
            for t in range(tiles_ref.shape[0]):
                flat_ref[t, n * half * height : (n + 1) * half * height, :] = jnp.dot(
                    lines, tiles_ref[t], preferred_element_type=jnp.float32
                )
        else:
            flat_ref[n * half * height : (n + 1) * half * height, :] = lines
    for copy in started:
        copy.wait()

    def project(k, carry):
        acc = None
        for r in range(crossed):
            t = tile_ref[r, k]
            rows = pl.ds(pl.multiple_of(slot_of(slab_ref[r, k]) * height, height), height)
            if dense:
                part = flat_ref[t, rows, :]
            else:
                part = jnp.dot(flat_ref[rows, :], tiles_ref[t], preferred_element_type=jnp.float32)
            acc = part if acc is None else acc + part
        proj_ref[k] = acc
        return carry

    lax.fori_loop(0, blocks, project, 0, unroll=dense)
    for b in range(batches):
        k = block_ref[b]
        for j in range(size):
            i = b * size + j
            residual = images_ref[i].astype(jnp.float32) - wave_ref[i] * proj_ref[k]
            power = residual * residual * noise_ref[...]
            power = sum(power[n * 8 : (n + 1) * 8] for n in range(height // 8))
            part_ref[i * 8 : (i + 1) * 8, :] = sum(power[:, n * LANES : (n + 1) * LANES] for n in range(pixels // LANES))
    total = sum(part_ref[pl.ds(n, count, 8), :] for n in range(8))
    total = jnp.sum(jnp.transpose(total), axis=0, keepdims=True)
    score_ref[...] = total * (1.0 / (height * pixels))


def on_device(volume, tiles, slab_ids, tile_ids, batch_block, images, defocus, inv_sigma2):
    blocks, crossed = slab_ids.shape
    height, length = volume.shape[1:]
    count, _, pixels = images.shape
    kinds = tiles.shape[0]
    devices = lax.axis_size("slab")
    shape = far, wide, cores = grid_of(devices)
    half = devices // 2
    rows = blocks * height
    slabs, kind_rows, row = slab_ids.T, tile_ids.T, defocus.reshape(1, count)

    def swap(array, offset):
        return lax.ppermute(array, "slab", [(i, i ^ offset) for i in range(devices)])

    vmem = pl.BlockSpec(memory_space=pltpu.VMEM)
    hbm = pl.BlockSpec(memory_space=pltpu.HBM)
    params = pltpu.CompilerParams(vmem_limit_bytes=VMEM_BYTES)
    f32, bf16 = jnp.float32, jnp.bfloat16
    pairs_scratch = [pltpu.SMEM((crossed, blocks), jnp.int32), pltpu.SMEM((crossed, blocks), jnp.int32)]
    block_scratch = pltpu.SMEM(batch_block.shape, jnp.int32)
    noise_scratch = pltpu.VMEM((height, pixels), f32)

    def call(kernel, outs, inputs, operands, scratch, flops, moved, name):
        operands = [
            pltpu.with_memory_space_constraint(x, pltpu.HBM) if spec is hbm else x for x, spec in zip(operands, inputs)
        ]
        return pl.pallas_call(
            kernel,
            out_shape=tuple(jax.ShapeDtypeStruct(s, t) for s, t in outs),
            in_specs=inputs,
            out_specs=(vmem,) * len(outs),
            scratch_shapes=scratch,
            compiler_params=params,
            cost_estimate=pl.CostEstimate(flops=flops, bytes_accessed=moved, transcendentals=0),
            name=name,
        )(*operands)

    def hop(array, offset):
        return jnp.concatenate([array, swap(array, offset)], axis=0)

    offsets = [z * wide * cores for z in powers(far)] + [x * cores for x in powers(wide)]
    gathered = hop(volume, offsets[0])

    sums, wave, tiles_near, images_near = call(
        sum_kernel,
        [((2, rows, pixels), bf16), (images.shape, f32), (tiles.shape, bf16), (images.shape, bf16)],
        [hbm] * 5,
        (batch_block, row, inv_sigma2, tiles, images),
        [
            block_scratch,
            pltpu.VMEM((1, count), f32),
            noise_scratch,
            pltpu.VMEM((2, height, count), f32),
            pltpu.VMEM((2, count, pixels), f32),
            pltpu.VMEM((2, blocks, height, pixels), f32),
            pltpu.SemaphoreType.DMA((CHUNKS + 4,)),
        ],
        0,
        10 << 20,
        "sums",
    )
    sums, gathered = lax.optimization_barrier((sums, gathered))
    gathered = hop(gathered, offsets[1])

    place = (2, height, length)
    send, keep_far, keep_near = call(
        functools.partial(insert_kernel, shape),
        [((half, *place), bf16), (((wide - 1) * far, *place), f32), ((far, *place), f32)],
        [hbm, hbm, vmem, vmem],
        (slabs, kind_rows, sums, tiles_near),
        [
            *pairs_scratch,
            pltpu.VMEM((2, kinds * rows + height, length // 2), f32),
            pltpu.SMEM((devices * blocks,), jnp.int32),
            pltpu.SemaphoreType.DMA((2,)),
        ],
        4 * rows * pixels * kinds * length,
        8 << 20,
        "insert",
    )
    send, gathered = lax.optimization_barrier((send, gathered))
    for offset in offsets[2:]:
        gathered = hop(gathered, offset)
    other = swap(gathered, 1)
    mate = swap(send, 1)
    beyond = (keep_far + mate[far:].astype(f32)).astype(bf16)
    other, _ = lax.optimization_barrier((other, beyond))

    if devices * kinds <= blocks * crossed:
        flat = pltpu.VMEM((kinds, devices * height, pixels), f32)
    else:
        flat = pltpu.VMEM((devices * height, length), bf16)
    (scores,) = call(
        functools.partial(score_kernel, shape),
        [((1, count), f32)],
        [hbm] * 4 + [vmem] * 5,
        (slabs, kind_rows, batch_block, inv_sigma2, wave, gathered, other, images_near, tiles_near),
        [
            *pairs_scratch,
            block_scratch,
            noise_scratch,
            flat,
            pltpu.VMEM((blocks, height, pixels), f32),
            pltpu.VMEM((count * 8, LANES), f32),
            pltpu.SemaphoreType.DMA((4,)),
        ],
        2 * devices * height * length * kinds * pixels,
        8 << 20,
        "scores",
    )

    mine = keep_near + mate[:far].astype(f32)
    for x in range(1, wide):
        came, scores = lax.optimization_barrier((swap(beyond[(x - 1) * far : x * far], x * cores), scores))
        mine = mine + came.astype(f32)
    lines = [[z * wide * cores + low for z in range(far)] for low in range(wide * cores)]
    came = lax.all_to_all(mine.astype(bf16), "slab", 0, 0, axis_index_groups=lines, tiled=True)
    total = jnp.sum(came.astype(f32), axis=0)
    return scores.reshape(count), total[0:1], total[1:2]


def solution(mesh):
    placed = (
        P(("parts", "slab"), None, None),
        P(),
        P(("parts", "slab"), None),
        P(("parts", "slab"), None),
        P(("parts", "slab")),
        P(("parts", "slab"), None, None),
        P(("parts", "slab")),
        P("parts", None),
    )
    return jax.shard_map(
        on_device,
        mesh=mesh,
        in_specs=placed,
        out_specs=(
            P(("parts", "slab")),
            P(("parts", "slab"), None, None),
            P(("parts", "slab"), None, None),
        ),
        check_vma=False,
    )
```

```python
import functools

import jax
import jax.numpy as jnp
from jax import lax
from jax.experimental import pallas as pl
from jax.experimental.pallas import tpu as pltpu
from jax.sharding import PartitionSpec as P

LANES = 128
CHUNKS = 4
VMEM_BYTES = 32 * 1024 * 1024


def grid_of(devices):
    cores = 2 if devices % 2 == 0 else 1
    chips = devices // cores
    wide = 1
    while (2 * wide) ** 3 <= chips:
        wide *= 2
    return chips // wide, wide, cores


def powers(size):
    return [1 << n for n in range(size.bit_length() - 1)]


def sin_cos(angle):
    turns = jnp.floor(angle * 0.3183098861837907 + 0.5)
    rest = angle - turns * 3.140625
    rest = rest - turns * 9.675025939941406e-4
    rest = rest - turns * 1.5099580252808664e-7
    half = turns * 0.5
    sign = 1.0 - 4.0 * (half - jnp.floor(half))
    sq = rest * rest
    sin = rest * (1.0 + sq * (-1.0 / 6 + sq * (1.0 / 120 + sq * (-1.0 / 5040 + sq * (1.0 / 362880 + sq * (-1.0 / 39916800))))))
    cos = 1.0 + sq * (-0.5 + sq * (1.0 / 24 + sq * (-1.0 / 720 + sq * (1.0 / 40320 + sq * (-1.0 / 3628800 + sq * (1.0 / 479001600))))))
    return sign * sin, sign * cos


def tables(defocus_ref, height, pixels, line_ref, pixel_ref):
    images = defocus_ref.shape[1]
    defocus = defocus_ref[...]
    rows = lax.broadcasted_iota(jnp.int32, (height, images), 0)
    line = ((rows // 2 + 1).astype(jnp.float32) / (height // 2)) ** 2
    line_ref[0], line_ref[1] = sin_cos(defocus * line + 0.3)
    column = jnp.transpose(jnp.broadcast_to(defocus, (LANES, images)))
    part = 32
    lanes = lax.broadcasted_iota(jnp.int32, (part, LANES), 1)
    for n in range(images // part):
        rows = slice(n * part, (n + 1) * part)
        for m in range(pixels // LANES):
            pixel = ((lanes + (m * LANES + 1)).astype(jnp.float32) / pixels) ** 2
            at = slice(m * LANES, (m + 1) * LANES)
            pixel_ref[0, rows, at], pixel_ref[1, rows, at] = sin_cos(column[rows] * pixel)


def contrast_of(line_ref, pixel_ref, i):
    sin_line, cos_line = line_ref[0, :, i : i + 1], line_ref[1, :, i : i + 1]
    return sin_line * pixel_ref[1, i : i + 1, :] + cos_line * pixel_ref[0, i : i + 1, :]


def copies(pairs, sems):
    started = [pltpu.make_async_copy(source, target, sems.at[n]) for n, (source, target) in enumerate(pairs)]
    for copy in started:
        copy.start()
    return started


def sum_kernel(block_hbm, defocus_hbm, noise_hbm, tiles_hbm, images_hbm,
               sums_ref, wave_ref, tiles_ref, images_ref,
               block_ref, defocus_ref, noise_ref, line_ref, pixel_ref, acc_ref, sems):
    count = images_ref.shape[0]
    part = count // CHUNKS
    small = [(defocus_hbm, defocus_ref), (block_hbm, block_ref), (noise_hbm, noise_ref)]
    large = [(images_hbm.at[pl.ds(n * part, part)], images_ref.at[pl.ds(n * part, part)]) for n in range(CHUNKS)]
    started = copies(small + large + [(tiles_hbm, tiles_ref)], sems)
    height, pixels = noise_ref.shape
    batches = block_ref.shape[0]
    size = count // batches
    acc_ref[...] = jnp.zeros_like(acc_ref)
    for copy in started[: len(small)]:
        copy.wait()
    tables(defocus_ref, height, pixels, line_ref, pixel_ref)
    for b in range(batches):
        if b % (batches // CHUNKS) == 0:
            started[len(small) + b // (batches // CHUNKS)].wait()
        data = jnp.zeros((height, pixels), jnp.float32)
        weight = jnp.zeros((height, pixels), jnp.float32)
        for j in range(size):
            i = b * size + j
            wave = contrast_of(line_ref, pixel_ref, i)
            wave_ref[i] = wave
            data = data + wave * images_ref[i].astype(jnp.float32)
            weight = weight + wave * wave
        k = block_ref[b]
        acc_ref[0, k] = acc_ref[0, k] + data
        acc_ref[1, k] = acc_ref[1, k] + weight
    sums = (acc_ref[...] * noise_ref[...][None, None]).astype(jnp.bfloat16)
    sums_ref[...] = sums.reshape(sums_ref.shape)
    started[-1].wait()


def insert_kernel(shape, slab_hbm, tile_hbm, sums_ref, tiles_ref, send_ref, far_ref, near_ref,
                  slab_ref, tile_ref, first_ref, second_ref, place_ref, sems):
    far, wide, cores = shape
    started = copies([(slab_hbm, slab_ref), (tile_hbm, tile_ref)], sems)
    crossed, blocks = slab_ref.shape
    kinds, length, _ = tiles_ref.shape
    sides, rows, _ = sums_ref.shape
    height = rows // blocks
    devices = place_ref.shape[0] // blocks
    columns = length // 2
    each = devices // kinds
    halves = (first_ref, second_ref)

    def multiply(n, t):
        at = pl.multiple_of(t * rows, rows)
        for side in range(sides):
            halves[n][side, pl.ds(at, rows), :] = lax.dot_general(
                sums_ref[side],
                tiles_ref[t, n * columns : (n + 1) * columns, :],
                (((1,), (1,)), ((), ())),
                preferred_element_type=jnp.float32,
            )

    for ref in halves:
        ref[:, pl.ds(kinds * rows, height), :] = jnp.zeros((sides, height, columns), jnp.float32)
    for t in range(kinds // 2):
        multiply(0, t)

    for copy in started:
        copy.wait()

    def clear(n, carry):
        for m in range(blocks):
            place_ref[n * blocks + m] = kinds * rows
        return carry

    lax.fori_loop(0, devices, clear, 0, unroll=devices <= 16)
    for k in range(blocks):
        for r in range(crossed):
            place_ref[slab_ref[r, k] * blocks + k] = tile_ref[r, k] * rows + k * height
    for t in range(kinds // 2, kinds):
        multiply(0, t)

    me = lax.axis_index("slab")

    def total(n, side, x, z, core):
        s = me ^ ((z * wide + x) * cores + core)
        acc = None
        for k in range(blocks):
            at = pl.multiple_of(place_ref[s * blocks + k], height)
            part = halves[n][side, pl.ds(at, height), :]
            acc = part if acc is None else acc + part
        return acc

    for n in range(2):
        done = 0
        for ref, start, core in ((send_ref, 0, 1), (far_ref, 1, 0), (near_ref, 0, 0)):

            def step(i, carry, ref=ref, start=start, core=core, done=done, n=n):
                for m in range(each):
                    slot = i * each + m
                    x, z = start + slot // far, lax.rem(slot, far)
                    for side in range(sides):
                        part = total(n, side, x, z, core).astype(ref.dtype)
                        ref[slot, side, :, n * columns : (n + 1) * columns] = part
                if n == 0:
                    multiply(1, done + i)
                return carry

            steps = ref.shape[0] // each
            lax.fori_loop(0, steps, step, 0)
            done += steps


def score_kernel(shape, slab_hbm, tile_hbm, block_hbm, noise_hbm, wave_ref, near_ref, other_ref, images_ref, tiles_ref,
                 score_ref, slab_ref, tile_ref, block_ref, noise_ref, flat_ref, proj_ref, part_ref, sems):
    far, wide, cores = shape
    started = copies([(slab_hbm, slab_ref), (tile_hbm, tile_ref), (block_hbm, block_ref), (noise_hbm, noise_ref)], sems)
    height, pixels = noise_ref.shape
    crossed, blocks = slab_ref.shape
    batches = block_ref.shape[0]
    count = images_ref.shape[0]
    size = count // batches
    half = near_ref.shape[0]
    me = lax.axis_index("slab")
    dense = 2 * half * tiles_ref.shape[0] <= crossed * blocks

    def slot_of(s):
        away = me ^ s
        core, chip = lax.rem(away, cores), away // cores
        return core * half + lax.rem(chip, wide) * far + chip // wide

    for n, ref in enumerate((near_ref, other_ref)):
        lines = ref[...].reshape(half * height, ref.shape[2])
        if dense:
            for t in range(tiles_ref.shape[0]):
                flat_ref[t, n * half * height : (n + 1) * half * height, :] = jnp.dot(
                    lines, tiles_ref[t], preferred_element_type=jnp.float32
                )
        else:
            flat_ref[n * half * height : (n + 1) * half * height, :] = lines
    for copy in started:
        copy.wait()

    def project(k, carry):
        acc = None
        for r in range(crossed):
            t = tile_ref[r, k]
            rows = pl.ds(pl.multiple_of(slot_of(slab_ref[r, k]) * height, height), height)
            if dense:
                part = flat_ref[t, rows, :]
            else:
                part = jnp.dot(flat_ref[rows, :], tiles_ref[t], preferred_element_type=jnp.float32)
            acc = part if acc is None else acc + part
        proj_ref[k] = acc
        return carry

    lax.fori_loop(0, blocks, project, 0, unroll=dense)
    for b in range(batches):
        k = block_ref[b]
        for j in range(size):
            i = b * size + j
            residual = images_ref[i].astype(jnp.float32) - wave_ref[i] * proj_ref[k]
            power = residual * residual * noise_ref[...]
            power = sum(power[n * 8 : (n + 1) * 8] for n in range(height // 8))
            part_ref[i * 8 : (i + 1) * 8, :] = sum(power[:, n * LANES : (n + 1) * LANES] for n in range(pixels // LANES))
    total = sum(part_ref[pl.ds(n, count, 8), :] for n in range(8))
    total = jnp.sum(jnp.transpose(total), axis=0, keepdims=True)
    score_ref[...] = total * (1.0 / (height * pixels))


def on_device(volume, tiles, slab_ids, tile_ids, batch_block, images, defocus, inv_sigma2):
    blocks, crossed = slab_ids.shape
    height, length = volume.shape[1:]
    count, _, pixels = images.shape
    kinds = tiles.shape[0]
    devices = lax.axis_size("slab")
    shape = far, wide, cores = grid_of(devices)
    half = devices // 2
    rows = blocks * height
    slabs, kind_rows, row = slab_ids.T, tile_ids.T, defocus.reshape(1, count)

    def swap(array, offset):
        return lax.ppermute(array, "slab", [(i, i ^ offset) for i in range(devices)])

    vmem = pl.BlockSpec(memory_space=pltpu.VMEM)
    hbm = pl.BlockSpec(memory_space=pltpu.HBM)
    params = pltpu.CompilerParams(vmem_limit_bytes=VMEM_BYTES)
    f32, bf16 = jnp.float32, jnp.bfloat16
    pairs_scratch = [pltpu.SMEM((crossed, blocks), jnp.int32), pltpu.SMEM((crossed, blocks), jnp.int32)]
    block_scratch = pltpu.SMEM(batch_block.shape, jnp.int32)
    noise_scratch = pltpu.VMEM((height, pixels), f32)

    def call(kernel, outs, inputs, operands, scratch, flops, moved, name):
        operands = [
            pltpu.with_memory_space_constraint(x, pltpu.HBM) if spec is hbm else x for x, spec in zip(operands, inputs)
        ]
        return pl.pallas_call(
            kernel,
            out_shape=tuple(jax.ShapeDtypeStruct(s, t) for s, t in outs),
            in_specs=inputs,
            out_specs=(vmem,) * len(outs),
            scratch_shapes=scratch,
            compiler_params=params,
            cost_estimate=pl.CostEstimate(flops=flops, bytes_accessed=moved, transcendentals=0),
            name=name,
        )(*operands)

    def hop(array, offset):
        return jnp.concatenate([array, swap(array, offset)], axis=0)

    offsets = [z * wide * cores for z in powers(far)] + [x * cores for x in powers(wide)]
    gathered = hop(volume, offsets[0])

    sums, wave, tiles_near, images_near = call(
        sum_kernel,
        [((2, rows, pixels), bf16), (images.shape, f32), (tiles.shape, bf16), (images.shape, bf16)],
        [hbm] * 5,
        (batch_block, row, inv_sigma2, tiles, images),
        [
            block_scratch,
            pltpu.VMEM((1, count), f32),
            noise_scratch,
            pltpu.VMEM((2, height, count), f32),
            pltpu.VMEM((2, count, pixels), f32),
            pltpu.VMEM((2, blocks, height, pixels), f32),
            pltpu.SemaphoreType.DMA((CHUNKS + 4,)),
        ],
        0,
        10 << 20,
        "sums",
    )
    sums, gathered = lax.optimization_barrier((sums, gathered))
    gathered = hop(gathered, offsets[1])

    place = (2, height, length)
    send, keep_far, keep_near = call(
        functools.partial(insert_kernel, shape),
        [((half, *place), bf16), (((wide - 1) * far, *place), f32), ((far, *place), f32)],
        [hbm, hbm, vmem, vmem],
        (slabs, kind_rows, sums, tiles_near),
        [
            *pairs_scratch,
            pltpu.VMEM((2, kinds * rows + height, length // 2), f32),
            pltpu.VMEM((2, kinds * rows + height, length // 2), f32),
            pltpu.SMEM((devices * blocks,), jnp.int32),
            pltpu.SemaphoreType.DMA((2,)),
        ],
        4 * rows * pixels * kinds * length,
        8 << 20,
        "insert",
    )
    send, gathered = lax.optimization_barrier((send, gathered))
    mate = swap(send, 1)
    beyond = (keep_far + mate[far:].astype(f32)).astype(bf16)
    for offset in offsets[2:]:
        came, _ = lax.optimization_barrier((swap(gathered, offset), beyond))
        gathered = jnp.concatenate([gathered, came], axis=0)
    other = swap(gathered, 1)

    if devices * kinds <= blocks * crossed:
        flat = pltpu.VMEM((kinds, devices * height, pixels), f32)
    else:
        flat = pltpu.VMEM((devices * height, length), bf16)
    (scores,) = call(
        functools.partial(score_kernel, shape),
        [((1, count), f32)],
        [hbm] * 4 + [vmem] * 5,
        (slabs, kind_rows, batch_block, inv_sigma2, wave, gathered, other, images_near, tiles_near),
        [
            *pairs_scratch,
            block_scratch,
            noise_scratch,
            flat,
            pltpu.VMEM((blocks, height, pixels), f32),
            pltpu.VMEM((count * 8, LANES), f32),
            pltpu.SemaphoreType.DMA((4,)),
        ],
        0,
        0,
        "scores",
    )

    mine = keep_near + mate[:far].astype(f32)
    for x in range(1, wide):
        came, scores = lax.optimization_barrier((swap(beyond[(x - 1) * far : x * far], x * cores), scores))
        mine = mine + came.astype(f32)
    total = mine[0]
    for z in range(far - 1, 0, -1):
        total = total + swap(mine[z].astype(bf16), z * wide * cores).astype(f32)
    return scores.reshape(count), total[0:1], total[1:2]


def solution(mesh):
    placed = (
        P(("parts", "slab"), None, None),
        P(),
        P(("parts", "slab"), None),
        P(("parts", "slab"), None),
        P(("parts", "slab")),
        P(("parts", "slab"), None, None),
        P(("parts", "slab")),
        P("parts", None),
    )
    return jax.shard_map(
        on_device,
        mesh=mesh,
        in_specs=placed,
        out_specs=(
            P(("parts", "slab")),
            P(("parts", "slab"), None, None),
            P(("parts", "slab"), None, None),
        ),
        check_vma=False,
    )
```

```python
import functools

import jax
import jax.numpy as jnp
from jax import lax
from jax.experimental import pallas as pl
from jax.experimental.pallas import tpu as pltpu
from jax.sharding import PartitionSpec as P

LANES = 128
CHUNKS = 4
VMEM_BYTES = 32 * 1024 * 1024


def grid_of(devices):
    cores = 2 if devices % 2 == 0 else 1
    chips = devices // cores
    wide = 1
    while (2 * wide) ** 3 <= chips:
        wide *= 2
    return chips // wide, wide, cores


def powers(size):
    return [1 << n for n in range(size.bit_length() - 1)]


def sin_cos(angle):
    turns = jnp.floor(angle * 0.3183098861837907 + 0.5)
    rest = angle - turns * 3.140625
    rest = rest - turns * 9.675025939941406e-4
    rest = rest - turns * 1.5099580252808664e-7
    half = turns * 0.5
    sign = 1.0 - 4.0 * (half - jnp.floor(half))
    sq = rest * rest
    sin = rest * (1.0 + sq * (-1.0 / 6 + sq * (1.0 / 120 + sq * (-1.0 / 5040 + sq * (1.0 / 362880 + sq * (-1.0 / 39916800))))))
    cos = 1.0 + sq * (-0.5 + sq * (1.0 / 24 + sq * (-1.0 / 720 + sq * (1.0 / 40320 + sq * (-1.0 / 3628800 + sq * (1.0 / 479001600))))))
    return sign * sin, sign * cos


def tables(defocus_ref, height, pixels, line_ref, pixel_ref):
    images = defocus_ref.shape[1]
    defocus = defocus_ref[...]
    rows = lax.broadcasted_iota(jnp.int32, (height, images), 0)
    line = ((rows // 2 + 1).astype(jnp.float32) / (height // 2)) ** 2
    line_ref[0], line_ref[1] = sin_cos(defocus * line + 0.3)
    column = jnp.transpose(jnp.broadcast_to(defocus, (LANES, images)))
    part = 32
    lanes = lax.broadcasted_iota(jnp.int32, (part, LANES), 1)
    for n in range(images // part):
        rows = slice(n * part, (n + 1) * part)
        for m in range(pixels // LANES):
            pixel = ((lanes + (m * LANES + 1)).astype(jnp.float32) / pixels) ** 2
            at = slice(m * LANES, (m + 1) * LANES)
            pixel_ref[0, rows, at], pixel_ref[1, rows, at] = sin_cos(column[rows] * pixel)


def contrast_of(line_ref, pixel_ref, i):
    sin_line, cos_line = line_ref[0, :, i : i + 1], line_ref[1, :, i : i + 1]
    return sin_line * pixel_ref[1, i : i + 1, :] + cos_line * pixel_ref[0, i : i + 1, :]


def copies(pairs, sems):
    started = [pltpu.make_async_copy(source, target, sems.at[n]) for n, (source, target) in enumerate(pairs)]
    for copy in started:
        copy.start()
    return started


def sum_kernel(block_hbm, defocus_hbm, noise_hbm, tiles_hbm, images_hbm,
               sums_ref, wave_ref, tiles_ref, images_ref,
               block_ref, defocus_ref, noise_ref, line_ref, pixel_ref, acc_ref, sems):
    count = images_ref.shape[0]
    part = count // CHUNKS
    small = [(defocus_hbm, defocus_ref), (block_hbm, block_ref), (noise_hbm, noise_ref)]
    large = [(images_hbm.at[pl.ds(n * part, part)], images_ref.at[pl.ds(n * part, part)]) for n in range(CHUNKS)]
    started = copies(small + large + [(tiles_hbm, tiles_ref)], sems)
    height, pixels = noise_ref.shape
    batches = block_ref.shape[0]
    size = count // batches
    acc_ref[...] = jnp.zeros_like(acc_ref)
    for copy in started[: len(small)]:
        copy.wait()
    tables(defocus_ref, height, pixels, line_ref, pixel_ref)
    for b in range(batches):
        if b % (batches // CHUNKS) == 0:
            started[len(small) + b // (batches // CHUNKS)].wait()
        data = jnp.zeros((height, pixels), jnp.float32)
        weight = jnp.zeros((height, pixels), jnp.float32)
        for j in range(size):
            i = b * size + j
            wave = contrast_of(line_ref, pixel_ref, i)
            wave_ref[i] = wave
            data = data + wave * images_ref[i].astype(jnp.float32)
            weight = weight + wave * wave
        k = block_ref[b]
        acc_ref[k, 0] = acc_ref[k, 0] + data
        acc_ref[k, 1] = acc_ref[k, 1] + weight
    sums = (acc_ref[...] * noise_ref[...][None, None]).astype(jnp.bfloat16)
    sums_ref[...] = sums.reshape(sums_ref.shape)
    started[-1].wait()


def insert_kernel(shape, slab_hbm, tile_hbm, sums_ref, tiles_ref, send_ref, far_ref, near_ref,
                  slab_ref, tile_ref, parts_ref, place_ref, sems):
    far, wide, cores = shape
    started = copies([(slab_hbm, slab_ref), (tile_hbm, tile_ref)], sems)
    crossed, blocks = slab_ref.shape
    kinds = tiles_ref.shape[0]
    rows = sums_ref.shape[0]
    height = rows // (2 * blocks)
    devices = place_ref.shape[0] // blocks

    def multiply(t):
        parts_ref[t * rows : (t + 1) * rows, :] = lax.dot_general(
            sums_ref[...], tiles_ref[t], (((1,), (1,)), ((), ())), preferred_element_type=jnp.float32
        )

    parts_ref[pl.ds(kinds * rows, 2 * height), :] = jnp.zeros((2 * height, parts_ref.shape[1]), jnp.float32)
    for t in range(kinds // 2):
        multiply(t)

    for copy in started:
        copy.wait()

    def clear(n, carry):
        for m in range(blocks):
            place_ref[n * blocks + m] = kinds * rows
        return carry

    lax.fori_loop(0, devices, clear, 0, unroll=devices <= 16)
    for k in range(blocks):
        for r in range(crossed):
            place_ref[slab_ref[r, k] * blocks + k] = tile_ref[r, k] * rows + k * 2 * height
    for t in range(kinds // 2, kinds):
        multiply(t)
    me = lax.axis_index("slab")

    def total(x, z, core, kind):
        s = me ^ ((z * wide + x) * cores + core)
        acc = None
        for k in range(blocks):
            at = pl.multiple_of(place_ref[s * blocks + k] + kind * height, height)
            part = parts_ref[pl.ds(at, height), :]
            acc = part if acc is None else acc + part
        return acc

    def fill(ref, start, core):
        def step(slot, carry):
            x, z = start + slot // far, lax.rem(slot, far)
            for kind in range(2):
                ref[slot, kind] = total(x, z, core, kind).astype(ref.dtype)
            return carry

        lax.fori_loop(0, ref.shape[0], step, 0)

    fill(send_ref, 0, 1)
    fill(far_ref, 1, 0)
    fill(near_ref, 0, 0)


def score_kernel(shape, slab_hbm, tile_hbm, block_hbm, noise_hbm, wave_ref, images_ref, tiles_ref, *refs):
    far, wide, cores = shape
    columns, refs = refs[: wide * cores], refs[wide * cores :]
    score_ref, slab_ref, tile_ref, block_ref, noise_ref, flat_ref, proj_ref, part_ref, sems = refs
    started = copies([(slab_hbm, slab_ref), (tile_hbm, tile_ref), (block_hbm, block_ref), (noise_hbm, noise_ref)], sems)
    height, pixels = noise_ref.shape
    crossed, blocks = slab_ref.shape
    batches = block_ref.shape[0]
    count = images_ref.shape[0]
    size = count // batches
    me = lax.axis_index("slab")
    dense = far * len(columns) * tiles_ref.shape[0] <= crossed * blocks

    def slot_of(s):
        away = me ^ s
        core, chip = lax.rem(away, cores), away // cores
        return (core * wide + lax.rem(chip, wide)) * far + chip // wide

    for n, ref in enumerate(columns):
        lines = ref[...].reshape(far * height, ref.shape[2])
        at = slice(n * far * height, (n + 1) * far * height)
        if dense:
            for t in range(tiles_ref.shape[0]):
                flat_ref[t, at, :] = jnp.dot(lines, tiles_ref[t], preferred_element_type=jnp.float32)
        else:
            flat_ref[at, :] = lines
    for copy in started:
        copy.wait()

    def project(k, carry):
        acc = None
        for r in range(crossed):
            t = tile_ref[r, k]
            rows = pl.ds(pl.multiple_of(slot_of(slab_ref[r, k]) * height, height), height)
            if dense:
                part = flat_ref[t, rows, :]
            else:
                part = jnp.dot(flat_ref[rows, :], tiles_ref[t], preferred_element_type=jnp.float32)
            acc = part if acc is None else acc + part
        proj_ref[k] = acc
        return carry

    lax.fori_loop(0, blocks, project, 0, unroll=dense)
    for b in range(batches):
        k = block_ref[b]
        for j in range(size):
            i = b * size + j
            residual = images_ref[i].astype(jnp.float32) - wave_ref[i] * proj_ref[k]
            power = residual * residual * noise_ref[...]
            power = sum(power[n * 8 : (n + 1) * 8] for n in range(height // 8))
            part_ref[i * 8 : (i + 1) * 8, :] = sum(power[:, n * LANES : (n + 1) * LANES] for n in range(pixels // LANES))
    total = sum(part_ref[pl.ds(n, count, 8), :] for n in range(8))
    total = jnp.sum(jnp.transpose(total), axis=0, keepdims=True)
    score_ref[...] = total * (1.0 / (height * pixels))


def on_device(volume, tiles, slab_ids, tile_ids, batch_block, images, defocus, inv_sigma2):
    blocks, crossed = slab_ids.shape
    height, length = volume.shape[1:]
    count, _, pixels = images.shape
    kinds = tiles.shape[0]
    devices = lax.axis_size("slab")
    shape = far, wide, cores = grid_of(devices)
    half = devices // 2
    rows = blocks * 2 * height
    slabs, kind_rows, row = slab_ids.T, tile_ids.T, defocus.reshape(1, count)

    def swap(array, offset):
        return lax.ppermute(array, "slab", [(i, i ^ offset) for i in range(devices)])

    vmem = pl.BlockSpec(memory_space=pltpu.VMEM)
    hbm = pl.BlockSpec(memory_space=pltpu.HBM)
    params = pltpu.CompilerParams(vmem_limit_bytes=VMEM_BYTES)
    f32, bf16 = jnp.float32, jnp.bfloat16
    pairs_scratch = [pltpu.SMEM((crossed, blocks), jnp.int32), pltpu.SMEM((crossed, blocks), jnp.int32)]
    block_scratch = pltpu.SMEM(batch_block.shape, jnp.int32)
    noise_scratch = pltpu.VMEM((height, pixels), f32)

    def call(kernel, outs, inputs, operands, scratch, flops, moved, name):
        operands = [
            pltpu.with_memory_space_constraint(x, pltpu.HBM) if spec is hbm else x for x, spec in zip(operands, inputs)
        ]
        return pl.pallas_call(
            kernel,
            out_shape=tuple(jax.ShapeDtypeStruct(s, t) for s, t in outs),
            in_specs=inputs,
            out_specs=(vmem,) * len(outs),
            scratch_shapes=scratch,
            compiler_params=params,
            cost_estimate=pl.CostEstimate(flops=flops, bytes_accessed=moved, transcendentals=0),
            name=name,
        )(*operands)

    def hop(array, offset):
        return jnp.concatenate([array, swap(array, offset)], axis=0)

    offsets = [z * wide * cores for z in powers(far)]
    gathered = hop(volume, offsets[0])

    sums, wave, tiles_near, images_near = call(
        sum_kernel,
        [((rows, pixels), bf16), (images.shape, f32), (tiles.shape, bf16), (images.shape, bf16)],
        [hbm] * 5,
        (batch_block, row, inv_sigma2, tiles, images),
        [
            block_scratch,
            pltpu.VMEM((1, count), f32),
            noise_scratch,
            pltpu.VMEM((2, height, count), f32),
            pltpu.VMEM((2, count, pixels), f32),
            pltpu.VMEM((blocks, 2, height, pixels), f32),
            pltpu.SemaphoreType.DMA((CHUNKS + 4,)),
        ],
        0,
        10 << 20,
        "sums",
    )
    sums, gathered = lax.optimization_barrier((sums, gathered))
    for offset in offsets[1:]:
        gathered = hop(gathered, offset)

    place = (2, height, length)
    send, keep_far, keep_near = call(
        functools.partial(insert_kernel, shape),
        [((half, *place), bf16), (((wide - 1) * far, *place), f32), ((far, *place), f32)],
        [hbm, hbm, vmem, vmem],
        (slabs, kind_rows, sums, tiles_near),
        [
            *pairs_scratch,
            pltpu.VMEM((kinds * rows + 2 * height, length), f32),
            pltpu.SMEM((devices * blocks,), jnp.int32),
            pltpu.SemaphoreType.DMA((2,)),
        ],
        2 * rows * pixels * kinds * length,
        8 << 20,
        "insert",
    )
    send, gathered = lax.optimization_barrier((send, gathered))
    mate = swap(send, 1)
    beyond = (keep_far + mate[far:].astype(f32)).astype(bf16)
    columns = [gathered]
    for x in range(1, wide):
        columns.append(lax.optimization_barrier((swap(gathered, x * cores), beyond))[0])
    columns += [swap(column, 1) for column in columns]

    if devices * kinds <= blocks * crossed:
        flat = pltpu.VMEM((kinds, devices * height, pixels), f32)
    else:
        flat = pltpu.VMEM((devices * height, length), bf16)
    (scores,) = call(
        functools.partial(score_kernel, shape),
        [((1, count), f32)],
        [hbm] * 4 + [vmem] * (3 + len(columns)),
        (slabs, kind_rows, batch_block, inv_sigma2, wave, images_near, tiles_near, *columns),
        [
            *pairs_scratch,
            block_scratch,
            noise_scratch,
            flat,
            pltpu.VMEM((blocks, height, pixels), f32),
            pltpu.VMEM((count * 8, LANES), f32),
            pltpu.SemaphoreType.DMA((4,)),
        ],
        0,
        0,
        "scores",
    )

    mine = keep_near + mate[:far].astype(f32)
    for x in range(1, wide):
        came, scores = lax.optimization_barrier((swap(beyond[(x - 1) * far : x * far], x * cores), scores))
        mine = mine + came.astype(f32)
    total = mine[0]
    for z in range(1, far):
        total = total + swap(mine[z].astype(bf16), z * wide * cores).astype(f32)
    return scores.reshape(count), total[0:1], total[1:2]


def solution(mesh):
    placed = (
        P(("parts", "slab"), None, None),
        P(),
        P(("parts", "slab"), None),
        P(("parts", "slab"), None),
        P(("parts", "slab")),
        P(("parts", "slab"), None, None),
        P(("parts", "slab")),
        P("parts", None),
    )
    return jax.shard_map(
        on_device,
        mesh=mesh,
        in_specs=placed,
        out_specs=(
            P(("parts", "slab")),
            P(("parts", "slab"), None, None),
            P(("parts", "slab"), None, None),
        ),
        check_vma=False,
    )
```

```python
import functools

import jax
import jax.numpy as jnp
from jax import lax
from jax.experimental import pallas as pl
from jax.experimental.pallas import tpu as pltpu
from jax.sharding import PartitionSpec as P

LANES = 128
CHUNKS = 4
VMEM_BYTES = 32 * 1024 * 1024


def grid_of(devices):
    cores = 2 if devices % 2 == 0 else 1
    chips = devices // cores
    wide = 1
    while (2 * wide) ** 3 <= chips:
        wide *= 2
    return chips // wide, wide, cores


def powers(size):
    return [1 << n for n in range(size.bit_length() - 1)]


def sin_cos(angle):
    turns = jnp.floor(angle * 0.3183098861837907 + 0.5)
    rest = angle - turns * 3.140625
    rest = rest - turns * 9.675025939941406e-4
    rest = rest - turns * 1.5099580252808664e-7
    half = turns * 0.5
    sign = 1.0 - 4.0 * (half - jnp.floor(half))
    sq = rest * rest
    sin = rest * (1.0 + sq * (-1.0 / 6 + sq * (1.0 / 120 + sq * (-1.0 / 5040 + sq * (1.0 / 362880 + sq * (-1.0 / 39916800))))))
    cos = 1.0 + sq * (-0.5 + sq * (1.0 / 24 + sq * (-1.0 / 720 + sq * (1.0 / 40320 + sq * (-1.0 / 3628800 + sq * (1.0 / 479001600))))))
    return sign * sin, sign * cos


def tables(defocus_ref, height, pixels, line_ref, pixel_ref):
    images = defocus_ref.shape[1]
    defocus = defocus_ref[...]
    rows = lax.broadcasted_iota(jnp.int32, (height, images), 0)
    line = ((rows // 2 + 1).astype(jnp.float32) / (height // 2)) ** 2
    line_ref[0], line_ref[1] = sin_cos(defocus * line + 0.3)
    column = jnp.transpose(jnp.broadcast_to(defocus, (LANES, images)))
    part = 32
    lanes = lax.broadcasted_iota(jnp.int32, (part, LANES), 1)
    for n in range(images // part):
        rows = slice(n * part, (n + 1) * part)
        for m in range(pixels // LANES):
            pixel = ((lanes + (m * LANES + 1)).astype(jnp.float32) / pixels) ** 2
            at = slice(m * LANES, (m + 1) * LANES)
            pixel_ref[0, rows, at], pixel_ref[1, rows, at] = sin_cos(column[rows] * pixel)


def contrast_of(line_ref, pixel_ref, i):
    sin_line, cos_line = line_ref[0, :, i : i + 1], line_ref[1, :, i : i + 1]
    return sin_line * pixel_ref[1, i : i + 1, :] + cos_line * pixel_ref[0, i : i + 1, :]


def copies(pairs, sems):
    started = [pltpu.make_async_copy(source, target, sems.at[n]) for n, (source, target) in enumerate(pairs)]
    for copy in started:
        copy.start()
    return started


def sum_kernel(block_hbm, defocus_hbm, noise_hbm, tiles_hbm, images_hbm,
               sums_ref, wave_ref, tiles_ref, images_ref,
               block_ref, defocus_ref, noise_ref, line_ref, pixel_ref, acc_ref, sems):
    count = images_ref.shape[0]
    part = count // CHUNKS
    small = [(defocus_hbm, defocus_ref), (block_hbm, block_ref), (noise_hbm, noise_ref)]
    large = [(images_hbm.at[pl.ds(n * part, part)], images_ref.at[pl.ds(n * part, part)]) for n in range(CHUNKS)]
    started = copies(small + large, sems)
    last = pltpu.make_async_copy(tiles_hbm, tiles_ref, sems.at[len(started)])
    height, pixels = noise_ref.shape
    batches = block_ref.shape[0]
    size = count // batches
    acc_ref[...] = jnp.zeros_like(acc_ref)
    for copy in started[: len(small)]:
        copy.wait()
    tables(defocus_ref, height, pixels, line_ref, pixel_ref)
    for b in range(batches):
        if b % (batches // CHUNKS) == 0:
            started[len(small) + b // (batches // CHUNKS)].wait()
        if b == 0:
            last.start()
        data = jnp.zeros((height, pixels), jnp.float32)
        weight = jnp.zeros((height, pixels), jnp.float32)
        for j in range(size):
            i = b * size + j
            wave = contrast_of(line_ref, pixel_ref, i)
            wave_ref[i] = wave
            data = data + wave * images_ref[i].astype(jnp.float32)
            weight = weight + wave * wave
        k = block_ref[b]
        acc_ref[k, 0] = acc_ref[k, 0] + data
        acc_ref[k, 1] = acc_ref[k, 1] + weight
    sums = (acc_ref[...] * noise_ref[...][None, None]).astype(jnp.bfloat16)
    sums_ref[...] = sums.reshape(sums_ref.shape)
    last.wait()


def insert_kernel(shape, slab_hbm, tile_hbm, sums_ref, tiles_ref, send_ref, far_ref, near_ref,
                  slab_ref, tile_ref, parts_ref, place_ref, sems):
    far, wide, cores = shape
    started = copies([(slab_hbm, slab_ref), (tile_hbm, tile_ref)], sems)
    crossed, blocks = slab_ref.shape
    kinds = tiles_ref.shape[0]
    rows = sums_ref.shape[0]
    height = rows // (2 * blocks)
    devices = place_ref.shape[0] // blocks

    def multiply(t):
        parts_ref[t * rows : (t + 1) * rows, :] = lax.dot_general(
            sums_ref[...], tiles_ref[t], (((1,), (1,)), ((), ())), preferred_element_type=jnp.float32
        )

    parts_ref[pl.ds(kinds * rows, 2 * height), :] = jnp.zeros((2 * height, parts_ref.shape[1]), jnp.float32)
    for t in range(kinds // 2):
        multiply(t)

    for copy in started:
        copy.wait()

    def clear(n, carry):
        for m in range(blocks):
            place_ref[n * blocks + m] = kinds * rows
        return carry

    lax.fori_loop(0, devices, clear, 0, unroll=devices <= 16)
    for k in range(blocks):
        for r in range(crossed):
            place_ref[slab_ref[r, k] * blocks + k] = tile_ref[r, k] * rows + k * 2 * height
    for t in range(kinds // 2, kinds):
        multiply(t)
    me = lax.axis_index("slab")

    def total(x, z, core, kind):
        s = me ^ ((z * wide + x) * cores + core)
        acc = None
        for k in range(blocks):
            at = pl.multiple_of(place_ref[s * blocks + k] + kind * height, height)
            part = parts_ref[pl.ds(at, height), :]
            acc = part if acc is None else acc + part
        return acc

    def fill(ref, start, core):
        def step(slot, carry):
            x, z = start + slot // far, lax.rem(slot, far)
            for kind in range(2):
                ref[slot, kind] = total(x, z, core, kind).astype(ref.dtype)
            return carry

        lax.fori_loop(0, ref.shape[0], step, 0)

    fill(send_ref, 0, 1)
    fill(far_ref, 1, 0)
    fill(near_ref, 0, 0)


def project_kernel(shape, slab_hbm, tile_hbm, tiles_ref, *refs):
    far, wide, cores = shape
    columns, refs = refs[: wide * cores], refs[wide * cores :]
    proj_ref, slab_ref, tile_ref, lines_ref, flat_ref, sems = refs
    started = copies([(slab_hbm, slab_ref), (tile_hbm, tile_ref)], sems)
    crossed, blocks = slab_ref.shape
    kinds = tiles_ref.shape[0]
    _, height, length = columns[0].shape
    dense = far * len(columns) * kinds <= crossed * blocks
    for n, ref in enumerate(columns):
        lines_ref[n * far * height : (n + 1) * far * height, :] = ref[...].reshape(far * height, length)
    if dense:
        for t in range(kinds):
            flat_ref[t] = jnp.dot(lines_ref[...], tiles_ref[t], preferred_element_type=jnp.float32)
    for copy in started:
        copy.wait()
    me = lax.axis_index("slab")

    def slot_of(s):
        away = me ^ s
        core, x, z = away & (cores - 1), (away // cores) & (wide - 1), away // (cores * wide)
        return (core * wide + x) * far + z

    def project(k, carry):
        acc = None
        for r in range(crossed):
            t = tile_ref[r, k]
            rows = pl.ds(pl.multiple_of(slot_of(slab_ref[r, k]) * height, height), height)
            if dense:
                part = flat_ref[t, rows, :]
            else:
                part = jnp.dot(lines_ref[rows, :], tiles_ref[t], preferred_element_type=jnp.float32)
            acc = part if acc is None else acc + part
        proj_ref[k] = acc
        return carry

    lax.fori_loop(0, blocks, project, 0, unroll=dense)


def score_kernel(block_hbm, noise_hbm, proj_ref, wave_ref, images_ref, score_ref, block_ref, noise_ref, part_ref, sems):
    started = copies([(block_hbm, block_ref), (noise_hbm, noise_ref)], sems)
    height, pixels = noise_ref.shape
    batches = block_ref.shape[0]
    count = images_ref.shape[0]
    size = count // batches
    for copy in started:
        copy.wait()
    noise = noise_ref[...]
    for b in range(batches):
        proj = proj_ref[block_ref[b]]
        for j in range(size):
            i = b * size + j
            residual = images_ref[i].astype(jnp.float32) - wave_ref[i] * proj
            power = residual * residual * noise
            power = sum(power[n * 8 : (n + 1) * 8] for n in range(height // 8))
            part_ref[i * 8 : (i + 1) * 8, :] = sum(power[:, n * LANES : (n + 1) * LANES] for n in range(pixels // LANES))
    total = sum(part_ref[pl.ds(n, count, 8), :] for n in range(8))
    total = jnp.sum(jnp.transpose(total), axis=0, keepdims=True)
    score_ref[...] = total * (1.0 / (height * pixels))


def on_device(volume, tiles, slab_ids, tile_ids, batch_block, images, defocus, inv_sigma2):
    blocks, crossed = slab_ids.shape
    height, length = volume.shape[1:]
    count, _, pixels = images.shape
    kinds = tiles.shape[0]
    devices = lax.axis_size("slab")
    shape = far, wide, cores = grid_of(devices)
    half = devices // 2
    rows = blocks * 2 * height
    slabs, kind_rows, row = slab_ids.T, tile_ids.T, defocus.reshape(1, count)

    def swap(array, offset):
        return lax.ppermute(array, "slab", [(i, i ^ offset) for i in range(devices)])

    vmem = pl.BlockSpec(memory_space=pltpu.VMEM)
    hbm = pl.BlockSpec(memory_space=pltpu.HBM)
    params = pltpu.CompilerParams(vmem_limit_bytes=VMEM_BYTES)
    f32, bf16 = jnp.float32, jnp.bfloat16
    pairs_scratch = [pltpu.SMEM((crossed, blocks), jnp.int32), pltpu.SMEM((crossed, blocks), jnp.int32)]
    block_scratch = pltpu.SMEM(batch_block.shape, jnp.int32)
    noise_scratch = pltpu.VMEM((height, pixels), f32)

    def call(kernel, outs, inputs, operands, scratch, flops, moved, name):
        operands = [
            pltpu.with_memory_space_constraint(x, pltpu.HBM) if spec is hbm else x for x, spec in zip(operands, inputs)
        ]
        return pl.pallas_call(
            kernel,
            out_shape=tuple(jax.ShapeDtypeStruct(s, t) for s, t in outs),
            in_specs=inputs,
            out_specs=(vmem,) * len(outs),
            scratch_shapes=scratch,
            compiler_params=params,
            cost_estimate=pl.CostEstimate(flops=flops, bytes_accessed=moved, transcendentals=0),
            name=name,
        )(*operands)

    def hop(array, offset):
        return jnp.concatenate([array, swap(array, offset)], axis=0)

    offsets = [z * wide * cores for z in powers(far)]
    gathered = hop(volume, offsets[0])

    sums, wave, tiles_near, images_near = call(
        sum_kernel,
        [((rows, pixels), bf16), (images.shape, f32), (tiles.shape, bf16), (images.shape, bf16)],
        [hbm] * 5,
        (batch_block, row, inv_sigma2, tiles, images),
        [
            block_scratch,
            pltpu.VMEM((1, count), f32),
            noise_scratch,
            pltpu.VMEM((2, height, count), f32),
            pltpu.VMEM((2, count, pixels), f32),
            pltpu.VMEM((blocks, 2, height, pixels), f32),
            pltpu.SemaphoreType.DMA((CHUNKS + 4,)),
        ],
        0,
        10 << 20,
        "sums",
    )
    sums, gathered = lax.optimization_barrier((sums, gathered))
    for offset in offsets[1:]:
        gathered = hop(gathered, offset)

    place = (2, height, length)
    send, keep_far, keep_near = call(
        functools.partial(insert_kernel, shape),
        [((half, *place), bf16), (((wide - 1) * far, *place), f32), ((far, *place), f32)],
        [hbm, hbm, vmem, vmem],
        (slabs, kind_rows, sums, tiles_near),
        [
            *pairs_scratch,
            pltpu.VMEM((kinds * rows + 2 * height, length), f32),
            pltpu.SMEM((devices * blocks,), jnp.int32),
            pltpu.SemaphoreType.DMA((2,)),
        ],
        2 * rows * pixels * kinds * length,
        8 << 20,
        "insert",
    )
    send, gathered = lax.optimization_barrier((send, gathered))
    mate = swap(send, 1)
    beyond = (keep_far + mate[far:].astype(f32)).astype(bf16)
    columns = [gathered]
    for x in range(1, wide):
        columns.append(lax.optimization_barrier((swap(gathered, x * cores), beyond))[0])
    columns += [swap(column, 1) for column in columns]
    if devices * kinds <= blocks * crossed:
        flat = pltpu.VMEM((kinds, devices * height, pixels), f32)
    else:
        flat = pltpu.VMEM((8, LANES), f32)
    (proj,) = call(
        functools.partial(project_kernel, shape),
        [((blocks, height, pixels), f32)],
        [hbm] * 2 + [vmem] * (1 + len(columns)),
        (slabs, kind_rows, tiles_near, *columns),
        [*pairs_scratch, pltpu.VMEM((devices * height, length), bf16), flat, pltpu.SemaphoreType.DMA((2,))],
        2 * devices * height * length * kinds * pixels,
        8 << 20,
        "project",
    )

    mine = keep_near + mate[:far].astype(f32)
    for x in range(1, wide):
        mine = mine + swap(beyond[(x - 1) * far : x * far], x * cores).astype(f32)
    proj, outgoing = lax.optimization_barrier((proj, mine.astype(bf16)))
    (scores,) = call(
        score_kernel,
        [((1, count), f32)],
        [hbm] * 2 + [vmem] * 3,
        (batch_block, inv_sigma2, proj, wave, images_near),
        [block_scratch, noise_scratch, pltpu.VMEM((count * 8, LANES), f32), pltpu.SemaphoreType.DMA((2,))],
        1 << 30,
        8 << 20,
        "scores",
    )
    total = mine[0]
    for z in range(1, far):
        total = total + swap(outgoing[z], z * wide * cores).astype(f32)
    return scores.reshape(count), total[0:1], total[1:2]


def solution(mesh):
    placed = (
        P(("parts", "slab"), None, None),
        P(),
        P(("parts", "slab"), None),
        P(("parts", "slab"), None),
        P(("parts", "slab")),
        P(("parts", "slab"), None, None),
        P(("parts", "slab")),
        P("parts", None),
    )
    return jax.shard_map(
        on_device,
        mesh=mesh,
        in_specs=placed,
        out_specs=(
            P(("parts", "slab")),
            P(("parts", "slab"), None, None),
            P(("parts", "slab"), None, None),
        ),
        check_vma=False,
    )
```

```python
import functools

import jax
import jax.numpy as jnp
from jax import lax
from jax.experimental import pallas as pl
from jax.experimental.pallas import tpu as pltpu
from jax.sharding import PartitionSpec as P

LANES = 128
CHUNKS = 4
VMEM_BYTES = 32 * 1024 * 1024


def grid_of(devices):
    cores = 2 if devices % 2 == 0 else 1
    chips = devices // cores
    wide = 1
    while (2 * wide) ** 3 <= chips:
        wide *= 2
    return chips // wide, wide, cores


def powers(size):
    return [1 << n for n in range(size.bit_length() - 1)]


def sin_cos(angle):
    turns = jnp.floor(angle * 0.3183098861837907 + 0.5)
    rest = angle - turns * 3.140625
    rest = rest - turns * 9.675025939941406e-4
    rest = rest - turns * 1.5099580252808664e-7
    half = turns * 0.5
    sign = 1.0 - 4.0 * (half - jnp.floor(half))
    sq = rest * rest
    sin = rest * (1.0 + sq * (-1.0 / 6 + sq * (1.0 / 120 + sq * (-1.0 / 5040 + sq * (1.0 / 362880 + sq * (-1.0 / 39916800))))))
    cos = 1.0 + sq * (-0.5 + sq * (1.0 / 24 + sq * (-1.0 / 720 + sq * (1.0 / 40320 + sq * (-1.0 / 3628800 + sq * (1.0 / 479001600))))))
    return sign * sin, sign * cos


def tables(defocus_ref, height, pixels, line_ref, pixel_ref):
    images = defocus_ref.shape[1]
    defocus = defocus_ref[...]
    rows = lax.broadcasted_iota(jnp.int32, (height, images), 0)
    line = ((rows // 2 + 1).astype(jnp.float32) / (height // 2)) ** 2
    line_ref[0], line_ref[1] = sin_cos(defocus * line + 0.3)
    column = jnp.transpose(jnp.broadcast_to(defocus, (LANES, images)))
    part = 32
    lanes = lax.broadcasted_iota(jnp.int32, (part, LANES), 1)
    for n in range(images // part):
        rows = slice(n * part, (n + 1) * part)
        for m in range(pixels // LANES):
            pixel = ((lanes + (m * LANES + 1)).astype(jnp.float32) / pixels) ** 2
            at = slice(m * LANES, (m + 1) * LANES)
            pixel_ref[0, rows, at], pixel_ref[1, rows, at] = sin_cos(column[rows] * pixel)


def contrast_of(line_ref, pixel_ref, i):
    sin_line, cos_line = line_ref[0, :, i : i + 1], line_ref[1, :, i : i + 1]
    return sin_line * pixel_ref[1, i : i + 1, :] + cos_line * pixel_ref[0, i : i + 1, :]


def copies(pairs, sems):
    started = [pltpu.make_async_copy(source, target, sems.at[n]) for n, (source, target) in enumerate(pairs)]
    for copy in started:
        copy.start()
    return started


def sum_kernel(block_hbm, defocus_hbm, noise_hbm, tiles_hbm, images_hbm,
               sums_ref, wave_ref, tiles_ref, images_ref,
               block_ref, defocus_ref, noise_ref, line_ref, pixel_ref, acc_ref, sems):
    count = images_ref.shape[0]
    part = count // CHUNKS
    small = [(defocus_hbm, defocus_ref), (block_hbm, block_ref), (noise_hbm, noise_ref)]
    large = [(images_hbm.at[pl.ds(n * part, part)], images_ref.at[pl.ds(n * part, part)]) for n in range(CHUNKS)]
    started = copies(small + large, sems)
    last = pltpu.make_async_copy(tiles_hbm, tiles_ref, sems.at[len(started)])
    height, pixels = noise_ref.shape
    batches = block_ref.shape[0]
    size = count // batches
    acc_ref[...] = jnp.zeros_like(acc_ref)
    for copy in started[: len(small)]:
        copy.wait()
    tables(defocus_ref, height, pixels, line_ref, pixel_ref)
    for b in range(batches):
        if b % (batches // CHUNKS) == 0:
            started[len(small) + b // (batches // CHUNKS)].wait()
        if b == 0:
            last.start()
        data = jnp.zeros((height, pixels), jnp.float32)
        weight = jnp.zeros((height, pixels), jnp.float32)
        for j in range(size):
            i = b * size + j
            wave = contrast_of(line_ref, pixel_ref, i)
            wave_ref[i] = wave
            data = data + wave * images_ref[i].astype(jnp.float32)
            weight = weight + wave * wave
        k = block_ref[b]
        acc_ref[k, 0] = acc_ref[k, 0] + data
        acc_ref[k, 1] = acc_ref[k, 1] + weight
    sums = (acc_ref[...] * noise_ref[...][None, None]).astype(jnp.bfloat16)
    sums_ref[...] = sums.reshape(sums_ref.shape)
    last.wait()


def insert_kernel(shape, slab_hbm, tile_hbm, sums_ref, tiles_ref, send_ref, far_ref, near_ref,
                  slab_ref, tile_ref, parts_ref, place_ref, count_ref, sems):
    far, wide, cores = shape
    started = copies([(slab_hbm, slab_ref), (tile_hbm, tile_ref)], sems)
    crossed, blocks = slab_ref.shape
    kinds = tiles_ref.shape[0]
    rows = sums_ref.shape[0]
    height = rows // (2 * blocks)
    devices = count_ref.shape[0]

    def multiply(t):
        parts_ref[t * rows : (t + 1) * rows, :] = lax.dot_general(
            sums_ref[...], tiles_ref[t], (((1,), (1,)), ((), ())), preferred_element_type=jnp.float32
        )

    parts_ref[pl.ds(kinds * rows, 2 * height), :] = jnp.zeros((2 * height, parts_ref.shape[1]), jnp.float32)
    for t in range(kinds // 2):
        multiply(t)

    for copy in started:
        copy.wait()
    stride = blocks + 1

    def clear(s, carry):
        count_ref[s] = 0
        return carry

    def close(s, carry):
        place_ref[s * stride + count_ref[s]] = kinds * rows
        return carry

    lax.fori_loop(0, devices, clear, 0, unroll=devices <= 16)
    for k in range(blocks):
        for r in range(crossed):
            s = slab_ref[r, k]
            at = count_ref[s]
            place_ref[s * stride + at] = tile_ref[r, k] * rows + k * 2 * height
            count_ref[s] = at + 1
    lax.fori_loop(0, devices, close, 0, unroll=devices <= 16)
    for t in range(kinds // 2, kinds):
        multiply(t)
    me = lax.axis_index("slab")

    def total(x, z, core):
        s = me ^ ((z * wide + x) * cores + core)

        def rows_of(n):
            return parts_ref[pl.ds(pl.multiple_of(place_ref[s * stride + n], 2 * height), 2 * height), :]

        def add_two(n, acc):
            return acc + rows_of(2 * n) + rows_of(2 * n + 1)

        zero = jnp.zeros((2 * height, parts_ref.shape[1]), jnp.float32)
        return lax.fori_loop(0, (count_ref[s] + 1) >> 1, add_two, zero)

    def fill(ref, start, core):
        def step(slot, carry):
            x, z = start + slot // far, lax.rem(slot, far)
            ref[slot] = total(x, z, core).astype(ref.dtype).reshape(2, height, parts_ref.shape[1])
            return carry

        lax.fori_loop(0, ref.shape[0], step, 0)

    fill(send_ref, 0, 1)
    fill(far_ref, 1, 0)
    fill(near_ref, 0, 0)


def project_kernel(shape, slab_hbm, tile_hbm, tiles_ref, *refs):
    far, wide, cores = shape
    columns, refs = refs[: wide * cores], refs[wide * cores :]
    proj_ref, slab_ref, tile_ref, lines_ref, flat_ref, sems = refs
    started = copies([(slab_hbm, slab_ref), (tile_hbm, tile_ref)], sems)
    crossed, blocks = slab_ref.shape
    kinds = tiles_ref.shape[0]
    _, height, length = columns[0].shape
    dense = far * len(columns) * kinds <= crossed * blocks
    for n, ref in enumerate(columns):
        core, x = n // wide, n % wide
        for z in range(far):
            away = (z * wide + x) * cores + core
            lines_ref[away * height : (away + 1) * height, :] = ref[z]
    if dense:
        for t in range(kinds):
            flat_ref[t] = jnp.dot(lines_ref[...], tiles_ref[t], preferred_element_type=jnp.float32)
    for copy in started:
        copy.wait()
    me = lax.axis_index("slab")

    def project(k, carry):
        acc = None
        for r in range(crossed):
            t = tile_ref[r, k]
            rows = pl.ds(pl.multiple_of((me ^ slab_ref[r, k]) * height, height), height)
            if dense:
                part = flat_ref[t, rows, :]
            else:
                part = jnp.dot(lines_ref[rows, :], tiles_ref[t], preferred_element_type=jnp.float32)
            acc = part if acc is None else acc + part
        proj_ref[k] = acc
        return carry

    lax.fori_loop(0, blocks, project, 0, unroll=dense)


def score_kernel(block_hbm, noise_hbm, proj_ref, wave_ref, images_ref, score_ref, block_ref, noise_ref, part_ref, sems):
    started = copies([(block_hbm, block_ref), (noise_hbm, noise_ref)], sems)
    height, pixels = noise_ref.shape
    batches = block_ref.shape[0]
    count = images_ref.shape[0]
    size = count // batches
    for copy in started:
        copy.wait()
    noise = noise_ref[...]
    for b in range(batches):
        proj = proj_ref[block_ref[b]]
        for j in range(size):
            i = b * size + j
            residual = images_ref[i].astype(jnp.float32) - wave_ref[i] * proj
            power = residual * residual * noise
            power = sum(power[n * 8 : (n + 1) * 8] for n in range(height // 8))
            part_ref[i * 8 : (i + 1) * 8, :] = sum(power[:, n * LANES : (n + 1) * LANES] for n in range(pixels // LANES))
    total = sum(part_ref[pl.ds(n, count, 8), :] for n in range(8))
    total = jnp.sum(jnp.transpose(total), axis=0, keepdims=True)
    score_ref[...] = total * (1.0 / (height * pixels))


def on_device(volume, tiles, slab_ids, tile_ids, batch_block, images, defocus, inv_sigma2):
    blocks, crossed = slab_ids.shape
    height, length = volume.shape[1:]
    count, _, pixels = images.shape
    kinds = tiles.shape[0]
    devices = lax.axis_size("slab")
    shape = far, wide, cores = grid_of(devices)
    half = devices // 2
    rows = blocks * 2 * height
    slabs, kind_rows, row = slab_ids.T, tile_ids.T, defocus.reshape(1, count)

    def swap(array, offset):
        return lax.ppermute(array, "slab", [(i, i ^ offset) for i in range(devices)])

    vmem = pl.BlockSpec(memory_space=pltpu.VMEM)
    hbm = pl.BlockSpec(memory_space=pltpu.HBM)
    params = pltpu.CompilerParams(vmem_limit_bytes=VMEM_BYTES)
    f32, bf16 = jnp.float32, jnp.bfloat16
    pairs_scratch = [pltpu.SMEM((crossed, blocks), jnp.int32), pltpu.SMEM((crossed, blocks), jnp.int32)]
    block_scratch = pltpu.SMEM(batch_block.shape, jnp.int32)
    noise_scratch = pltpu.VMEM((height, pixels), f32)

    def call(kernel, outs, inputs, operands, scratch, flops, moved, name):
        operands = [
            pltpu.with_memory_space_constraint(x, pltpu.HBM) if spec is hbm else x for x, spec in zip(operands, inputs)
        ]
        return pl.pallas_call(
            kernel,
            out_shape=tuple(jax.ShapeDtypeStruct(s, t) for s, t in outs),
            in_specs=inputs,
            out_specs=(vmem,) * len(outs),
            scratch_shapes=scratch,
            compiler_params=params,
            cost_estimate=pl.CostEstimate(flops=flops, bytes_accessed=moved, transcendentals=0),
            name=name,
        )(*operands)

    def hop(array, offset):
        return jnp.concatenate([array, swap(array, offset)], axis=0)

    offsets = [z * wide * cores for z in powers(far)]
    gathered = hop(volume, offsets[0])

    sums, wave, tiles_near, images_near = call(
        sum_kernel,
        [((rows, pixels), bf16), (images.shape, f32), (tiles.shape, bf16), (images.shape, bf16)],
        [hbm] * 5,
        (batch_block, row, inv_sigma2, tiles, images),
        [
            block_scratch,
            pltpu.VMEM((1, count), f32),
            noise_scratch,
            pltpu.VMEM((2, height, count), f32),
            pltpu.VMEM((2, count, pixels), f32),
            pltpu.VMEM((blocks, 2, height, pixels), f32),
            pltpu.SemaphoreType.DMA((CHUNKS + 4,)),
        ],
        0,
        10 << 20,
        "sums",
    )
    sums, gathered = lax.optimization_barrier((sums, gathered))
    for offset in offsets[1:]:
        gathered = hop(gathered, offset)

    place = (2, height, length)
    send, keep_far, keep_near = call(
        functools.partial(insert_kernel, shape),
        [((half, *place), bf16), (((wide - 1) * far, *place), f32), ((far, *place), f32)],
        [hbm, hbm, vmem, vmem],
        (slabs, kind_rows, sums, tiles_near),
        [
            *pairs_scratch,
            pltpu.VMEM((kinds * rows + 2 * height, length), f32),
            pltpu.SMEM((devices * (blocks + 1),), jnp.int32),
            pltpu.SMEM((devices,), jnp.int32),
            pltpu.SemaphoreType.DMA((2,)),
        ],
        2 * rows * pixels * kinds * length,
        8 << 20,
        "insert",
    )
    send, gathered = lax.optimization_barrier((send, gathered))
    mate = swap(send, 1)
    beyond = (keep_far + mate[far:].astype(f32)).astype(bf16)
    columns = [gathered]
    for x in range(1, wide):
        columns.append(lax.optimization_barrier((swap(gathered, x * cores), beyond))[0])
    columns += [swap(column, 1) for column in columns]
    if devices * kinds <= blocks * crossed:
        flat = pltpu.VMEM((kinds, devices * height, pixels), f32)
    else:
        flat = pltpu.VMEM((8, LANES), f32)
    (proj,) = call(
        functools.partial(project_kernel, shape),
        [((blocks, height, pixels), f32)],
        [hbm] * 2 + [vmem] * (1 + len(columns)),
        (slabs, kind_rows, tiles_near, *columns),
        [*pairs_scratch, pltpu.VMEM((devices * height, length), bf16), flat, pltpu.SemaphoreType.DMA((2,))],
        2 * devices * height * length * kinds * pixels,
        8 << 20,
        "project",
    )

    mine = keep_near + mate[:far].astype(f32)
    for x in range(1, wide):
        mine = mine + swap(beyond[(x - 1) * far : x * far], x * cores).astype(f32)
    proj, outgoing = lax.optimization_barrier((proj, mine.astype(bf16)))
    (scores,) = call(
        score_kernel,
        [((1, count), f32)],
        [hbm] * 2 + [vmem] * 3,
        (batch_block, inv_sigma2, proj, wave, images_near),
        [block_scratch, noise_scratch, pltpu.VMEM((count * 8, LANES), f32), pltpu.SemaphoreType.DMA((2,))],
        1 << 30,
        8 << 20,
        "scores",
    )
    total = mine[0]
    for z in range(1, far):
        total = total + swap(outgoing[z], z * wide * cores).astype(f32)
    return scores.reshape(count), total[0:1], total[1:2]


def solution(mesh):
    placed = (
        P(("parts", "slab"), None, None),
        P(),
        P(("parts", "slab"), None),
        P(("parts", "slab"), None),
        P(("parts", "slab")),
        P(("parts", "slab"), None, None),
        P(("parts", "slab")),
        P("parts", None),
    )
    return jax.shard_map(
        on_device,
        mesh=mesh,
        in_specs=placed,
        out_specs=(
            P(("parts", "slab")),
            P(("parts", "slab"), None, None),
            P(("parts", "slab"), None, None),
        ),
        check_vma=False,
    )
```

```python
import functools

import jax
import jax.numpy as jnp
from jax import lax
from jax.experimental import pallas as pl
from jax.experimental.pallas import tpu as pltpu
from jax.sharding import PartitionSpec as P

LANES = 128
CHUNKS = 4
VMEM_BYTES = 32 * 1024 * 1024


def grid_of(devices):
    cores = 2 if devices % 2 == 0 else 1
    chips = devices // cores
    wide = 1
    while (2 * wide) ** 3 <= chips:
        wide *= 2
    return chips // wide, wide, cores


def powers(size):
    return [1 << n for n in range(size.bit_length() - 1)]


def sin_cos(angle):
    turns = jnp.floor(angle * 0.3183098861837907 + 0.5)
    rest = angle - turns * 3.140625
    rest = rest - turns * 9.675025939941406e-4
    rest = rest - turns * 1.5099580252808664e-7
    half = turns * 0.5
    sign = 1.0 - 4.0 * (half - jnp.floor(half))
    sq = rest * rest
    sin = rest * (1.0 + sq * (-1.0 / 6 + sq * (1.0 / 120 + sq * (-1.0 / 5040 + sq * (1.0 / 362880 + sq * (-1.0 / 39916800))))))
    cos = 1.0 + sq * (-0.5 + sq * (1.0 / 24 + sq * (-1.0 / 720 + sq * (1.0 / 40320 + sq * (-1.0 / 3628800 + sq * (1.0 / 479001600))))))
    return sign * sin, sign * cos


def tables(defocus_ref, height, pixels, line_ref, pixel_ref):
    images = defocus_ref.shape[1]
    defocus = defocus_ref[...]
    rows = lax.broadcasted_iota(jnp.int32, (height, images), 0)
    line = ((rows // 2 + 1).astype(jnp.float32) / (height // 2)) ** 2
    line_ref[0], line_ref[1] = sin_cos(defocus * line + 0.3)
    column = jnp.transpose(jnp.broadcast_to(defocus, (LANES, images)))
    part = 32
    lanes = lax.broadcasted_iota(jnp.int32, (part, LANES), 1)
    for n in range(images // part):
        rows = slice(n * part, (n + 1) * part)
        for m in range(pixels // LANES):
            pixel = ((lanes + (m * LANES + 1)).astype(jnp.float32) / pixels) ** 2
            at = slice(m * LANES, (m + 1) * LANES)
            pixel_ref[0, rows, at], pixel_ref[1, rows, at] = sin_cos(column[rows] * pixel)


def contrast_of(line_ref, pixel_ref, i):
    sin_line, cos_line = line_ref[0, :, i : i + 1], line_ref[1, :, i : i + 1]
    return sin_line * pixel_ref[1, i : i + 1, :] + cos_line * pixel_ref[0, i : i + 1, :]


def copies(pairs, sems):
    started = [pltpu.make_async_copy(source, target, sems.at[n]) for n, (source, target) in enumerate(pairs)]
    for copy in started:
        copy.start()
    return started


def row_tables(shape, kinds, height, slab, tile, place_ref, route_ref):
    far, wide, cores = shape
    devices, blocks = place_ref.shape
    rows, half = blocks * 2 * height, devices // 2
    me = lax.axis_index("slab")
    slot = lax.broadcasted_iota(jnp.int32, (devices, blocks), 0)
    block = lax.broadcasted_iota(jnp.int32, (devices, blocks), 1)
    within = slot & (half - 1)
    core = jnp.where(slot < half, cores - 1, 0)
    named = me ^ (((within & (far - 1)) * wide + within // far) * cores + core)
    place = jnp.full((devices, blocks), kinds * rows, jnp.int32)
    for r in range(slab.shape[0]):
        row = tile[r : r + 1, :] * rows + block * (2 * height)
        place = jnp.where(slab[r : r + 1, :] == named, row, place)
    place_ref[...] = place
    route_ref[...] = (tile * devices + (me ^ slab)) * height


def sum_kernel(shape, kinds, slab_hbm, tile_hbm, block_hbm, defocus_hbm, noise_hbm, tiles_hbm, images_hbm,
               sums_ref, wave_ref, tiles_ref, images_ref, place_ref, route_ref,
               slab_ref, tile_ref, block_ref, defocus_ref, noise_ref, line_ref, pixel_ref, acc_ref, sems):
    count = images_ref.shape[0]
    part = count // CHUNKS
    small = [(defocus_hbm, defocus_ref), (block_hbm, block_ref), (noise_hbm, noise_ref), (slab_hbm, slab_ref), (tile_hbm, tile_ref)]
    large = [(images_hbm.at[pl.ds(n * part, part)], images_ref.at[pl.ds(n * part, part)]) for n in range(CHUNKS)]
    started = copies(small + large, sems)
    last = pltpu.make_async_copy(tiles_hbm, tiles_ref, sems.at[len(started)])
    height, pixels = noise_ref.shape
    batches = block_ref.shape[0]
    size = count // batches
    acc_ref[...] = jnp.zeros_like(acc_ref)
    for copy in started[: len(small)]:
        copy.wait()
    tables(defocus_ref, height, pixels, line_ref, pixel_ref)
    row_tables(shape, kinds, height, slab_ref[...], tile_ref[...], place_ref, route_ref)
    for b in range(batches):
        if b % (batches // CHUNKS) == 0:
            started[len(small) + b // (batches // CHUNKS)].wait()
        if b == 0:
            last.start()
        data = jnp.zeros((height, pixels), jnp.float32)
        weight = jnp.zeros((height, pixels), jnp.float32)
        for j in range(size):
            i = b * size + j
            wave = contrast_of(line_ref, pixel_ref, i)
            wave_ref[i] = wave
            data = data + wave * images_ref[i].astype(jnp.float32)
            weight = weight + wave * wave
        k = block_ref[b]
        acc_ref[k, 0] = acc_ref[k, 0] + data
        acc_ref[k, 1] = acc_ref[k, 1] + weight
    sums = (acc_ref[...] * noise_ref[...][None, None]).astype(jnp.bfloat16)
    sums_ref[...] = sums.reshape(sums_ref.shape)
    last.wait()


def insert_kernel(shape, place_vmem, sums_ref, tiles_ref, send_ref, far_ref, near_ref, parts_ref, place_ref, sems):
    far, wide, cores = shape
    (started,) = copies([(place_vmem, place_ref)], sems)
    devices, blocks = place_ref.shape
    kinds = tiles_ref.shape[0]
    rows = sums_ref.shape[0]
    length = parts_ref.shape[1]
    height = rows // (2 * blocks)
    half = devices // 2
    parts_ref[pl.ds(kinds * rows, 2 * height), :] = jnp.zeros((2 * height, length), jnp.float32)
    for t in range(kinds):
        parts_ref[t * rows : (t + 1) * rows, :] = lax.dot_general(
            sums_ref[...], tiles_ref[t], (((1,), (1,)), ((), ())), preferred_element_type=jnp.float32
        )
    started.wait()

    def fill(ref, start):
        def step(slot, carry):
            acc = None
            for k in range(blocks):
                at = pl.multiple_of(place_ref[start + slot, k], 2 * height)
                part = parts_ref[pl.ds(at, 2 * height), :]
                acc = part if acc is None else acc + part
            ref[slot] = acc.astype(ref.dtype).reshape(2, height, length)
            return carry

        lax.fori_loop(0, ref.shape[0], step, 0)

    fill(send_ref, 0)
    fill(far_ref, half + far)
    fill(near_ref, half)


def project_kernel(shape, route_vmem, tiles_ref, *refs):
    far, wide, cores = shape
    columns, refs = refs[: wide * cores], refs[wide * cores :]
    proj_ref, route_ref, lines_ref, flat_ref, sems = refs
    (started,) = copies([(route_vmem, route_ref)], sems)
    crossed, blocks = route_ref.shape
    kinds = tiles_ref.shape[0]
    height = columns[0].shape[1]
    rows = lines_ref.shape[0]
    dense = far * len(columns) * kinds <= crossed * blocks
    for n, ref in enumerate(columns):
        core, x = n // wide, n % wide
        for z in range(far):
            away = (z * wide + x) * cores + core
            lines_ref[away * height : (away + 1) * height, :] = ref[z]
    if dense:
        for t in range(kinds):
            flat_ref[t * rows : (t + 1) * rows, :] = jnp.dot(lines_ref[...], tiles_ref[t], preferred_element_type=jnp.float32)
    started.wait()

    def project(k, carry):
        acc = None
        for r in range(crossed):
            at = route_ref[r, k]
            if dense:
                part = flat_ref[pl.ds(pl.multiple_of(at, height), height), :]
            else:
                t, at = at // rows, pl.multiple_of(lax.rem(at, rows), height)
                part = jnp.dot(lines_ref[pl.ds(at, height), :], tiles_ref[t], preferred_element_type=jnp.float32)
            acc = part if acc is None else acc + part
        proj_ref[k] = acc
        return carry

    lax.fori_loop(0, blocks, project, 0, unroll=dense)


def score_kernel(block_hbm, noise_hbm, proj_ref, wave_ref, images_ref, score_ref, block_ref, noise_ref, part_ref, sems):
    started = copies([(block_hbm, block_ref), (noise_hbm, noise_ref)], sems)
    height, pixels = noise_ref.shape
    batches = block_ref.shape[0]
    count = images_ref.shape[0]
    size = count // batches
    for copy in started:
        copy.wait()
    noise = noise_ref[...]
    for b in range(batches):
        proj = proj_ref[block_ref[b]]
        for j in range(size):
            i = b * size + j
            residual = images_ref[i].astype(jnp.float32) - wave_ref[i] * proj
            power = residual * residual * noise
            power = sum(power[n * 8 : (n + 1) * 8] for n in range(height // 8))
            part_ref[i * 8 : (i + 1) * 8, :] = sum(power[:, n * LANES : (n + 1) * LANES] for n in range(pixels // LANES))
    total = sum(part_ref[pl.ds(n, count, 8), :] for n in range(8))
    total = jnp.sum(jnp.transpose(total), axis=0, keepdims=True)
    score_ref[...] = total * (1.0 / (height * pixels))


def on_device(volume, tiles, slab_ids, tile_ids, batch_block, images, defocus, inv_sigma2):
    blocks, crossed = slab_ids.shape
    height, length = volume.shape[1:]
    count, _, pixels = images.shape
    kinds = tiles.shape[0]
    devices = lax.axis_size("slab")
    shape = far, wide, cores = grid_of(devices)
    half = devices // 2
    rows = blocks * 2 * height
    slabs, kind_rows, row = slab_ids.T, tile_ids.T, defocus.reshape(1, count)

    def swap(array, offset):
        return lax.ppermute(array, "slab", [(i, i ^ offset) for i in range(devices)])

    vmem = pl.BlockSpec(memory_space=pltpu.VMEM)
    hbm = pl.BlockSpec(memory_space=pltpu.HBM)
    params = pltpu.CompilerParams(vmem_limit_bytes=VMEM_BYTES)
    f32, bf16 = jnp.float32, jnp.bfloat16
    i32 = jnp.int32
    block_scratch = pltpu.SMEM(batch_block.shape, jnp.int32)
    noise_scratch = pltpu.VMEM((height, pixels), f32)

    def call(kernel, outs, inputs, operands, scratch, flops, moved, name):
        operands = [
            pltpu.with_memory_space_constraint(x, pltpu.HBM) if spec is hbm else x for x, spec in zip(operands, inputs)
        ]
        return pl.pallas_call(
            kernel,
            out_shape=tuple(jax.ShapeDtypeStruct(s, t) for s, t in outs),
            in_specs=inputs,
            out_specs=(vmem,) * len(outs),
            scratch_shapes=scratch,
            compiler_params=params,
            cost_estimate=pl.CostEstimate(flops=flops, bytes_accessed=moved, transcendentals=0),
            name=name,
        )(*operands)

    def hop(array, offset):
        return jnp.concatenate([array, swap(array, offset)], axis=0)

    offsets = [z * wide * cores for z in powers(far)]
    gathered = hop(volume, offsets[0])

    sums, wave, tiles_near, images_near, place_rows, route_rows = call(
        functools.partial(sum_kernel, shape, kinds),
        [
            ((rows, pixels), bf16),
            (images.shape, f32),
            (tiles.shape, bf16),
            (images.shape, bf16),
            ((devices, blocks), i32),
            ((crossed, blocks), i32),
        ],
        [hbm] * 7,
        (slabs, kind_rows, batch_block, row, inv_sigma2, tiles, images),
        [
            pltpu.VMEM((crossed, blocks), i32),
            pltpu.VMEM((crossed, blocks), i32),
            block_scratch,
            pltpu.VMEM((1, count), f32),
            noise_scratch,
            pltpu.VMEM((2, height, count), f32),
            pltpu.VMEM((2, count, pixels), f32),
            pltpu.VMEM((blocks, 2, height, pixels), f32),
            pltpu.SemaphoreType.DMA((CHUNKS + 6,)),
        ],
        0,
        10 << 20,
        "sums",
    )
    sums, gathered = lax.optimization_barrier((sums, gathered))
    for offset in offsets[1:]:
        gathered = hop(gathered, offset)

    place = (2, height, length)
    send, keep_far, keep_near = call(
        functools.partial(insert_kernel, shape),
        [((half, *place), bf16), (((wide - 1) * far, *place), f32), ((far, *place), f32)],
        [vmem] * 3,
        (place_rows, sums, tiles_near),
        [
            pltpu.VMEM((kinds * rows + 2 * height, length), f32),
            pltpu.SMEM((devices, blocks), i32),
            pltpu.SemaphoreType.DMA((1,)),
        ],
        2 * rows * pixels * kinds * length,
        8 << 20,
        "insert",
    )
    send, gathered = lax.optimization_barrier((send, gathered))
    mate = swap(send, 1)
    beyond = (keep_far + mate[far:].astype(f32)).astype(bf16)
    columns = [gathered]
    for x in range(1, wide):
        columns.append(lax.optimization_barrier((swap(gathered, x * cores), beyond))[0])
    columns += [swap(column, 1) for column in columns]
    if devices * kinds <= blocks * crossed:
        flat = pltpu.VMEM((kinds * devices * height, pixels), f32)
    else:
        flat = pltpu.VMEM((8, LANES), f32)
    (proj,) = call(
        functools.partial(project_kernel, shape),
        [((blocks, height, pixels), f32)],
        [vmem] * (2 + len(columns)),
        (route_rows, tiles_near, *columns),
        [pltpu.SMEM((crossed, blocks), i32), pltpu.VMEM((devices * height, length), bf16), flat, pltpu.SemaphoreType.DMA((1,))],
        2 * devices * height * length * kinds * pixels,
        8 << 20,
        "project",
    )

    mine = keep_near + mate[:far].astype(f32)
    for x in range(1, wide):
        mine = mine + swap(beyond[(x - 1) * far : x * far], x * cores).astype(f32)
    proj, outgoing = lax.optimization_barrier((proj, mine.astype(bf16)))
    (scores,) = call(
        score_kernel,
        [((1, count), f32)],
        [hbm] * 2 + [vmem] * 3,
        (batch_block, inv_sigma2, proj, wave, images_near),
        [block_scratch, noise_scratch, pltpu.VMEM((count * 8, LANES), f32), pltpu.SemaphoreType.DMA((2,))],
        1 << 30,
        8 << 20,
        "scores",
    )
    total = mine[0]
    for z in range(1, far):
        total = total + swap(outgoing[z], z * wide * cores).astype(f32)
    return scores.reshape(count), total[0:1], total[1:2]


def solution(mesh):
    placed = (
        P(("parts", "slab"), None, None),
        P(),
        P(("parts", "slab"), None),
        P(("parts", "slab"), None),
        P(("parts", "slab")),
        P(("parts", "slab"), None, None),
        P(("parts", "slab")),
        P("parts", None),
    )
    return jax.shard_map(
        on_device,
        mesh=mesh,
        in_specs=placed,
        out_specs=(
            P(("parts", "slab")),
            P(("parts", "slab"), None, None),
            P(("parts", "slab"), None, None),
        ),
        check_vma=False,
    )
```

```python
import functools

import jax
import jax.numpy as jnp
from jax import lax
from jax.experimental import pallas as pl
from jax.experimental.pallas import tpu as pltpu
from jax.sharding import PartitionSpec as P

LANES = 128
CHUNKS = 4
VMEM_BYTES = 24 * 1024 * 1024


def grid_of(devices):
    cores = 2 if devices % 2 == 0 else 1
    chips = devices // cores
    wide = 1
    while (2 * wide) ** 3 <= chips:
        wide *= 2
    return chips // wide, wide, cores


def powers(size):
    return [1 << n for n in range(size.bit_length() - 1)]


def sin_cos(angle):
    turns = jnp.floor(angle * 0.3183098861837907 + 0.5)
    rest = angle - turns * 3.140625
    rest = rest - turns * 9.675025939941406e-4
    rest = rest - turns * 1.5099580252808664e-7
    half = turns * 0.5
    sign = 1.0 - 4.0 * (half - jnp.floor(half))
    sq = rest * rest
    sin = rest * (1.0 + sq * (-1.0 / 6 + sq * (1.0 / 120 + sq * (-1.0 / 5040 + sq * (1.0 / 362880 + sq * (-1.0 / 39916800))))))
    cos = 1.0 + sq * (-0.5 + sq * (1.0 / 24 + sq * (-1.0 / 720 + sq * (1.0 / 40320 + sq * (-1.0 / 3628800 + sq * (1.0 / 479001600))))))
    return sign * sin, sign * cos


def tables(defocus_ref, height, pixels, line_ref, pixel_ref):
    images = defocus_ref.shape[1]
    defocus = defocus_ref[...]
    rows = lax.broadcasted_iota(jnp.int32, (height, images), 0)
    line = ((rows // 2 + 1).astype(jnp.float32) / (height // 2)) ** 2
    line_ref[0], line_ref[1] = sin_cos(defocus * line + 0.3)
    column = jnp.transpose(jnp.broadcast_to(defocus, (LANES, images)))
    part = 32
    lanes = lax.broadcasted_iota(jnp.int32, (part, LANES), 1)
    for n in range(images // part):
        rows = slice(n * part, (n + 1) * part)
        for m in range(pixels // LANES):
            pixel = ((lanes + (m * LANES + 1)).astype(jnp.float32) / pixels) ** 2
            at = slice(m * LANES, (m + 1) * LANES)
            pixel_ref[0, rows, at], pixel_ref[1, rows, at] = sin_cos(column[rows] * pixel)


def contrast_of(line_ref, pixel_ref, i):
    sin_line, cos_line = line_ref[0, :, i : i + 1], line_ref[1, :, i : i + 1]
    return sin_line * pixel_ref[1, i : i + 1, :] + cos_line * pixel_ref[0, i : i + 1, :]


def copies(pairs, sems):
    started = [pltpu.make_async_copy(source, target, sems.at[n]) for n, (source, target) in enumerate(pairs)]
    for copy in started:
        copy.start()
    return started


def row_tables(shape, kinds, height, slab, tile, place_ref, route_ref):
    far, wide, cores = shape
    devices, blocks = place_ref.shape
    rows, half = blocks * 2 * height, devices // 2
    me = lax.axis_index("slab")
    slot = lax.broadcasted_iota(jnp.int32, (devices, blocks), 0)
    block = lax.broadcasted_iota(jnp.int32, (devices, blocks), 1)
    within = slot & (half - 1)
    core = jnp.where(slot < half, cores - 1, 0)
    named = me ^ (((within & (far - 1)) * wide + within // far) * cores + core)
    place = jnp.full((devices, blocks), kinds * rows, jnp.int32)
    for r in range(slab.shape[0]):
        row = tile[r : r + 1, :] * rows + block * (2 * height)
        place = jnp.where(slab[r : r + 1, :] == named, row, place)
    place_ref[...] = place
    route_ref[...] = (tile * devices + (me ^ slab)) * height


def sum_kernel(shape, kinds, slab_hbm, tile_hbm, block_hbm, defocus_hbm, noise_hbm, tiles_hbm, images_hbm,
               sums_ref, wave_ref, tiles_ref, images_ref, place_ref, route_ref,
               slab_ref, tile_ref, block_ref, defocus_ref, noise_ref, line_ref, pixel_ref, acc_ref, sems):
    count = images_ref.shape[0]
    part = count // CHUNKS
    small = [(defocus_hbm, defocus_ref), (block_hbm, block_ref), (noise_hbm, noise_ref), (slab_hbm, slab_ref), (tile_hbm, tile_ref)]
    large = [(images_hbm.at[pl.ds(n * part, part)], images_ref.at[pl.ds(n * part, part)]) for n in range(CHUNKS)]
    started = copies(small + large, sems)
    last = pltpu.make_async_copy(tiles_hbm, tiles_ref, sems.at[len(started)])
    height, pixels = noise_ref.shape
    batches = block_ref.shape[0]
    size = count // batches
    acc_ref[...] = jnp.zeros_like(acc_ref)
    for copy in started[: len(small)]:
        copy.wait()
    tables(defocus_ref, height, pixels, line_ref, pixel_ref)
    row_tables(shape, kinds, height, slab_ref[...], tile_ref[...], place_ref, route_ref)
    for b in range(batches):
        if b % (batches // CHUNKS) == 0:
            started[len(small) + b // (batches // CHUNKS)].wait()
        if b == 0:
            last.start()
        data = jnp.zeros((height, pixels), jnp.float32)
        weight = jnp.zeros((height, pixels), jnp.float32)
        for j in range(size):
            i = b * size + j
            wave = contrast_of(line_ref, pixel_ref, i)
            wave_ref[i] = wave
            data = data + wave * images_ref[i].astype(jnp.float32)
            weight = weight + wave * wave
        k = block_ref[b]
        acc_ref[k, 0] = acc_ref[k, 0] + data
        acc_ref[k, 1] = acc_ref[k, 1] + weight
    sums = (acc_ref[...] * noise_ref[...][None, None]).astype(jnp.bfloat16)
    sums_ref[...] = sums.reshape(sums_ref.shape)
    last.wait()


def fill(ref, start, place_ref, parts_ref, mate_ref=None, offset=0):
    sides, height, length = ref.shape[1:]

    def step(slot, carry):
        acc = None
        for k in range(place_ref.shape[1]):
            at = pl.multiple_of(place_ref[start + slot, k], sides * height)
            part = parts_ref[pl.ds(at, sides * height), :]
            acc = part if acc is None else acc + part
        acc = acc.reshape(sides, height, length)
        if mate_ref is not None:
            acc = acc + mate_ref[offset + slot].astype(jnp.float32)
        ref[slot] = acc.astype(ref.dtype)
        return carry

    lax.fori_loop(0, ref.shape[0], step, 0)


def insert_kernel(place_vmem, sums_ref, tiles_ref, send_ref, parts_ref, place_ref, sems):
    (started,) = copies([(place_vmem, place_ref)], sems)
    kinds = tiles_ref.shape[0]
    rows = sums_ref.shape[0]
    zeros = parts_ref.shape[0] - kinds * rows
    parts_ref[kinds * rows :, :] = jnp.zeros((zeros, parts_ref.shape[1]), jnp.float32)
    for t in range(kinds):
        parts_ref[t * rows : (t + 1) * rows, :] = lax.dot_general(
            sums_ref[...], tiles_ref[t], (((1,), (1,)), ((), ())), preferred_element_type=jnp.float32
        )
    started.wait()
    fill(send_ref, 0, place_ref, parts_ref)


def keep_kernel(place_vmem, parts_ref, mate_ref, far_ref, near_ref, place_ref, sems):
    (started,) = copies([(place_vmem, place_ref)], sems)
    half, far = place_ref.shape[0] // 2, near_ref.shape[0]
    started.wait()
    fill(far_ref, half + far, place_ref, parts_ref, mate_ref, far)
    fill(near_ref, half, place_ref, parts_ref, mate_ref, 0)


def project_kernel(shape, route_vmem, tiles_ref, *refs):
    far, wide, cores = shape
    columns, refs = refs[: wide * cores], refs[wide * cores :]
    proj_ref, route_ref, lines_ref, flat_ref, sems = refs
    (started,) = copies([(route_vmem, route_ref)], sems)
    crossed, blocks = route_ref.shape
    kinds = tiles_ref.shape[0]
    height = columns[0].shape[1]
    rows = lines_ref.shape[0]
    dense = far * len(columns) * kinds <= crossed * blocks
    for n, ref in enumerate(columns):
        core, x = n // wide, n % wide
        for z in range(far):
            away = (z * wide + x) * cores + core
            lines_ref[away * height : (away + 1) * height, :] = ref[z]
    if dense:
        for t in range(kinds):
            flat_ref[t * rows : (t + 1) * rows, :] = jnp.dot(lines_ref[...], tiles_ref[t], preferred_element_type=jnp.float32)
    started.wait()

    def project(k, carry):
        acc = None
        for r in range(crossed):
            at = route_ref[r, k]
            if dense:
                part = flat_ref[pl.ds(pl.multiple_of(at, height), height), :]
            else:
                t, at = at // rows, pl.multiple_of(lax.rem(at, rows), height)
                part = jnp.dot(lines_ref[pl.ds(at, height), :], tiles_ref[t], preferred_element_type=jnp.float32)
            acc = part if acc is None else acc + part
        proj_ref[k] = acc
        return carry

    lax.fori_loop(0, blocks, project, 0, unroll=dense)


def score_kernel(block_hbm, noise_hbm, proj_ref, wave_ref, images_ref, score_ref, block_ref, noise_ref, part_ref, sems):
    started = copies([(block_hbm, block_ref), (noise_hbm, noise_ref)], sems)
    height, pixels = noise_ref.shape
    batches = block_ref.shape[0]
    count = images_ref.shape[0]
    size = count // batches
    for copy in started:
        copy.wait()
    noise = noise_ref[...]
    for b in range(batches):
        proj = proj_ref[block_ref[b]]
        for j in range(size):
            i = b * size + j
            residual = images_ref[i].astype(jnp.float32) - wave_ref[i] * proj
            power = residual * residual * noise
            power = sum(power[n * 8 : (n + 1) * 8] for n in range(height // 8))
            part_ref[i * 8 : (i + 1) * 8, :] = sum(power[:, n * LANES : (n + 1) * LANES] for n in range(pixels // LANES))
    total = sum(part_ref[pl.ds(n, count, 8), :] for n in range(8))
    total = jnp.sum(jnp.transpose(total), axis=0, keepdims=True)
    score_ref[...] = total * (1.0 / (height * pixels))


def on_device(volume, tiles, slab_ids, tile_ids, batch_block, images, defocus, inv_sigma2):
    blocks, crossed = slab_ids.shape
    height, length = volume.shape[1:]
    count, _, pixels = images.shape
    kinds = tiles.shape[0]
    devices = lax.axis_size("slab")
    shape = far, wide, cores = grid_of(devices)
    half = devices // 2
    rows = blocks * 2 * height
    slabs, kind_rows, row = slab_ids.T, tile_ids.T, defocus.reshape(1, count)

    def swap(array, offset):
        return lax.ppermute(array, "slab", [(i, i ^ offset) for i in range(devices)])

    vmem = pl.BlockSpec(memory_space=pltpu.VMEM)
    hbm = pl.BlockSpec(memory_space=pltpu.HBM)
    params = pltpu.CompilerParams(vmem_limit_bytes=VMEM_BYTES)
    f32, bf16 = jnp.float32, jnp.bfloat16
    i32 = jnp.int32
    block_scratch = pltpu.SMEM(batch_block.shape, jnp.int32)
    noise_scratch = pltpu.VMEM((height, pixels), f32)

    def call(kernel, outs, inputs, operands, scratch, flops, moved, name):
        operands = [
            pltpu.with_memory_space_constraint(x, pltpu.HBM) if spec is hbm else x for x, spec in zip(operands, inputs)
        ]
        return pl.pallas_call(
            kernel,
            out_shape=tuple(jax.ShapeDtypeStruct(s, t) for s, t in outs),
            in_specs=inputs,
            out_specs=(vmem,) * len(outs),
            scratch_shapes=scratch,
            compiler_params=params,
            cost_estimate=pl.CostEstimate(flops=flops, bytes_accessed=moved, transcendentals=0),
            name=name,
        )(*operands)

    def hop(array, offset):
        return jnp.concatenate([array, swap(array, offset)], axis=0)

    offsets = [z * wide * cores for z in powers(far)]
    gathered = hop(volume, offsets[0])

    sums, wave, tiles_near, images_near, place_rows, route_rows = call(
        functools.partial(sum_kernel, shape, kinds),
        [
            ((rows, pixels), bf16),
            (images.shape, f32),
            (tiles.shape, bf16),
            (images.shape, bf16),
            ((devices, blocks), i32),
            ((crossed, blocks), i32),
        ],
        [hbm] * 7,
        (slabs, kind_rows, batch_block, row, inv_sigma2, tiles, images),
        [
            pltpu.VMEM((crossed, blocks), i32),
            pltpu.VMEM((crossed, blocks), i32),
            block_scratch,
            pltpu.VMEM((1, count), f32),
            noise_scratch,
            pltpu.VMEM((2, height, count), f32),
            pltpu.VMEM((2, count, pixels), f32),
            pltpu.VMEM((blocks, 2, height, pixels), f32),
            pltpu.SemaphoreType.DMA((CHUNKS + 6,)),
        ],
        0,
        10 << 20,
        "sums",
    )

    place = (2, height, length)
    send, parts = call(
        insert_kernel,
        [((half, *place), bf16), ((kinds * rows + 2 * height, length), f32)],
        [vmem] * 3,
        (place_rows, sums, tiles_near),
        [pltpu.SMEM((devices, blocks), i32), pltpu.SemaphoreType.DMA((1,))],
        2 * rows * pixels * kinds * length,
        8 << 20,
        "insert",
    )
    send, gathered = lax.optimization_barrier((send, gathered))
    for offset in offsets[1:]:
        gathered = hop(gathered, offset)
    beyond, mine = call(
        keep_kernel,
        [(((wide - 1) * far, *place), bf16), ((far, *place), f32)],
        [vmem] * 3,
        (place_rows, parts, swap(send, 1)),
        [pltpu.SMEM((devices, blocks), i32), pltpu.SemaphoreType.DMA((1,))],
        0,
        0,
        "keep",
    )
    held, _ = lax.optimization_barrier((gathered, beyond))
    columns = [gathered] + [swap(held, x * cores) for x in range(1, wide)]
    columns += [swap(column, 1) for column in columns]
    for x in range(1, wide):
        mine = mine + swap(beyond[(x - 1) * far : x * far], x * cores).astype(f32)
    outgoing = mine.astype(bf16)
    _, *columns = lax.optimization_barrier((outgoing, *columns))
    if devices * kinds <= blocks * crossed:
        flat = pltpu.VMEM((kinds * devices * height, pixels), f32)
    else:
        flat = pltpu.VMEM((8, LANES), f32)
    (proj,) = call(
        functools.partial(project_kernel, shape),
        [((blocks, height, pixels), f32)],
        [vmem] * (2 + len(columns)),
        (route_rows, tiles_near, *columns),
        [pltpu.SMEM((crossed, blocks), i32), pltpu.VMEM((devices * height, length), bf16), flat, pltpu.SemaphoreType.DMA((1,))],
        0,
        0,
        "project",
    )

    (scores,) = call(
        score_kernel,
        [((1, count), f32)],
        [hbm] * 2 + [vmem] * 3,
        (batch_block, inv_sigma2, proj, wave, images_near),
        [block_scratch, noise_scratch, pltpu.VMEM((count * 8, LANES), f32), pltpu.SemaphoreType.DMA((2,))],
        0,
        0,
        "scores",
    )
    total = mine[0]
    for z in range(1, far):
        total = total + swap(outgoing[z], z * wide * cores).astype(f32)
    return scores.reshape(count), total[0:1], total[1:2]


def solution(mesh):
    placed = (
        P(("parts", "slab"), None, None),
        P(),
        P(("parts", "slab"), None),
        P(("parts", "slab"), None),
        P(("parts", "slab")),
        P(("parts", "slab"), None, None),
        P(("parts", "slab")),
        P("parts", None),
    )
    return jax.shard_map(
        on_device,
        mesh=mesh,
        in_specs=placed,
        out_specs=(
            P(("parts", "slab")),
            P(("parts", "slab"), None, None),
            P(("parts", "slab"), None, None),
        ),
        check_vma=False,
    )
```

```python
import functools

import jax
import jax.numpy as jnp
from jax import lax
from jax.experimental import pallas as pl
from jax.experimental.pallas import tpu as pltpu
from jax.sharding import PartitionSpec as P

LANES = 128
CHUNKS = 4
VMEM_BYTES = 24 * 1024 * 1024


def grid_of(devices):
    cores = 2 if devices % 2 == 0 else 1
    chips = devices // cores
    wide = 1
    while (2 * wide) ** 3 <= chips:
        wide *= 2
    return chips // wide, wide, cores


def powers(size):
    return [1 << n for n in range(size.bit_length() - 1)]


def sin_cos(angle):
    turns = jnp.floor(angle * 0.3183098861837907 + 0.5)
    rest = angle - turns * 3.140625
    rest = rest - turns * 9.675025939941406e-4
    rest = rest - turns * 1.5099580252808664e-7
    half = turns * 0.5
    sign = 1.0 - 4.0 * (half - jnp.floor(half))
    sq = rest * rest
    sin = rest * (1.0 + sq * (-1.0 / 6 + sq * (1.0 / 120 + sq * (-1.0 / 5040 + sq * (1.0 / 362880 + sq * (-1.0 / 39916800))))))
    cos = 1.0 + sq * (-0.5 + sq * (1.0 / 24 + sq * (-1.0 / 720 + sq * (1.0 / 40320 + sq * (-1.0 / 3628800 + sq * (1.0 / 479001600))))))
    return sign * sin, sign * cos


def tables(defocus_ref, height, pixels, line_ref, pixel_ref):
    images = defocus_ref.shape[1]
    defocus = defocus_ref[...]
    rows = lax.broadcasted_iota(jnp.int32, (height, images), 0)
    line = ((rows // 2 + 1).astype(jnp.float32) / (height // 2)) ** 2
    line_ref[0], line_ref[1] = sin_cos(defocus * line + 0.3)
    column = jnp.transpose(jnp.broadcast_to(defocus, (LANES, images)))
    part = 32
    lanes = lax.broadcasted_iota(jnp.int32, (part, LANES), 1)
    for n in range(images // part):
        rows = slice(n * part, (n + 1) * part)
        for m in range(pixels // LANES):
            pixel = ((lanes + (m * LANES + 1)).astype(jnp.float32) / pixels) ** 2
            at = slice(m * LANES, (m + 1) * LANES)
            pixel_ref[0, rows, at], pixel_ref[1, rows, at] = sin_cos(column[rows] * pixel)


def contrast_of(line_ref, pixel_ref, i):
    sin_line, cos_line = line_ref[0, :, i : i + 1], line_ref[1, :, i : i + 1]
    return sin_line * pixel_ref[1, i : i + 1, :] + cos_line * pixel_ref[0, i : i + 1, :]


def copies(pairs, sems):
    started = [pltpu.make_async_copy(source, target, sems.at[n]) for n, (source, target) in enumerate(pairs)]
    for copy in started:
        copy.start()
    return started


def row_tables(shape, kinds, height, slab, tile, place_ref, route_ref):
    far, wide, cores = shape
    devices, blocks = place_ref.shape
    rows, half = blocks * 2 * height, devices // 2
    me = lax.axis_index("slab")
    slot = lax.broadcasted_iota(jnp.int32, (devices, blocks), 0)
    block = lax.broadcasted_iota(jnp.int32, (devices, blocks), 1)
    within = slot & (half - 1)
    core = jnp.where(slot < half, cores - 1, 0)
    named = me ^ (((within & (far - 1)) * wide + within // far) * cores + core)
    place = jnp.full((devices, blocks), kinds * rows, jnp.int32)
    for r in range(slab.shape[0]):
        row = tile[r : r + 1, :] * rows + block * (2 * height)
        place = jnp.where(slab[r : r + 1, :] == named, row, place)
    place_ref[...] = place
    route_ref[...] = (tile * devices + (me ^ slab)) * height


def sum_kernel(shape, kinds, slab_hbm, tile_hbm, block_hbm, defocus_hbm, noise_hbm, tiles_hbm, images_hbm,
               sums_ref, wave_ref, tiles_ref, images_ref, place_ref, route_ref,
               slab_ref, tile_ref, block_ref, defocus_ref, noise_ref, line_ref, pixel_ref, acc_ref, sems):
    count = images_ref.shape[0]
    part = count // CHUNKS
    small = [(defocus_hbm, defocus_ref), (block_hbm, block_ref), (noise_hbm, noise_ref), (slab_hbm, slab_ref), (tile_hbm, tile_ref)]
    large = [(images_hbm.at[pl.ds(n * part, part)], images_ref.at[pl.ds(n * part, part)]) for n in range(CHUNKS)]
    started = copies(small + large, sems)
    last = pltpu.make_async_copy(tiles_hbm, tiles_ref, sems.at[len(started)])
    height, pixels = noise_ref.shape
    batches = block_ref.shape[0]
    size = count // batches
    acc_ref[...] = jnp.zeros_like(acc_ref)
    for copy in started[: len(small)]:
        copy.wait()
    tables(defocus_ref, height, pixels, line_ref, pixel_ref)
    row_tables(shape, kinds, height, slab_ref[...], tile_ref[...], place_ref, route_ref)
    for b in range(batches):
        if b % (batches // CHUNKS) == 0:
            started[len(small) + b // (batches // CHUNKS)].wait()
        if b == 0:
            last.start()
        data = jnp.zeros((height, pixels), jnp.float32)
        weight = jnp.zeros((height, pixels), jnp.float32)
        for j in range(size):
            i = b * size + j
            wave = contrast_of(line_ref, pixel_ref, i)
            wave_ref[i] = wave
            data = data + wave * images_ref[i].astype(jnp.float32)
            weight = weight + wave * wave
        k = block_ref[b]
        acc_ref[k, 0] = acc_ref[k, 0] + data
        acc_ref[k, 1] = acc_ref[k, 1] + weight
    sums = (acc_ref[...] * noise_ref[...][None, None]).astype(jnp.bfloat16)
    sums_ref[...] = sums.reshape(sums_ref.shape)
    last.wait()


def fill(ref, start, place_ref, parts_ref, mate_ref=None, offset=0):
    sides, height, length = ref.shape[1:]

    def step(slot, carry):
        acc = None
        for k in range(place_ref.shape[1]):
            at = pl.multiple_of(place_ref[start + slot, k], sides * height)
            part = parts_ref[pl.ds(at, sides * height), :]
            acc = part if acc is None else acc + part
        acc = acc.reshape(sides, height, length)
        if mate_ref is not None:
            acc = acc + mate_ref[offset + slot].astype(jnp.float32)
        ref[slot] = acc.astype(ref.dtype)
        return carry

    lax.fori_loop(0, ref.shape[0], step, 0)


def insert_kernel(place_vmem, sums_ref, tiles_ref, send_ref, parts_ref, place_ref, sems):
    (started,) = copies([(place_vmem, place_ref)], sems)
    kinds = tiles_ref.shape[0]
    rows = sums_ref.shape[0]
    zeros = parts_ref.shape[0] - kinds * rows
    parts_ref[kinds * rows :, :] = jnp.zeros((zeros, parts_ref.shape[1]), jnp.float32)
    for t in range(kinds):
        parts_ref[t * rows : (t + 1) * rows, :] = lax.dot_general(
            sums_ref[...], tiles_ref[t], (((1,), (1,)), ((), ())), preferred_element_type=jnp.float32
        )
    started.wait()
    fill(send_ref, 0, place_ref, parts_ref)


def keep_kernel(place_vmem, parts_ref, mate_ref, far_ref, near_ref, place_ref, sems):
    (started,) = copies([(place_vmem, place_ref)], sems)
    half, far = place_ref.shape[0] // 2, near_ref.shape[0]
    started.wait()
    fill(far_ref, half + far, place_ref, parts_ref, mate_ref, far)
    fill(near_ref, half, place_ref, parts_ref, mate_ref, 0)


def project_kernel(places, route_vmem, tiles_ref, *refs):
    columns, refs = refs[: len(places)], refs[len(places) :]
    proj_ref, route_ref, lines_ref, flat_ref, sems = refs
    (started,) = copies([(route_vmem, route_ref)], sems)
    crossed, blocks = route_ref.shape
    kinds = tiles_ref.shape[0]
    height = columns[0].shape[1]
    rows = lines_ref.shape[0]
    dense = rows // height * kinds <= crossed * blocks
    for ref, aways in zip(columns, places):
        for n, away in enumerate(aways):
            lines_ref[away * height : (away + 1) * height, :] = ref[n]
    if dense:
        for t in range(kinds):
            flat_ref[t * rows : (t + 1) * rows, :] = jnp.dot(lines_ref[...], tiles_ref[t], preferred_element_type=jnp.float32)
    started.wait()

    def project(k, carry):
        acc = None
        for r in range(crossed):
            at = route_ref[r, k]
            if dense:
                part = flat_ref[pl.ds(pl.multiple_of(at, height), height), :]
            else:
                t, at = at // rows, pl.multiple_of(lax.rem(at, rows), height)
                part = jnp.dot(lines_ref[pl.ds(at, height), :], tiles_ref[t], preferred_element_type=jnp.float32)
            acc = part if acc is None else acc + part
        proj_ref[k] = acc
        return carry

    lax.fori_loop(0, blocks, project, 0, unroll=dense)


def score_kernel(block_hbm, noise_hbm, proj_ref, wave_ref, images_ref, score_ref, block_ref, noise_ref, part_ref, sems):
    started = copies([(block_hbm, block_ref), (noise_hbm, noise_ref)], sems)
    height, pixels = noise_ref.shape
    batches = block_ref.shape[0]
    count = images_ref.shape[0]
    size = count // batches
    for copy in started:
        copy.wait()
    noise = noise_ref[...]
    for b in range(batches):
        proj = proj_ref[block_ref[b]]
        for j in range(size):
            i = b * size + j
            residual = images_ref[i].astype(jnp.float32) - wave_ref[i] * proj
            power = residual * residual * noise
            power = sum(power[n * 8 : (n + 1) * 8] for n in range(height // 8))
            part_ref[i * 8 : (i + 1) * 8, :] = sum(power[:, n * LANES : (n + 1) * LANES] for n in range(pixels // LANES))
    total = sum(part_ref[pl.ds(n, count, 8), :] for n in range(8))
    total = jnp.sum(jnp.transpose(total), axis=0, keepdims=True)
    score_ref[...] = total * (1.0 / (height * pixels))


def on_device(volume, tiles, slab_ids, tile_ids, batch_block, images, defocus, inv_sigma2):
    blocks, crossed = slab_ids.shape
    height, length = volume.shape[1:]
    count, _, pixels = images.shape
    kinds = tiles.shape[0]
    devices = lax.axis_size("slab")
    shape = far, wide, cores = grid_of(devices)
    half = devices // 2
    rows = blocks * 2 * height
    slabs, kind_rows, row = slab_ids.T, tile_ids.T, defocus.reshape(1, count)

    def swap(array, offset):
        return lax.ppermute(array, "slab", [(i, i ^ offset) for i in range(devices)])

    vmem = pl.BlockSpec(memory_space=pltpu.VMEM)
    hbm = pl.BlockSpec(memory_space=pltpu.HBM)
    params = pltpu.CompilerParams(vmem_limit_bytes=VMEM_BYTES)
    f32, bf16 = jnp.float32, jnp.bfloat16
    i32 = jnp.int32
    block_scratch = pltpu.SMEM(batch_block.shape, jnp.int32)
    noise_scratch = pltpu.VMEM((height, pixels), f32)

    def call(kernel, outs, inputs, operands, scratch, flops, moved, name):
        operands = [
            pltpu.with_memory_space_constraint(x, pltpu.HBM) if spec is hbm else x for x, spec in zip(operands, inputs)
        ]
        return pl.pallas_call(
            kernel,
            out_shape=tuple(jax.ShapeDtypeStruct(s, t) for s, t in outs),
            in_specs=inputs,
            out_specs=(vmem,) * len(outs),
            scratch_shapes=scratch,
            compiler_params=params,
            cost_estimate=pl.CostEstimate(flops=flops, bytes_accessed=moved, transcendentals=0),
            name=name,
        )(*operands)

    def hop(array, offset):
        return jnp.concatenate([array, swap(array, offset)], axis=0)

    along_z = [z * wide * cores for z in reversed(powers(far))]
    offsets = along_z[:1] + [x * cores for x in powers(wide)] + along_z[1:]
    away = [0]
    for offset in offsets[:-1]:
        away += [a ^ offset for a in away]
    gathered = hop(volume, offsets[0])

    sums, wave, tiles_near, images_near, place_rows, route_rows = call(
        functools.partial(sum_kernel, shape, kinds),
        [
            ((rows, pixels), bf16),
            (images.shape, f32),
            (tiles.shape, bf16),
            (images.shape, bf16),
            ((devices, blocks), i32),
            ((crossed, blocks), i32),
        ],
        [hbm] * 7,
        (slabs, kind_rows, batch_block, row, inv_sigma2, tiles, images),
        [
            pltpu.VMEM((crossed, blocks), i32),
            pltpu.VMEM((crossed, blocks), i32),
            block_scratch,
            pltpu.VMEM((1, count), f32),
            noise_scratch,
            pltpu.VMEM((2, height, count), f32),
            pltpu.VMEM((2, count, pixels), f32),
            pltpu.VMEM((blocks, 2, height, pixels), f32),
            pltpu.SemaphoreType.DMA((CHUNKS + 6,)),
        ],
        0,
        10 << 20,
        "sums",
    )

    place = (2, height, length)
    send, parts = call(
        insert_kernel,
        [((half, *place), bf16), ((kinds * rows + 2 * height, length), f32)],
        [vmem] * 3,
        (place_rows, sums, tiles_near),
        [pltpu.SMEM((devices, blocks), i32), pltpu.SemaphoreType.DMA((1,))],
        2 * rows * pixels * kinds * length,
        8 << 20,
        "insert",
    )
    send, gathered = lax.optimization_barrier((send, gathered))
    for offset in offsets[1:-1]:
        gathered = hop(gathered, offset)
    beyond, mine = call(
        keep_kernel,
        [(((wide - 1) * far, *place), bf16), ((far, *place), f32)],
        [vmem] * 3,
        (place_rows, parts, swap(send, 1)),
        [pltpu.SMEM((devices, blocks), i32), pltpu.SemaphoreType.DMA((1,))],
        0,
        0,
        "keep",
    )
    held, _ = lax.optimization_barrier((gathered, beyond))
    columns = [gathered, swap(held, offsets[-1])]
    columns += [swap(column, 1) for column in columns]
    places = [[a ^ last for a in away] for last in (0, offsets[-1], 1, offsets[-1] ^ 1)]
    for x in range(1, wide):
        mine = mine + swap(beyond[(x - 1) * far : x * far], x * cores).astype(f32)
    outgoing = mine.astype(bf16)
    _, *columns = lax.optimization_barrier((outgoing, *columns))
    if devices * kinds <= blocks * crossed:
        flat = pltpu.VMEM((kinds * devices * height, pixels), f32)
    else:
        flat = pltpu.VMEM((8, LANES), f32)
    (proj,) = call(
        functools.partial(project_kernel, places),
        [((blocks, height, pixels), f32)],
        [vmem] * (2 + len(columns)),
        (route_rows, tiles_near, *columns),
        [pltpu.SMEM((crossed, blocks), i32), pltpu.VMEM((devices * height, length), bf16), flat, pltpu.SemaphoreType.DMA((1,))],
        0,
        0,
        "project",
    )

    (scores,) = call(
        score_kernel,
        [((1, count), f32)],
        [hbm] * 2 + [vmem] * 3,
        (batch_block, inv_sigma2, proj, wave, images_near),
        [block_scratch, noise_scratch, pltpu.VMEM((count * 8, LANES), f32), pltpu.SemaphoreType.DMA((2,))],
        0,
        0,
        "scores",
    )
    total = mine[0]
    for z in range(1, far):
        total = total + swap(outgoing[z], z * wide * cores).astype(f32)
    return scores.reshape(count), total[0:1], total[1:2]


def solution(mesh):
    placed = (
        P(("parts", "slab"), None, None),
        P(),
        P(("parts", "slab"), None),
        P(("parts", "slab"), None),
        P(("parts", "slab")),
        P(("parts", "slab"), None, None),
        P(("parts", "slab")),
        P("parts", None),
    )
    return jax.shard_map(
        on_device,
        mesh=mesh,
        in_specs=placed,
        out_specs=(
            P(("parts", "slab")),
            P(("parts", "slab"), None, None),
            P(("parts", "slab"), None, None),
        ),
        check_vma=False,
    )
```

```python
import functools

import jax
import jax.numpy as jnp
from jax import lax
from jax.experimental import pallas as pl
from jax.experimental.pallas import tpu as pltpu
from jax.sharding import PartitionSpec as P

LANES = 128
CHUNKS = 4
VMEM_BYTES = 24 * 1024 * 1024


def grid_of(devices):
    cores = 2 if devices % 2 == 0 else 1
    chips = devices // cores
    wide = 1
    while (2 * wide) ** 3 <= chips:
        wide *= 2
    return chips // wide, wide, cores


def powers(size):
    return [1 << n for n in range(size.bit_length() - 1)]


def sin_cos(angle):
    turns = jnp.floor(angle * 0.3183098861837907 + 0.5)
    rest = angle - turns * 3.140625
    rest = rest - turns * 9.675025939941406e-4
    rest = rest - turns * 1.5099580252808664e-7
    half = turns * 0.5
    sign = 1.0 - 4.0 * (half - jnp.floor(half))
    sq = rest * rest
    sin = rest * (1.0 + sq * (-1.0 / 6 + sq * (1.0 / 120 + sq * (-1.0 / 5040 + sq * (1.0 / 362880 + sq * (-1.0 / 39916800))))))
    cos = 1.0 + sq * (-0.5 + sq * (1.0 / 24 + sq * (-1.0 / 720 + sq * (1.0 / 40320 + sq * (-1.0 / 3628800 + sq * (1.0 / 479001600))))))
    return sign * sin, sign * cos


def tables(defocus_ref, height, pixels, line_ref, pixel_ref):
    images = defocus_ref.shape[1]
    defocus = defocus_ref[...]
    rows = lax.broadcasted_iota(jnp.int32, (height, images), 0)
    line = ((rows // 2 + 1).astype(jnp.float32) / (height // 2)) ** 2
    line_ref[0], line_ref[1] = sin_cos(defocus * line + 0.3)
    column = jnp.transpose(jnp.broadcast_to(defocus, (LANES, images)))
    part = 32
    lanes = lax.broadcasted_iota(jnp.int32, (part, LANES), 1)
    for n in range(images // part):
        rows = slice(n * part, (n + 1) * part)
        for m in range(pixels // LANES):
            pixel = ((lanes + (m * LANES + 1)).astype(jnp.float32) / pixels) ** 2
            at = slice(m * LANES, (m + 1) * LANES)
            pixel_ref[0, rows, at], pixel_ref[1, rows, at] = sin_cos(column[rows] * pixel)


def contrast_of(line_ref, pixel_ref, i):
    sin_line, cos_line = line_ref[0, :, i : i + 1], line_ref[1, :, i : i + 1]
    return sin_line * pixel_ref[1, i : i + 1, :] + cos_line * pixel_ref[0, i : i + 1, :]


def copies(pairs, sems):
    started = [pltpu.make_async_copy(source, target, sems.at[n]) for n, (source, target) in enumerate(pairs)]
    for copy in started:
        copy.start()
    return started


def row_tables(shape, kinds, height, slab, tile, place_ref, route_ref):
    far, wide, cores = shape
    devices, blocks = place_ref.shape
    rows, half = blocks * 2 * height, devices // 2
    me = lax.axis_index("slab")
    slot = lax.broadcasted_iota(jnp.int32, (devices, blocks), 0)
    block = lax.broadcasted_iota(jnp.int32, (devices, blocks), 1)
    within = slot & (half - 1)
    core = jnp.where(slot < half, cores - 1, 0)
    named = me ^ (((within & (far - 1)) * wide + within // far) * cores + core)
    place = jnp.full((devices, blocks), kinds * rows, jnp.int32)
    for r in range(slab.shape[0]):
        row = tile[r : r + 1, :] * rows + block * (2 * height)
        place = jnp.where(slab[r : r + 1, :] == named, row, place)
    place_ref[...] = place
    route_ref[...] = (tile * devices + (me ^ slab)) * height


def sum_kernel(shape, kinds, slab_hbm, tile_hbm, block_hbm, defocus_hbm, noise_hbm, tiles_hbm, images_hbm,
               sums_ref, wave_ref, tiles_ref, images_ref, place_ref, route_ref,
               slab_ref, tile_ref, block_ref, defocus_ref, noise_ref, line_ref, pixel_ref, acc_ref, sems):
    count = images_ref.shape[0]
    part = count // CHUNKS
    small = [(defocus_hbm, defocus_ref), (block_hbm, block_ref), (noise_hbm, noise_ref), (slab_hbm, slab_ref), (tile_hbm, tile_ref)]
    large = [(images_hbm.at[pl.ds(n * part, part)], images_ref.at[pl.ds(n * part, part)]) for n in range(CHUNKS)]
    started = copies(small + large, sems)
    last = pltpu.make_async_copy(tiles_hbm, tiles_ref, sems.at[len(started)])
    height, pixels = noise_ref.shape
    batches = block_ref.shape[0]
    size = count // batches
    acc_ref[...] = jnp.zeros_like(acc_ref)
    for copy in started[: len(small)]:
        copy.wait()
    tables(defocus_ref, height, pixels, line_ref, pixel_ref)
    row_tables(shape, kinds, height, slab_ref[...], tile_ref[...], place_ref, route_ref)
    for b in range(batches):
        if b % (batches // CHUNKS) == 0:
            started[len(small) + b // (batches // CHUNKS)].wait()
        if b == 0:
            last.start()
        data = jnp.zeros((height, pixels), jnp.float32)
        weight = jnp.zeros((height, pixels), jnp.float32)
        for j in range(size):
            i = b * size + j
            wave = contrast_of(line_ref, pixel_ref, i)
            wave_ref[i] = wave
            data = data + wave * images_ref[i].astype(jnp.float32)
            weight = weight + wave * wave
        k = block_ref[b]
        acc_ref[k, 0] = acc_ref[k, 0] + data
        acc_ref[k, 1] = acc_ref[k, 1] + weight
    sums = (acc_ref[...] * noise_ref[...][None, None]).astype(jnp.bfloat16)
    sums_ref[...] = sums.reshape(sums_ref.shape)
    last.wait()


def fill(ref, start, place_ref, parts_ref, mate_ref=None, offset=0):
    sides, height, length = ref.shape[1:]

    def step(slot, carry):
        acc = None
        for k in range(place_ref.shape[1]):
            at = pl.multiple_of(place_ref[start + slot, k], sides * height)
            part = parts_ref[pl.ds(at, sides * height), :]
            acc = part if acc is None else acc + part
        acc = acc.reshape(sides, height, length)
        if mate_ref is not None:
            acc = acc + mate_ref[offset + slot].astype(jnp.float32)
        ref[slot] = acc.astype(ref.dtype)
        return carry

    lax.fori_loop(0, ref.shape[0], step, 0)


def insert_kernel(place_vmem, sums_ref, tiles_ref, send_ref, parts_ref, place_ref, sems):
    (started,) = copies([(place_vmem, place_ref)], sems)
    kinds = tiles_ref.shape[0]
    rows = sums_ref.shape[0]
    zeros = parts_ref.shape[0] - kinds * rows
    parts_ref[kinds * rows :, :] = jnp.zeros((zeros, parts_ref.shape[1]), jnp.float32)
    for t in range(kinds):
        parts_ref[t * rows : (t + 1) * rows, :] = lax.dot_general(
            sums_ref[...], tiles_ref[t], (((1,), (1,)), ((), ())), preferred_element_type=jnp.float32
        )
    started.wait()
    fill(send_ref, 0, place_ref, parts_ref)


def far_kernel(place_vmem, parts_ref, mate_ref, main_ref, own_ref, place_ref, sems):
    (started,) = copies([(place_vmem, place_ref)], sems)
    half, far = place_ref.shape[0] // 2, main_ref.shape[1] + 1
    started.wait()
    for n in range(main_ref.shape[0]):
        slot = (n + 1) * far
        fill(main_ref.at[n], half + slot + 1, place_ref, parts_ref, mate_ref, slot + 1)
    for n in range(main_ref.shape[0]):
        slot = (n + 1) * far
        fill(own_ref.at[pl.ds(n, 1)], half + slot, place_ref, parts_ref, mate_ref, slot)


def near_kernel(place_vmem, parts_ref, mate_ref, near_ref, place_ref, sems):
    (started,) = copies([(place_vmem, place_ref)], sems)
    started.wait()
    fill(near_ref, place_ref.shape[0] // 2, place_ref, parts_ref, mate_ref)


def project_kernel(places, route_vmem, tiles_ref, *refs):
    columns, refs = refs[: len(places)], refs[len(places) :]
    proj_ref, route_ref, lines_ref, flat_ref, sems = refs
    (started,) = copies([(route_vmem, route_ref)], sems)
    crossed, blocks = route_ref.shape
    kinds = tiles_ref.shape[0]
    height = columns[0].shape[1]
    rows = lines_ref.shape[0]
    dense = rows // height * kinds <= crossed * blocks
    for ref, aways in zip(columns, places):
        for n, away in enumerate(aways):
            lines_ref[away * height : (away + 1) * height, :] = ref[n]
    if dense:
        for t in range(kinds):
            flat_ref[t * rows : (t + 1) * rows, :] = jnp.dot(lines_ref[...], tiles_ref[t], preferred_element_type=jnp.float32)
    started.wait()

    def project(k, carry):
        acc = None
        for r in range(crossed):
            at = route_ref[r, k]
            if dense:
                part = flat_ref[pl.ds(pl.multiple_of(at, height), height), :]
            else:
                t, at = at // rows, pl.multiple_of(lax.rem(at, rows), height)
                part = jnp.dot(lines_ref[pl.ds(at, height), :], tiles_ref[t], preferred_element_type=jnp.float32)
            acc = part if acc is None else acc + part
        proj_ref[k] = acc
        return carry

    lax.fori_loop(0, blocks, project, 0, unroll=dense)


def score_kernel(block_hbm, noise_hbm, proj_ref, wave_ref, images_ref, score_ref, block_ref, noise_ref, part_ref, sems):
    started = copies([(block_hbm, block_ref), (noise_hbm, noise_ref)], sems)
    height, pixels = noise_ref.shape
    batches = block_ref.shape[0]
    count = images_ref.shape[0]
    size = count // batches
    for copy in started:
        copy.wait()
    noise = noise_ref[...]
    for b in range(batches):
        proj = proj_ref[block_ref[b]]
        for j in range(size):
            i = b * size + j
            residual = images_ref[i].astype(jnp.float32) - wave_ref[i] * proj
            power = residual * residual * noise
            power = sum(power[n * 8 : (n + 1) * 8] for n in range(height // 8))
            part_ref[i * 8 : (i + 1) * 8, :] = sum(power[:, n * LANES : (n + 1) * LANES] for n in range(pixels // LANES))
    total = sum(part_ref[pl.ds(n, count, 8), :] for n in range(8))
    total = jnp.sum(jnp.transpose(total), axis=0, keepdims=True)
    score_ref[...] = total * (1.0 / (height * pixels))


def on_device(volume, tiles, slab_ids, tile_ids, batch_block, images, defocus, inv_sigma2):
    blocks, crossed = slab_ids.shape
    height, length = volume.shape[1:]
    count, _, pixels = images.shape
    kinds = tiles.shape[0]
    devices = lax.axis_size("slab")
    shape = far, wide, cores = grid_of(devices)
    half = devices // 2
    rows = blocks * 2 * height
    slabs, kind_rows, row = slab_ids.T, tile_ids.T, defocus.reshape(1, count)

    def swap(array, offset):
        return lax.ppermute(array, "slab", [(i, i ^ offset) for i in range(devices)])

    vmem = pl.BlockSpec(memory_space=pltpu.VMEM)
    hbm = pl.BlockSpec(memory_space=pltpu.HBM)
    params = pltpu.CompilerParams(vmem_limit_bytes=VMEM_BYTES)
    f32, bf16 = jnp.float32, jnp.bfloat16
    i32 = jnp.int32
    block_scratch = pltpu.SMEM(batch_block.shape, jnp.int32)
    noise_scratch = pltpu.VMEM((height, pixels), f32)

    def call(kernel, outs, inputs, operands, scratch, flops, moved, name):
        operands = [
            pltpu.with_memory_space_constraint(x, pltpu.HBM) if spec is hbm else x for x, spec in zip(operands, inputs)
        ]
        return pl.pallas_call(
            kernel,
            out_shape=tuple(jax.ShapeDtypeStruct(s, t) for s, t in outs),
            in_specs=inputs,
            out_specs=(vmem,) * len(outs),
            scratch_shapes=scratch,
            compiler_params=params,
            cost_estimate=pl.CostEstimate(flops=flops, bytes_accessed=moved, transcendentals=0),
            name=name,
        )(*operands)

    def hop(array, offset):
        return jnp.concatenate([array, swap(array, offset)], axis=0)

    along_z = [z * wide * cores for z in reversed(powers(far))]
    offsets = along_z[:1] + [x * cores for x in powers(wide)] + along_z[1:]
    away = [0]
    for offset in offsets[:-1]:
        away += [a ^ offset for a in away]
    gathered = hop(volume, offsets[0])

    sums, wave, tiles_near, images_near, place_rows, route_rows = call(
        functools.partial(sum_kernel, shape, kinds),
        [
            ((rows, pixels), bf16),
            (images.shape, f32),
            (tiles.shape, bf16),
            (images.shape, bf16),
            ((devices, blocks), i32),
            ((crossed, blocks), i32),
        ],
        [hbm] * 7,
        (slabs, kind_rows, batch_block, row, inv_sigma2, tiles, images),
        [
            pltpu.VMEM((crossed, blocks), i32),
            pltpu.VMEM((crossed, blocks), i32),
            block_scratch,
            pltpu.VMEM((1, count), f32),
            noise_scratch,
            pltpu.VMEM((2, height, count), f32),
            pltpu.VMEM((2, count, pixels), f32),
            pltpu.VMEM((blocks, 2, height, pixels), f32),
            pltpu.SemaphoreType.DMA((CHUNKS + 6,)),
        ],
        0,
        10 << 20,
        "sums",
    )

    place = (2, height, length)
    send, parts = call(
        insert_kernel,
        [((half, *place), bf16), ((kinds * rows + 2 * height, length), f32)],
        [vmem] * 3,
        (place_rows, sums, tiles_near),
        [pltpu.SMEM((devices, blocks), i32), pltpu.SemaphoreType.DMA((1,))],
        2 * rows * pixels * kinds * length,
        8 << 20,
        "insert",
    )
    send, gathered = lax.optimization_barrier((send, gathered))
    for offset in offsets[1:-1]:
        gathered = hop(gathered, offset)
    mate = swap(send, 1)
    place_scratch = [pltpu.SMEM((devices, blocks), i32), pltpu.SemaphoreType.DMA((1,))]
    main, own = call(
        far_kernel,
        [((wide - 1, far - 1, *place), bf16), ((wide - 1, *place), bf16)],
        [vmem] * 3,
        (place_rows, parts, mate),
        place_scratch,
        0,
        0,
        "far",
    )
    (near,) = call(
        near_kernel, [((far, *place), f32)], [vmem] * 3, (place_rows, parts, mate), place_scratch, 0, 0, "near"
    )
    held, _ = lax.optimization_barrier((gathered, main))
    columns = [gathered, swap(held, offsets[-1])]
    columns += [swap(column, 1) for column in columns]
    places = [[a ^ last for a in away] for last in (0, offsets[-1], 1, offsets[-1] ^ 1)]
    mine = near[1:]
    for x in range(1, wide):
        mine = mine + swap(main[x - 1], x * cores).astype(f32)
    total = near[0]
    for x in range(1, wide):
        total = total + swap(own[x - 1], x * cores).astype(f32)
    outgoing = mine.astype(bf16)
    _, *columns = lax.optimization_barrier((outgoing, *columns))
    if devices * kinds <= blocks * crossed:
        flat = pltpu.VMEM((kinds * devices * height, pixels), f32)
    else:
        flat = pltpu.VMEM((8, LANES), f32)
    (proj,) = call(
        functools.partial(project_kernel, places),
        [((blocks, height, pixels), f32)],
        [vmem] * (2 + len(columns)),
        (route_rows, tiles_near, *columns),
        [pltpu.SMEM((crossed, blocks), i32), pltpu.VMEM((devices * height, length), bf16), flat, pltpu.SemaphoreType.DMA((1,))],
        0,
        0,
        "project",
    )

    (scores,) = call(
        score_kernel,
        [((1, count), f32)],
        [hbm] * 2 + [vmem] * 3,
        (batch_block, inv_sigma2, proj, wave, images_near),
        [block_scratch, noise_scratch, pltpu.VMEM((count * 8, LANES), f32), pltpu.SemaphoreType.DMA((2,))],
        0,
        0,
        "scores",
    )
    for z in range(1, far):
        came = swap(outgoing[z - 1], z * wide * cores)
        if z == far - 1:
            came, scores = lax.optimization_barrier((came, scores))
        total = total + came.astype(f32)
    return scores.reshape(count), total[0:1], total[1:2]


def solution(mesh):
    placed = (
        P(("parts", "slab"), None, None),
        P(),
        P(("parts", "slab"), None),
        P(("parts", "slab"), None),
        P(("parts", "slab")),
        P(("parts", "slab"), None, None),
        P(("parts", "slab")),
        P("parts", None),
    )
    return jax.shard_map(
        on_device,
        mesh=mesh,
        in_specs=placed,
        out_specs=(
            P(("parts", "slab")),
            P(("parts", "slab"), None, None),
            P(("parts", "slab"), None, None),
        ),
        check_vma=False,
    )
```

```python
import functools

import jax
import jax.numpy as jnp
from jax import lax
from jax.experimental import pallas as pl
from jax.experimental.pallas import tpu as pltpu
from jax.sharding import PartitionSpec as P

LANES = 128
CHUNKS = 4
VMEM_BYTES = 24 * 1024 * 1024


def grid_of(devices):
    cores = 2 if devices % 2 == 0 else 1
    chips = devices // cores
    wide = 1
    while (2 * wide) ** 3 <= chips:
        wide *= 2
    return chips // wide, wide, cores


def powers(size):
    return [1 << n for n in range(size.bit_length() - 1)]


def sin_cos(angle):
    turns = jnp.floor(angle * 0.3183098861837907 + 0.5)
    rest = angle - turns * 3.140625
    rest = rest - turns * 9.675025939941406e-4
    rest = rest - turns * 1.5099580252808664e-7
    half = turns * 0.5
    sign = 1.0 - 4.0 * (half - jnp.floor(half))
    sq = rest * rest
    sin = rest * (1.0 + sq * (-1.0 / 6 + sq * (1.0 / 120 + sq * (-1.0 / 5040 + sq * (1.0 / 362880 + sq * (-1.0 / 39916800))))))
    cos = 1.0 + sq * (-0.5 + sq * (1.0 / 24 + sq * (-1.0 / 720 + sq * (1.0 / 40320 + sq * (-1.0 / 3628800 + sq * (1.0 / 479001600))))))
    return sign * sin, sign * cos


def tables(defocus_ref, height, pixels, line_ref, pixel_ref):
    images = defocus_ref.shape[1]
    defocus = defocus_ref[...]
    rows = lax.broadcasted_iota(jnp.int32, (height, images), 0)
    line = ((rows // 2 + 1).astype(jnp.float32) / (height // 2)) ** 2
    line_ref[0], line_ref[1] = sin_cos(defocus * line + 0.3)
    column = jnp.transpose(jnp.broadcast_to(defocus, (LANES, images)))
    part = 32
    lanes = lax.broadcasted_iota(jnp.int32, (part, LANES), 1)
    for n in range(images // part):
        rows = slice(n * part, (n + 1) * part)
        for m in range(pixels // LANES):
            pixel = ((lanes + (m * LANES + 1)).astype(jnp.float32) / pixels) ** 2
            at = slice(m * LANES, (m + 1) * LANES)
            pixel_ref[0, rows, at], pixel_ref[1, rows, at] = sin_cos(column[rows] * pixel)


def contrast_of(line_ref, pixel_ref, i):
    sin_line, cos_line = line_ref[0, :, i : i + 1], line_ref[1, :, i : i + 1]
    return sin_line * pixel_ref[1, i : i + 1, :] + cos_line * pixel_ref[0, i : i + 1, :]


def copies(pairs, sems):
    started = [pltpu.make_async_copy(source, target, sems.at[n]) for n, (source, target) in enumerate(pairs)]
    for copy in started:
        copy.start()
    return started


def row_tables(shape, kinds, height, slab, tile, owner, place_ref, route_ref):
    far, wide, cores = shape
    devices, blocks = place_ref.shape
    rows, half = blocks * 2 * height, devices // 2
    me = lax.axis_index("slab")
    slot = lax.broadcasted_iota(jnp.int32, (devices, blocks), 0)
    block = lax.broadcasted_iota(jnp.int32, (devices, blocks), 1)
    within = slot & (half - 1)
    core = jnp.where(slot < half, cores - 1, 0)
    named = me ^ (((within & (far - 1)) * wide + within // far) * cores + core)
    place = jnp.full((devices, blocks), kinds * rows, jnp.int32)
    for r in range(slab.shape[0]):
        row = tile[r : r + 1, :] * rows + block * (2 * height)
        place = jnp.where(slab[r : r + 1, :] == named, row, place)
    place_ref[...] = place
    row = (tile * devices + (me ^ slab)) * height
    route = jnp.zeros(route_ref.shape, jnp.int32)
    for k in range(blocks):
        route = jnp.where(owner == k, row[:, k : k + 1], route)
    route_ref[...] = route


def sum_kernel(shape, kinds, slab_hbm, tile_hbm, block_hbm, owner_hbm, defocus_hbm, noise_hbm, tiles_hbm, images_hbm,
               sums_ref, wave_ref, tiles_ref, images_ref, noise_ref, place_ref, route_ref,
               slab_ref, tile_ref, block_ref, owner_ref, defocus_ref, line_ref, pixel_ref, acc_ref, sems):
    count = images_ref.shape[0]
    part = count // CHUNKS
    small = [(defocus_hbm, defocus_ref), (block_hbm, block_ref), (noise_hbm, noise_ref)]
    small += [(slab_hbm, slab_ref), (tile_hbm, tile_ref), (owner_hbm, owner_ref)]
    large = [(images_hbm.at[pl.ds(n * part, part)], images_ref.at[pl.ds(n * part, part)]) for n in range(CHUNKS)]
    started = copies(small + large, sems)
    last = pltpu.make_async_copy(tiles_hbm, tiles_ref, sems.at[len(started)])
    height, pixels = noise_ref.shape
    batches = block_ref.shape[0]
    size = count // batches
    acc_ref[...] = jnp.zeros_like(acc_ref)
    for copy in started[: len(small)]:
        copy.wait()
    tables(defocus_ref, height, pixels, line_ref, pixel_ref)
    row_tables(shape, kinds, height, slab_ref[...], tile_ref[...], owner_ref[...], place_ref, route_ref)
    for b in range(batches):
        if b % (batches // CHUNKS) == 0:
            started[len(small) + b // (batches // CHUNKS)].wait()
        if b == 0:
            last.start()
        data = jnp.zeros((height, pixels), jnp.float32)
        weight = jnp.zeros((height, pixels), jnp.float32)
        for j in range(size):
            i = b * size + j
            wave = contrast_of(line_ref, pixel_ref, i)
            wave_ref[i] = wave
            data = data + wave * images_ref[i].astype(jnp.float32)
            weight = weight + wave * wave
        k = block_ref[b]
        acc_ref[k, 0] = acc_ref[k, 0] + data
        acc_ref[k, 1] = acc_ref[k, 1] + weight
    sums = (acc_ref[...] * noise_ref[...][None, None]).astype(jnp.bfloat16)
    sums_ref[...] = sums.reshape(sums_ref.shape)
    last.wait()


def fill(ref, start, place_ref, parts_ref, mate_ref=None):
    sides, height, length = ref.shape[1:]

    def step(slot, carry):
        acc = None
        for k in range(place_ref.shape[1]):
            at = pl.multiple_of(place_ref[start + slot, k], sides * height)
            part = parts_ref[pl.ds(at, sides * height), :]
            acc = part if acc is None else acc + part
        acc = acc.reshape(sides, height, length)
        if mate_ref is not None:
            acc = acc + mate_ref[slot].astype(jnp.float32)
        ref[slot] = acc.astype(ref.dtype)
        return carry

    lax.fori_loop(0, ref.shape[0], step, 0)


def insert_kernel(place_vmem, sums_ref, tiles_ref, send_ref, far_ref, parts_ref, place_ref, sems):
    (started,) = copies([(place_vmem, place_ref)], sems)
    kinds = tiles_ref.shape[0]
    rows = sums_ref.shape[0]
    zeros = parts_ref.shape[0] - kinds * rows
    parts_ref[kinds * rows :, :] = jnp.zeros((zeros, parts_ref.shape[1]), jnp.float32)
    for t in range(kinds):
        parts_ref[t * rows : (t + 1) * rows, :] = lax.dot_general(
            sums_ref[...], tiles_ref[t], (((1,), (1,)), ((), ())), preferred_element_type=jnp.float32
        )
    started.wait()
    fill(send_ref, 0, place_ref, parts_ref)
    devices = place_ref.shape[0]
    fill(far_ref, devices - far_ref.shape[0], place_ref, parts_ref)


def near_kernel(place_vmem, parts_ref, mate_ref, near_ref, place_ref, sems):
    (started,) = copies([(place_vmem, place_ref)], sems)
    started.wait()
    fill(near_ref, place_ref.shape[0] // 2, place_ref, parts_ref, mate_ref)


def project_kernel(places, route_vmem, tiles_ref, *refs):
    columns, refs = refs[: len(places)], refs[len(places) :]
    proj_ref, route_ref, lines_ref, flat_ref, sems = refs
    (started,) = copies([(route_vmem, route_ref)], sems)
    crossed, batches = route_ref.shape
    kinds = tiles_ref.shape[0]
    height = columns[0].shape[1]
    rows = lines_ref.shape[0]
    dense = rows // height * kinds <= crossed * batches
    for ref, aways in zip(columns, places):
        for n, away in enumerate(aways):
            lines_ref[away * height : (away + 1) * height, :] = ref[n]
    if dense:
        for t in range(kinds):
            flat_ref[t * rows : (t + 1) * rows, :] = jnp.dot(lines_ref[...], tiles_ref[t], preferred_element_type=jnp.float32)
    started.wait()

    def project(b, carry):
        acc = None
        for r in range(crossed):
            at = route_ref[r, b]
            if dense:
                part = flat_ref[pl.ds(pl.multiple_of(at, height), height), :]
            else:
                t, at = at // rows, pl.multiple_of(lax.rem(at, rows), height)
                part = jnp.dot(lines_ref[pl.ds(at, height), :], tiles_ref[t], preferred_element_type=jnp.float32)
            acc = part if acc is None else acc + part
        proj_ref[b] = acc
        return carry

    lax.fori_loop(0, batches, project, 0, unroll=dense)


def score_kernel(noise_ref, proj_ref, wave_ref, images_ref, score_ref, part_ref):
    height, pixels = noise_ref.shape
    count = images_ref.shape[0]
    size = count // proj_ref.shape[0]
    noise = noise_ref[...]
    for b in range(count // size):
        proj = proj_ref[b]
        for j in range(size):
            i = b * size + j
            residual = images_ref[i].astype(jnp.float32) - wave_ref[i] * proj
            power = residual * residual * noise
            power = sum(power[n * 8 : (n + 1) * 8] for n in range(height // 8))
            part_ref[i * 8 : (i + 1) * 8, :] = sum(power[:, n * LANES : (n + 1) * LANES] for n in range(pixels // LANES))
    total = sum(part_ref[pl.ds(n, count, 8), :] for n in range(8))
    total = jnp.sum(jnp.transpose(total), axis=0, keepdims=True)
    score_ref[...] = total * (1.0 / (height * pixels))


def on_device(volume, tiles, slab_ids, tile_ids, batch_block, images, defocus, inv_sigma2):
    blocks, crossed = slab_ids.shape
    height, length = volume.shape[1:]
    count, _, pixels = images.shape
    kinds = tiles.shape[0]
    devices = lax.axis_size("slab")
    shape = far, wide, cores = grid_of(devices)
    half = devices // 2
    rows = blocks * 2 * height
    slabs, kind_rows, row = slab_ids.T, tile_ids.T, defocus.reshape(1, count)

    def swap(array, offset):
        return lax.ppermute(array, "slab", [(i, i ^ offset) for i in range(devices)])

    vmem = pl.BlockSpec(memory_space=pltpu.VMEM)
    hbm = pl.BlockSpec(memory_space=pltpu.HBM)
    params = pltpu.CompilerParams(vmem_limit_bytes=VMEM_BYTES)
    f32, bf16 = jnp.float32, jnp.bfloat16
    i32 = jnp.int32

    def call(kernel, outs, inputs, operands, scratch, flops, moved, name):
        operands = [
            pltpu.with_memory_space_constraint(x, pltpu.HBM) if spec is hbm else x for x, spec in zip(operands, inputs)
        ]
        return pl.pallas_call(
            kernel,
            out_shape=tuple(jax.ShapeDtypeStruct(s, t) for s, t in outs),
            in_specs=inputs,
            out_specs=(vmem,) * len(outs),
            scratch_shapes=scratch,
            compiler_params=params,
            cost_estimate=pl.CostEstimate(flops=flops, bytes_accessed=moved, transcendentals=0),
            name=name,
        )(*operands)

    def hop(array, offset):
        return jnp.concatenate([array, swap(array, offset)], axis=0)

    along_z = [z * wide * cores for z in reversed(powers(far))]
    offsets = along_z[:1] + [x * cores for x in powers(wide)] + along_z[1:]
    away = [0]
    for offset in offsets[:-1]:
        away += [a ^ offset for a in away]
    gathered = hop(volume, offsets[0])

    batches = batch_block.shape[0]
    sums, wave, tiles_near, images_near, noise_near, place_rows, route_rows = call(
        functools.partial(sum_kernel, shape, kinds),
        [
            ((rows, pixels), bf16),
            (images.shape, f32),
            (tiles.shape, bf16),
            (images.shape, bf16),
            (inv_sigma2.shape, f32),
            ((devices, blocks), i32),
            ((crossed, batches), i32),
        ],
        [hbm] * 8,
        (slabs, kind_rows, batch_block, batch_block.reshape(1, batches), row, inv_sigma2, tiles, images),
        [
            pltpu.VMEM((crossed, blocks), i32),
            pltpu.VMEM((crossed, blocks), i32),
            pltpu.SMEM((batches,), i32),
            pltpu.VMEM((1, batches), i32),
            pltpu.VMEM((1, count), f32),
            pltpu.VMEM((2, height, count), f32),
            pltpu.VMEM((2, count, pixels), f32),
            pltpu.VMEM((blocks, 2, height, pixels), f32),
            pltpu.SemaphoreType.DMA((CHUNKS + 7,)),
        ],
        0,
        10 << 20,
        "sums",
    )

    place = (2, height, length)
    place_scratch = [pltpu.SMEM((devices, blocks), i32), pltpu.SemaphoreType.DMA((1,))]
    send, keep, parts = call(
        insert_kernel,
        [((half, *place), bf16), ((half - far, *place), f32), ((kinds * rows + 2 * height, length), f32)],
        [vmem] * 3,
        (place_rows, sums, tiles_near),
        place_scratch,
        2 * rows * pixels * kinds * length,
        8 << 20,
        "insert",
    )
    send, gathered = lax.optimization_barrier((send, gathered))
    mate = swap(send, 1)
    def along_x(start, stop):
        return (keep[start:stop] + mate[far + start : far + stop].astype(f32)).astype(bf16)

    main = [along_x(x * far + 1, (x + 1) * far) for x in range(wide - 1)]
    later = [along_x(x * far, x * far + 1) for x in range(wide - 1)]
    (near,) = call(
        near_kernel, [((far, *place), f32)], [vmem] * 3, (place_rows, parts, mate), place_scratch, 0, 0, "near"
    )
    for offset in offsets[1:-1]:
        came, _ = lax.optimization_barrier((swap(gathered, offset), main[0]))
        gathered = jnp.concatenate([gathered, came], axis=0)
    columns = [gathered, swap(gathered, offsets[-1])]
    columns += [swap(column, 1) for column in columns]
    places = [[a ^ last for a in away] for last in (0, offsets[-1], 1, offsets[-1] ^ 1)]
    mine, total = near[1:], near[0]
    for x in range(1, wide):
        mine = mine + swap(main[x - 1], x * cores).astype(f32)
        total = total + swap(later[x - 1], x * cores)[0].astype(f32)
    outgoing = mine.astype(bf16)
    _, *columns = lax.optimization_barrier((outgoing, *columns))
    if devices * kinds <= batches * crossed:
        flat = pltpu.VMEM((kinds * devices * height, pixels), f32)
    else:
        flat = pltpu.VMEM((8, LANES), f32)
    (proj,) = call(
        functools.partial(project_kernel, places),
        [((batches, height, pixels), f32)],
        [vmem] * (2 + len(columns)),
        (route_rows, tiles_near, *columns),
        [pltpu.SMEM((crossed, batches), i32), pltpu.VMEM((devices * height, length), bf16), flat, pltpu.SemaphoreType.DMA((1,))],
        0,
        0,
        "project",
    )

    (scores,) = call(
        score_kernel,
        [((1, count), f32)],
        [vmem] * 4,
        (noise_near, proj, wave, images_near),
        [pltpu.VMEM((count * 8, LANES), f32)],
        0,
        0,
        "scores",
    )
    for z in range(far - 1, 0, -1):
        came = swap(outgoing[z - 1], z * wide * cores)
        if z == far - 1:
            came, scores = lax.optimization_barrier((came, scores))
        total = total + came.astype(f32)
    return scores.reshape(count), total[0:1], total[1:2]


def solution(mesh):
    placed = (
        P(("parts", "slab"), None, None),
        P(),
        P(("parts", "slab"), None),
        P(("parts", "slab"), None),
        P(("parts", "slab")),
        P(("parts", "slab"), None, None),
        P(("parts", "slab")),
        P("parts", None),
    )
    return jax.shard_map(
        on_device,
        mesh=mesh,
        in_specs=placed,
        out_specs=(
            P(("parts", "slab")),
            P(("parts", "slab"), None, None),
            P(("parts", "slab"), None, None),
        ),
        check_vma=False,
    )
```

```python
import functools

import jax
import jax.numpy as jnp
from jax import lax
from jax.experimental import pallas as pl
from jax.experimental.pallas import tpu as pltpu
from jax.sharding import PartitionSpec as P

LANES = 128
CHUNKS = 4
VMEM_BYTES = 24 * 1024 * 1024


def grid_of(devices):
    cores = 2 if devices % 2 == 0 else 1
    chips = devices // cores
    wide = 1
    while (2 * wide) ** 3 <= chips:
        wide *= 2
    return chips // wide, wide, cores


def powers(size):
    return [1 << n for n in range(size.bit_length() - 1)]


def sin_cos(angle):
    turns = jnp.floor(angle * 0.3183098861837907 + 0.5)
    rest = angle - turns * 3.140625
    rest = rest - turns * 9.675025939941406e-4
    rest = rest - turns * 1.5099580252808664e-7
    half = turns * 0.5
    sign = 1.0 - 4.0 * (half - jnp.floor(half))
    sq = rest * rest
    sin = rest * (1.0 + sq * (-1.0 / 6 + sq * (1.0 / 120 + sq * (-1.0 / 5040 + sq * (1.0 / 362880 + sq * (-1.0 / 39916800))))))
    cos = 1.0 + sq * (-0.5 + sq * (1.0 / 24 + sq * (-1.0 / 720 + sq * (1.0 / 40320 + sq * (-1.0 / 3628800 + sq * (1.0 / 479001600))))))
    return sign * sin, sign * cos


def tables(defocus_ref, height, pixels, line_ref, pixel_ref):
    images = defocus_ref.shape[1]
    defocus = defocus_ref[...]
    rows = lax.broadcasted_iota(jnp.int32, (height, images), 0)
    line = ((rows // 2 + 1).astype(jnp.float32) / (height // 2)) ** 2
    line_ref[0], line_ref[1] = sin_cos(defocus * line + 0.3)
    column = jnp.transpose(jnp.broadcast_to(defocus, (LANES, images)))
    part = 32
    lanes = lax.broadcasted_iota(jnp.int32, (part, LANES), 1)
    for n in range(images // part):
        rows = slice(n * part, (n + 1) * part)
        for m in range(pixels // LANES):
            pixel = ((lanes + (m * LANES + 1)).astype(jnp.float32) / pixels) ** 2
            at = slice(m * LANES, (m + 1) * LANES)
            pixel_ref[0, rows, at], pixel_ref[1, rows, at] = sin_cos(column[rows] * pixel)


def contrast_of(line_ref, pixel_ref, i):
    sin_line, cos_line = line_ref[0, :, i : i + 1], line_ref[1, :, i : i + 1]
    return sin_line * pixel_ref[1, i : i + 1, :] + cos_line * pixel_ref[0, i : i + 1, :]


def copies(pairs, sems):
    started = [pltpu.make_async_copy(source, target, sems.at[n]) for n, (source, target) in enumerate(pairs)]
    for copy in started:
        copy.start()
    return started


def row_tables(shape, kinds, height, slab, tile, owner, place_ref, route_ref):
    far, wide, cores = shape
    devices, blocks = place_ref.shape
    rows, half = blocks * 2 * height, devices // 2
    me = lax.axis_index("slab")
    slot = lax.broadcasted_iota(jnp.int32, (devices, blocks), 0)
    block = lax.broadcasted_iota(jnp.int32, (devices, blocks), 1)
    within = slot & (half - 1)
    core = jnp.where(slot < half, cores - 1, 0)
    named = me ^ (((within & (far - 1)) * wide + within // far) * cores + core)
    place = jnp.full((devices, blocks), kinds * rows, jnp.int32)
    for r in range(slab.shape[0]):
        row = tile[r : r + 1, :] * rows + block * (2 * height)
        place = jnp.where(slab[r : r + 1, :] == named, row, place)
    place_ref[...] = place
    row = (tile * devices + (me ^ slab)) * height
    route = jnp.zeros(route_ref.shape, jnp.int32)
    for k in range(blocks):
        route = jnp.where(owner == k, row[:, k : k + 1], route)
    route_ref[...] = route


def sum_kernel(shape, kinds, slab_hbm, tile_hbm, block_hbm, owner_hbm, defocus_hbm, noise_hbm, tiles_hbm, images_hbm,
               sums_ref, wave_ref, tiles_ref, images_ref, noise_ref, place_ref, route_ref,
               slab_ref, tile_ref, block_ref, owner_ref, defocus_ref, line_ref, pixel_ref, acc_ref, sems):
    count = images_ref.shape[0]
    part = count // CHUNKS
    small = [(defocus_hbm, defocus_ref), (block_hbm, block_ref), (noise_hbm, noise_ref)]
    small += [(slab_hbm, slab_ref), (tile_hbm, tile_ref), (owner_hbm, owner_ref)]
    large = [(images_hbm.at[pl.ds(n * part, part)], images_ref.at[pl.ds(n * part, part)]) for n in range(CHUNKS)]
    started = copies(small + large, sems)
    last = pltpu.make_async_copy(tiles_hbm, tiles_ref, sems.at[len(started)])
    height, pixels = noise_ref.shape
    batches = block_ref.shape[0]
    size = count // batches
    acc_ref[...] = jnp.zeros_like(acc_ref)
    for copy in started[: len(small)]:
        copy.wait()
    tables(defocus_ref, height, pixels, line_ref, pixel_ref)
    row_tables(shape, kinds, height, slab_ref[...], tile_ref[...], owner_ref[...], place_ref, route_ref)
    for b in range(batches):
        if b % (batches // CHUNKS) == 0:
            started[len(small) + b // (batches // CHUNKS)].wait()
        if b == 0:
            last.start()
        data = jnp.zeros((height, pixels), jnp.float32)
        weight = jnp.zeros((height, pixels), jnp.float32)
        for j in range(size):
            i = b * size + j
            wave = contrast_of(line_ref, pixel_ref, i)
            wave_ref[i] = wave
            data = data + wave * images_ref[i].astype(jnp.float32)
            weight = weight + wave * wave
        k = block_ref[b]
        acc_ref[k, 0] = acc_ref[k, 0] + data
        acc_ref[k, 1] = acc_ref[k, 1] + weight
    sums = (acc_ref[...] * noise_ref[...][None, None]).astype(jnp.bfloat16)
    sums_ref[...] = sums.reshape(sums_ref.shape)
    last.wait()


def fill(ref, start, place_ref, parts_ref, mate_ref=None):
    sides, height, length = ref.shape[1:]

    def step(slot, carry):
        acc = None
        for k in range(place_ref.shape[1]):
            at = pl.multiple_of(place_ref[start + slot, k], sides * height)
            part = parts_ref[pl.ds(at, sides * height), :]
            acc = part if acc is None else acc + part
        acc = acc.reshape(sides, height, length)
        if mate_ref is not None:
            acc = acc + mate_ref[slot].astype(jnp.float32)
        ref[slot] = acc.astype(ref.dtype)
        return carry

    lax.fori_loop(0, ref.shape[0], step, 0)


def insert_kernel(place_vmem, sums_ref, tiles_ref, send_ref, far_ref, parts_ref, place_ref, sems):
    (started,) = copies([(place_vmem, place_ref)], sems)
    kinds = tiles_ref.shape[0]
    rows = sums_ref.shape[0]
    zeros = parts_ref.shape[0] - kinds * rows
    parts_ref[kinds * rows :, :] = jnp.zeros((zeros, parts_ref.shape[1]), jnp.float32)
    for t in range(kinds):
        parts_ref[t * rows : (t + 1) * rows, :] = lax.dot_general(
            sums_ref[...], tiles_ref[t], (((1,), (1,)), ((), ())), preferred_element_type=jnp.float32
        )
    started.wait()
    fill(send_ref, 0, place_ref, parts_ref)
    devices = place_ref.shape[0]
    fill(far_ref, devices - far_ref.shape[0], place_ref, parts_ref)


def near_kernel(place_vmem, parts_ref, mate_ref, near_ref, place_ref, sems):
    (started,) = copies([(place_vmem, place_ref)], sems)
    started.wait()
    fill(near_ref, place_ref.shape[0] // 2, place_ref, parts_ref, mate_ref)


def project_kernel(places, route_vmem, tiles_ref, *refs):
    columns, refs = refs[: len(places)], refs[len(places) :]
    proj_ref, route_ref, lines_ref, flat_ref, sems = refs
    (started,) = copies([(route_vmem, route_ref)], sems)
    crossed, batches = route_ref.shape
    kinds = tiles_ref.shape[0]
    height = columns[0].shape[1]
    rows = lines_ref.shape[0]
    dense = rows // height * kinds <= crossed * batches
    for ref, aways in zip(columns, places):
        for n, away in enumerate(aways):
            lines_ref[away * height : (away + 1) * height, :] = ref[n]
    if dense:
        for t in range(kinds):
            flat_ref[t * rows : (t + 1) * rows, :] = jnp.dot(lines_ref[...], tiles_ref[t], preferred_element_type=jnp.float32)
    started.wait()

    def project(b, carry):
        acc = None
        for r in range(crossed):
            at = route_ref[r, b]
            if dense:
                part = flat_ref[pl.ds(pl.multiple_of(at, height), height), :]
            else:
                t, at = at // rows, pl.multiple_of(lax.rem(at, rows), height)
                part = jnp.dot(lines_ref[pl.ds(at, height), :], tiles_ref[t], preferred_element_type=jnp.float32)
            acc = part if acc is None else acc + part
        proj_ref[b] = acc
        return carry

    lax.fori_loop(0, batches, project, 0, unroll=dense)


def score_kernel(noise_ref, proj_ref, wave_ref, images_ref, score_ref, part_ref):
    height, pixels = noise_ref.shape
    count = images_ref.shape[0]
    size = count // proj_ref.shape[0]
    noise = noise_ref[...]
    for b in range(count // size):
        proj = proj_ref[b]
        for j in range(size):
            i = b * size + j
            residual = images_ref[i].astype(jnp.float32) - wave_ref[i] * proj
            power = residual * residual * noise
            power = sum(power[n * 8 : (n + 1) * 8] for n in range(height // 8))
            part_ref[i * 8 : (i + 1) * 8, :] = sum(power[:, n * LANES : (n + 1) * LANES] for n in range(pixels // LANES))
    total = sum(part_ref[pl.ds(n, count, 8), :] for n in range(8))
    total = jnp.sum(jnp.transpose(total), axis=0, keepdims=True)
    score_ref[...] = total * (1.0 / (height * pixels))


def on_device(volume, tiles, slab_ids, tile_ids, batch_block, images, defocus, inv_sigma2):
    blocks, crossed = slab_ids.shape
    height, length = volume.shape[1:]
    count, _, pixels = images.shape
    kinds = tiles.shape[0]
    devices = lax.axis_size("slab")
    shape = far, wide, cores = grid_of(devices)
    half = devices // 2
    rows = blocks * 2 * height
    slabs, kind_rows, row = slab_ids.T, tile_ids.T, defocus.reshape(1, count)

    def swap(array, offset):
        return lax.ppermute(array, "slab", [(i, i ^ offset) for i in range(devices)])

    vmem = pl.BlockSpec(memory_space=pltpu.VMEM)
    hbm = pl.BlockSpec(memory_space=pltpu.HBM)
    params = pltpu.CompilerParams(vmem_limit_bytes=VMEM_BYTES)
    f32, bf16 = jnp.float32, jnp.bfloat16
    i32 = jnp.int32

    def call(kernel, outs, inputs, operands, scratch, flops, moved, name):
        operands = [
            pltpu.with_memory_space_constraint(x, pltpu.HBM) if spec is hbm else x for x, spec in zip(operands, inputs)
        ]
        return pl.pallas_call(
            kernel,
            out_shape=tuple(jax.ShapeDtypeStruct(s, t) for s, t in outs),
            in_specs=inputs,
            out_specs=(vmem,) * len(outs),
            scratch_shapes=scratch,
            compiler_params=params,
            cost_estimate=pl.CostEstimate(flops=flops, bytes_accessed=moved, transcendentals=0),
            name=name,
        )(*operands)

    def hop(array, offset):
        return jnp.concatenate([array, swap(array, offset)], axis=0)

    along_z = [z * wide * cores for z in reversed(powers(far))]
    offsets = along_z[:1] + [x * cores for x in powers(wide)] + along_z[1:]
    away = [0]
    for offset in offsets[:-1]:
        away += [a ^ offset for a in away]
    gathered = hop(volume, offsets[0])

    batches = batch_block.shape[0]
    sums, wave, tiles_near, images_near, noise_near, place_rows, route_rows = call(
        functools.partial(sum_kernel, shape, kinds),
        [
            ((rows, pixels), bf16),
            (images.shape, f32),
            (tiles.shape, bf16),
            (images.shape, bf16),
            (inv_sigma2.shape, f32),
            ((devices, blocks), i32),
            ((crossed, batches), i32),
        ],
        [hbm] * 8,
        (slabs, kind_rows, batch_block, batch_block.reshape(1, batches), row, inv_sigma2, tiles, images),
        [
            pltpu.VMEM((crossed, blocks), i32),
            pltpu.VMEM((crossed, blocks), i32),
            pltpu.SMEM((batches,), i32),
            pltpu.VMEM((1, batches), i32),
            pltpu.VMEM((1, count), f32),
            pltpu.VMEM((2, height, count), f32),
            pltpu.VMEM((2, count, pixels), f32),
            pltpu.VMEM((blocks, 2, height, pixels), f32),
            pltpu.SemaphoreType.DMA((CHUNKS + 7,)),
        ],
        0,
        10 << 20,
        "sums",
    )

    place = (2, height, length)
    place_scratch = [pltpu.SMEM((devices, blocks), i32), pltpu.SemaphoreType.DMA((1,))]
    send, keep, parts = call(
        insert_kernel,
        [((half, *place), bf16), ((half - far, *place), f32), ((kinds * rows + 2 * height, length), f32)],
        [vmem] * 3,
        (place_rows, sums, tiles_near),
        place_scratch,
        2 * rows * pixels * kinds * length,
        8 << 20,
        "insert",
    )
    send, gathered = lax.optimization_barrier((send, gathered))
    mate = swap(send, 1)
    def along_x(start, stop):
        return (keep[start:stop] + mate[far + start : far + stop].astype(f32)).astype(bf16)

    main = [along_x(x * far + 1, (x + 1) * far) for x in range(wide - 1)]
    later = [along_x(x * far, x * far + 1) for x in range(wide - 1)]
    (near,) = call(
        near_kernel, [((far, *place), f32)], [vmem] * 3, (place_rows, parts, mate), place_scratch, 0, 0, "near"
    )
    for offset in offsets[1:-1]:
        came, _ = lax.optimization_barrier((swap(gathered, offset), main[0]))
        gathered = jnp.concatenate([gathered, came], axis=0)
    columns = [gathered, swap(gathered, offsets[-1])]
    columns += [swap(column, 1) for column in columns]
    places = [[a ^ last for a in away] for last in (0, offsets[-1], 1, offsets[-1] ^ 1)]
    total, outgoing = near[0], [near[z] for z in range(1, far)]
    for x in range(1, wide):
        came = swap(main[x - 1], x * cores)
        outgoing = [mine + came[z].astype(f32) for z, mine in enumerate(outgoing)]
        total = total + swap(later[x - 1], x * cores)[0].astype(f32)
    outgoing = [mine.astype(bf16) for mine in outgoing]
    _, *columns = lax.optimization_barrier((outgoing[0], *columns))
    if devices * kinds <= batches * crossed:
        flat = pltpu.VMEM((kinds * devices * height, pixels), f32)
    else:
        flat = pltpu.VMEM((8, LANES), f32)
    (proj,) = call(
        functools.partial(project_kernel, places),
        [((batches, height, pixels), f32)],
        [vmem] * (2 + len(columns)),
        (route_rows, tiles_near, *columns),
        [pltpu.SMEM((crossed, batches), i32), pltpu.VMEM((devices * height, length), bf16), flat, pltpu.SemaphoreType.DMA((1,))],
        0,
        0,
        "project",
    )

    (scores,) = call(
        score_kernel,
        [((1, count), f32)],
        [vmem] * 4,
        (noise_near, proj, wave, images_near),
        [pltpu.VMEM((count * 8, LANES), f32)],
        0,
        0,
        "scores",
    )
    for z in range(1, far):
        came = swap(outgoing[z - 1], z * wide * cores)
        if z == far - 1:
            came, scores = lax.optimization_barrier((came, scores))
        total = total + came.astype(f32)
    return scores.reshape(count), total[0:1], total[1:2]


def solution(mesh):
    placed = (
        P(("parts", "slab"), None, None),
        P(),
        P(("parts", "slab"), None),
        P(("parts", "slab"), None),
        P(("parts", "slab")),
        P(("parts", "slab"), None, None),
        P(("parts", "slab")),
        P("parts", None),
    )
    return jax.shard_map(
        on_device,
        mesh=mesh,
        in_specs=placed,
        out_specs=(
            P(("parts", "slab")),
            P(("parts", "slab"), None, None),
            P(("parts", "slab"), None, None),
        ),
        check_vma=False,
    )
```

```python
import functools

import jax
import jax.numpy as jnp
from jax import lax
from jax.experimental import pallas as pl
from jax.experimental.pallas import tpu as pltpu
from jax.sharding import PartitionSpec as P

LANES = 128
CHUNKS = 4
VMEM_BYTES = 24 * 1024 * 1024


def grid_of(devices):
    cores = 2 if devices % 2 == 0 else 1
    chips = devices // cores
    wide = 1
    while (2 * wide) ** 3 <= chips:
        wide *= 2
    return chips // wide, wide, cores


def powers(size):
    return [1 << n for n in range(size.bit_length() - 1)]


def sin_cos(angle):
    turns = jnp.floor(angle * 0.3183098861837907 + 0.5)
    rest = angle - turns * 3.140625
    rest = rest - turns * 9.675025939941406e-4
    rest = rest - turns * 1.5099580252808664e-7
    half = turns * 0.5
    sign = 1.0 - 4.0 * (half - jnp.floor(half))
    sq = rest * rest
    sin = rest * (1.0 + sq * (-1.0 / 6 + sq * (1.0 / 120 + sq * (-1.0 / 5040 + sq * (1.0 / 362880 + sq * (-1.0 / 39916800))))))
    cos = 1.0 + sq * (-0.5 + sq * (1.0 / 24 + sq * (-1.0 / 720 + sq * (1.0 / 40320 + sq * (-1.0 / 3628800 + sq * (1.0 / 479001600))))))
    return sign * sin, sign * cos


def tables(defocus_ref, height, pixels, line_ref, pixel_ref):
    images = defocus_ref.shape[1]
    defocus = defocus_ref[...]
    rows = lax.broadcasted_iota(jnp.int32, (height, images), 0)
    line = ((rows // 2 + 1).astype(jnp.float32) / (height // 2)) ** 2
    line_ref[0], line_ref[1] = sin_cos(defocus * line + 0.3)
    column = jnp.transpose(jnp.broadcast_to(defocus, (LANES, images)))
    part = 32
    lanes = lax.broadcasted_iota(jnp.int32, (part, LANES), 1)
    for n in range(images // part):
        rows = slice(n * part, (n + 1) * part)
        for m in range(pixels // LANES):
            pixel = ((lanes + (m * LANES + 1)).astype(jnp.float32) / pixels) ** 2
            at = slice(m * LANES, (m + 1) * LANES)
            pixel_ref[0, rows, at], pixel_ref[1, rows, at] = sin_cos(column[rows] * pixel)


def contrast_of(line_ref, pixel_ref, i):
    sin_line, cos_line = line_ref[0, :, i : i + 1], line_ref[1, :, i : i + 1]
    return sin_line * pixel_ref[1, i : i + 1, :] + cos_line * pixel_ref[0, i : i + 1, :]


def copies(pairs, sems):
    started = [pltpu.make_async_copy(source, target, sems.at[n]) for n, (source, target) in enumerate(pairs)]
    for copy in started:
        copy.start()
    return started


def row_tables(shape, kinds, height, slab, tile, owner, place_ref, route_ref):
    far, wide, cores = shape
    devices, blocks = place_ref.shape
    rows, half = blocks * 2 * height, devices // 2
    me = lax.axis_index("slab")
    slot = lax.broadcasted_iota(jnp.int32, (devices, blocks), 0)
    block = lax.broadcasted_iota(jnp.int32, (devices, blocks), 1)
    within = slot & (half - 1)
    core = jnp.where(slot < half, cores - 1, 0)
    named = me ^ (((within & (far - 1)) * wide + within // far) * cores + core)
    place = jnp.full((devices, blocks), kinds * rows, jnp.int32)
    for r in range(slab.shape[0]):
        row = tile[r : r + 1, :] * rows + block * (2 * height)
        place = jnp.where(slab[r : r + 1, :] == named, row, place)
    place_ref[...] = place
    row = (tile * devices + (me ^ slab)) * height
    route = jnp.zeros(route_ref.shape, jnp.int32)
    for k in range(blocks):
        route = jnp.where(owner == k, row[:, k : k + 1], route)
    route_ref[...] = route


def sum_kernel(shape, kinds, slab_hbm, tile_hbm, block_hbm, owner_hbm, defocus_hbm, noise_hbm, tiles_hbm, images_hbm,
               sums_ref, wave_ref, tiles_ref, images_ref, noise_ref, place_ref, route_ref,
               slab_ref, tile_ref, block_ref, owner_ref, defocus_ref, line_ref, pixel_ref, acc_ref, sems):
    count = images_ref.shape[0]
    part = count // CHUNKS
    small = [(defocus_hbm, defocus_ref), (block_hbm, block_ref), (noise_hbm, noise_ref)]
    small += [(slab_hbm, slab_ref), (tile_hbm, tile_ref), (owner_hbm, owner_ref)]
    large = [(images_hbm.at[pl.ds(n * part, part)], images_ref.at[pl.ds(n * part, part)]) for n in range(CHUNKS)]
    started = copies(small + large, sems)
    last = pltpu.make_async_copy(tiles_hbm, tiles_ref, sems.at[len(started)])
    height, pixels = noise_ref.shape
    batches = block_ref.shape[0]
    size = count // batches
    acc_ref[...] = jnp.zeros_like(acc_ref)
    for copy in started[: len(small)]:
        copy.wait()
    tables(defocus_ref, height, pixels, line_ref, pixel_ref)
    row_tables(shape, kinds, height, slab_ref[...], tile_ref[...], owner_ref[...], place_ref, route_ref)
    for b in range(batches):
        if b % (batches // CHUNKS) == 0:
            started[len(small) + b // (batches // CHUNKS)].wait()
        if b == 0:
            last.start()
        data = jnp.zeros((height, pixels), jnp.float32)
        weight = jnp.zeros((height, pixels), jnp.float32)
        for j in range(size):
            i = b * size + j
            wave = contrast_of(line_ref, pixel_ref, i)
            wave_ref[i] = wave
            data = data + wave * images_ref[i].astype(jnp.float32)
            weight = weight + wave * wave
        k = block_ref[b]
        acc_ref[k, 0] = acc_ref[k, 0] + data
        acc_ref[k, 1] = acc_ref[k, 1] + weight
    sums = (acc_ref[...] * noise_ref[...][None, None]).astype(jnp.bfloat16)
    sums_ref[...] = sums.reshape(sums_ref.shape)
    last.wait()


def fill(ref, start, place_ref, parts_ref, mate_ref=None):
    sides, height, length = ref.shape[1:]

    def step(slot, carry):
        acc = None
        for k in range(place_ref.shape[1]):
            at = pl.multiple_of(place_ref[start + slot, k], sides * height)
            part = parts_ref[pl.ds(at, sides * height), :]
            acc = part if acc is None else acc + part
        acc = acc.reshape(sides, height, length)
        if mate_ref is not None:
            acc = acc + mate_ref[slot].astype(jnp.float32)
        ref[slot] = acc.astype(ref.dtype)
        return carry

    lax.fori_loop(0, ref.shape[0], step, 0)


def insert_kernel(place_vmem, sums_ref, tiles_ref, send_ref, far_ref, parts_ref, place_ref, sems):
    (started,) = copies([(place_vmem, place_ref)], sems)
    kinds = tiles_ref.shape[0]
    rows = sums_ref.shape[0]
    zeros = parts_ref.shape[0] - kinds * rows
    parts_ref[kinds * rows :, :] = jnp.zeros((zeros, parts_ref.shape[1]), jnp.float32)
    for t in range(kinds):
        parts_ref[t * rows : (t + 1) * rows, :] = lax.dot_general(
            sums_ref[...], tiles_ref[t], (((1,), (1,)), ((), ())), preferred_element_type=jnp.float32
        )
    started.wait()
    fill(send_ref, 0, place_ref, parts_ref)
    devices = place_ref.shape[0]
    fill(far_ref, devices - far_ref.shape[0], place_ref, parts_ref)


def near_kernel(place_vmem, parts_ref, mate_ref, near_ref, place_ref, sems):
    (started,) = copies([(place_vmem, place_ref)], sems)
    started.wait()
    fill(near_ref, place_ref.shape[0] // 2, place_ref, parts_ref, mate_ref)


def project_kernel(places, route_vmem, tiles_ref, *refs):
    columns, refs = refs[: len(places)], refs[len(places) :]
    proj_ref, route_ref, lines_ref, flat_ref, sems = refs
    (started,) = copies([(route_vmem, route_ref)], sems)
    crossed, batches = route_ref.shape
    kinds = tiles_ref.shape[0]
    height = columns[0].shape[1]
    rows = lines_ref.shape[0]
    dense = rows // height * kinds <= crossed * batches
    for ref, aways in zip(columns, places):
        for n, away in enumerate(aways):
            lines_ref[away * height : (away + 1) * height, :] = ref[n]
    if dense:
        for t in range(kinds):
            flat_ref[t * rows : (t + 1) * rows, :] = jnp.dot(lines_ref[...], tiles_ref[t], preferred_element_type=jnp.float32)
    started.wait()

    def project(b, carry):
        acc = None
        for r in range(crossed):
            at = route_ref[r, b]
            if dense:
                part = flat_ref[pl.ds(pl.multiple_of(at, height), height), :]
            else:
                t, at = at // rows, pl.multiple_of(lax.rem(at, rows), height)
                part = jnp.dot(lines_ref[pl.ds(at, height), :], tiles_ref[t], preferred_element_type=jnp.float32)
            acc = part if acc is None else acc + part
        proj_ref[b] = acc
        return carry

    lax.fori_loop(0, batches, project, 0, unroll=dense)


def score_kernel(noise_ref, proj_ref, wave_ref, images_ref, score_ref, part_ref):
    height, pixels = noise_ref.shape
    count = images_ref.shape[0]
    size = count // proj_ref.shape[0]
    noise = noise_ref[...]
    for b in range(count // size):
        proj = proj_ref[b]
        for j in range(size):
            i = b * size + j
            residual = images_ref[i].astype(jnp.float32) - wave_ref[i] * proj
            power = residual * residual * noise
            power = sum(power[n * 8 : (n + 1) * 8] for n in range(height // 8))
            part_ref[i * 8 : (i + 1) * 8, :] = sum(power[:, n * LANES : (n + 1) * LANES] for n in range(pixels // LANES))
    total = sum(part_ref[pl.ds(n, count, 8), :] for n in range(8))
    total = jnp.sum(jnp.transpose(total), axis=0, keepdims=True)
    score_ref[...] = total * (1.0 / (height * pixels))


def on_device(volume, tiles, slab_ids, tile_ids, batch_block, images, defocus, inv_sigma2):
    blocks, crossed = slab_ids.shape
    height, length = volume.shape[1:]
    count, _, pixels = images.shape
    kinds = tiles.shape[0]
    devices = lax.axis_size("slab")
    shape = far, wide, cores = grid_of(devices)
    half = devices // 2
    rows = blocks * 2 * height
    slabs, kind_rows, row = slab_ids.T, tile_ids.T, defocus.reshape(1, count)

    def swap(array, offset):
        return lax.ppermute(array, "slab", [(i, i ^ offset) for i in range(devices)])

    vmem = pl.BlockSpec(memory_space=pltpu.VMEM)
    hbm = pl.BlockSpec(memory_space=pltpu.HBM)
    params = pltpu.CompilerParams(vmem_limit_bytes=VMEM_BYTES)
    f32, bf16 = jnp.float32, jnp.bfloat16
    i32 = jnp.int32

    def call(kernel, outs, inputs, operands, scratch, flops, moved, name):
        operands = [
            pltpu.with_memory_space_constraint(x, pltpu.HBM) if spec is hbm else x for x, spec in zip(operands, inputs)
        ]
        return pl.pallas_call(
            kernel,
            out_shape=tuple(jax.ShapeDtypeStruct(s, t) for s, t in outs),
            in_specs=inputs,
            out_specs=(vmem,) * len(outs),
            scratch_shapes=scratch,
            compiler_params=params,
            cost_estimate=pl.CostEstimate(flops=flops, bytes_accessed=moved, transcendentals=0),
            name=name,
        )(*operands)

    def hop(array, offset):
        return jnp.concatenate([array, swap(array, offset)], axis=0)

    along_z = [z * wide * cores for z in reversed(powers(far))]
    offsets = along_z[:1] + [x * cores for x in powers(wide)] + along_z[1:]
    away = [0]
    for offset in offsets[:-1]:
        away += [a ^ offset for a in away]
    gathered = hop(volume, offsets[0])

    batches = batch_block.shape[0]
    sums, wave, tiles_near, images_near, noise_near, place_rows, route_rows = call(
        functools.partial(sum_kernel, shape, kinds),
        [
            ((rows, pixels), bf16),
            (images.shape, f32),
            (tiles.shape, bf16),
            (images.shape, bf16),
            (inv_sigma2.shape, f32),
            ((devices, blocks), i32),
            ((crossed, batches), i32),
        ],
        [hbm] * 8,
        (slabs, kind_rows, batch_block, batch_block.reshape(1, batches), row, inv_sigma2, tiles, images),
        [
            pltpu.VMEM((crossed, blocks), i32),
            pltpu.VMEM((crossed, blocks), i32),
            pltpu.SMEM((batches,), i32),
            pltpu.VMEM((1, batches), i32),
            pltpu.VMEM((1, count), f32),
            pltpu.VMEM((2, height, count), f32),
            pltpu.VMEM((2, count, pixels), f32),
            pltpu.VMEM((blocks, 2, height, pixels), f32),
            pltpu.SemaphoreType.DMA((CHUNKS + 7,)),
        ],
        0,
        10 << 20,
        "sums",
    )

    place = (2, height, length)
    place_scratch = [pltpu.SMEM((devices, blocks), i32), pltpu.SemaphoreType.DMA((1,))]
    send, keep, parts = call(
        insert_kernel,
        [((half, *place), bf16), ((half - far, *place), f32), ((kinds * rows + 2 * height, length), f32)],
        [vmem] * 3,
        (place_rows, sums, tiles_near),
        place_scratch,
        2 * rows * pixels * kinds * length,
        8 << 20,
        "insert",
    )
    send, gathered = lax.optimization_barrier((send, gathered))
    mate = swap(send, 1)
    def along_x(start, stop):
        return (keep[start:stop] + mate[far + start : far + stop].astype(f32)).astype(bf16)

    cut = max(1, far // 2)
    main = [along_x(x * far + cut, (x + 1) * far) for x in range(wide - 1)]
    later = [along_x(x * far, x * far + cut) for x in range(wide - 1)]
    (near,) = call(
        near_kernel, [((far, *place), f32)], [vmem] * 3, (place_rows, parts, mate), place_scratch, 0, 0, "near"
    )
    for offset in offsets[1:-1]:
        came, _ = lax.optimization_barrier((swap(gathered, offset), near))
        gathered = jnp.concatenate([gathered, came], axis=0)
    mine = [near[z] for z in range(far)]
    for x in range(1, wide):
        came = swap(main[x - 1], x * cores)
        for z in range(cut, far):
            mine[z] = mine[z] + came[z - cut].astype(f32)
    outgoing = {z: mine[z].astype(bf16) for z in range(cut, far)}
    for x in range(1, wide):
        came, _ = lax.optimization_barrier((swap(later[x - 1], x * cores), outgoing[far - 1]))
        for z in range(cut):
            mine[z] = mine[z] + came[z].astype(f32)
    outgoing.update({z: mine[z].astype(bf16) for z in range(1, cut)})
    total = mine[0]

    columns = [gathered, swap(gathered, offsets[-1])]
    columns += [swap(column, 1) for column in columns]
    _, *columns = lax.optimization_barrier((outgoing[1], *columns))
    places = [[a ^ last for a in away] for last in (0, offsets[-1], 1, offsets[-1] ^ 1)]
    if devices * kinds <= batches * crossed:
        flat = pltpu.VMEM((kinds * devices * height, pixels), f32)
    else:
        flat = pltpu.VMEM((8, LANES), f32)
    (proj,) = call(
        functools.partial(project_kernel, places),
        [((batches, height, pixels), f32)],
        [vmem] * (2 + len(columns)),
        (route_rows, tiles_near, *columns),
        [pltpu.SMEM((crossed, batches), i32), pltpu.VMEM((devices * height, length), bf16), flat, pltpu.SemaphoreType.DMA((1,))],
        0,
        0,
        "project",
    )

    (scores,) = call(
        score_kernel,
        [((1, count), f32)],
        [vmem] * 4,
        (noise_near, proj, wave, images_near),
        [pltpu.VMEM((count * 8, LANES), f32)],
        0,
        0,
        "scores",
    )
    for z in range(1, far):
        came = swap(outgoing[z], z * wide * cores)
        if z >= cut:
            came, scores = lax.optimization_barrier((came, scores))
        total = total + came.astype(f32)
    return scores.reshape(count), total[0:1], total[1:2]


def solution(mesh):
    placed = (
        P(("parts", "slab"), None, None),
        P(),
        P(("parts", "slab"), None),
        P(("parts", "slab"), None),
        P(("parts", "slab")),
        P(("parts", "slab"), None, None),
        P(("parts", "slab")),
        P("parts", None),
    )
    return jax.shard_map(
        on_device,
        mesh=mesh,
        in_specs=placed,
        out_specs=(
            P(("parts", "slab")),
            P(("parts", "slab"), None, None),
            P(("parts", "slab"), None, None),
        ),
        check_vma=False,
    )
```

```python
import functools

import jax
import jax.numpy as jnp
from jax import lax
from jax.experimental import pallas as pl
from jax.experimental.pallas import tpu as pltpu
from jax.sharding import PartitionSpec as P

LANES = 128
CHUNKS = 4
VMEM_BYTES = 24 * 1024 * 1024


def grid_of(devices):
    cores = 2 if devices % 2 == 0 else 1
    chips = devices // cores
    wide = 1
    while (2 * wide) ** 3 <= chips:
        wide *= 2
    return chips // wide, wide, cores


def powers(size):
    return [1 << n for n in range(size.bit_length() - 1)]


def sin_cos(angle):
    turns = jnp.floor(angle * 0.3183098861837907 + 0.5)
    rest = angle - turns * 3.140625
    rest = rest - turns * 9.675025939941406e-4
    rest = rest - turns * 1.5099580252808664e-7
    half = turns * 0.5
    sign = 1.0 - 4.0 * (half - jnp.floor(half))
    sq = rest * rest
    sin = rest * (1.0 + sq * (-1.0 / 6 + sq * (1.0 / 120 + sq * (-1.0 / 5040 + sq * (1.0 / 362880 + sq * (-1.0 / 39916800))))))
    cos = 1.0 + sq * (-0.5 + sq * (1.0 / 24 + sq * (-1.0 / 720 + sq * (1.0 / 40320 + sq * (-1.0 / 3628800 + sq * (1.0 / 479001600))))))
    return sign * sin, sign * cos


def tables(defocus_ref, height, pixels, line_ref, pixel_ref):
    images = defocus_ref.shape[1]
    defocus = defocus_ref[...]
    rows = lax.broadcasted_iota(jnp.int32, (height, images), 0)
    line = ((rows // 2 + 1).astype(jnp.float32) / (height // 2)) ** 2
    line_ref[0], line_ref[1] = sin_cos(defocus * line + 0.3)
    column = jnp.transpose(jnp.broadcast_to(defocus, (LANES, images)))
    part = 32
    lanes = lax.broadcasted_iota(jnp.int32, (part, LANES), 1)
    for n in range(images // part):
        rows = slice(n * part, (n + 1) * part)
        for m in range(pixels // LANES):
            pixel = ((lanes + (m * LANES + 1)).astype(jnp.float32) / pixels) ** 2
            at = slice(m * LANES, (m + 1) * LANES)
            pixel_ref[0, rows, at], pixel_ref[1, rows, at] = sin_cos(column[rows] * pixel)


def contrast_of(line_ref, pixel_ref, i):
    sin_line, cos_line = line_ref[0, :, i : i + 1], line_ref[1, :, i : i + 1]
    return sin_line * pixel_ref[1, i : i + 1, :] + cos_line * pixel_ref[0, i : i + 1, :]


def copies(pairs, sems):
    started = [pltpu.make_async_copy(source, target, sems.at[n]) for n, (source, target) in enumerate(pairs)]
    for copy in started:
        copy.start()
    return started


def row_tables(shape, kinds, height, slab, tile, owner, place_ref, route_ref):
    far, wide, cores = shape
    devices, blocks = place_ref.shape
    rows, half = blocks * 2 * height, devices // 2
    me = lax.axis_index("slab")
    slot = lax.broadcasted_iota(jnp.int32, (devices, blocks), 0)
    block = lax.broadcasted_iota(jnp.int32, (devices, blocks), 1)
    within = slot & (half - 1)
    core = jnp.where(slot < half, cores - 1, 0)
    named = me ^ (((within & (far - 1)) * wide + within // far) * cores + core)
    place = jnp.full((devices, blocks), kinds * rows, jnp.int32)
    for r in range(slab.shape[0]):
        row = tile[r : r + 1, :] * rows + block * (2 * height)
        place = jnp.where(slab[r : r + 1, :] == named, row, place)
    place_ref[...] = place
    row = (tile * devices + (me ^ slab)) * height
    route = jnp.zeros(route_ref.shape, jnp.int32)
    for k in range(blocks):
        route = jnp.where(owner == k, row[:, k : k + 1], route)
    route_ref[...] = route


def sum_kernel(shape, kinds, slab_hbm, tile_hbm, block_hbm, owner_hbm, defocus_hbm, noise_hbm, tiles_hbm, images_hbm,
               sums_ref, wave_ref, tiles_ref, images_ref, noise_ref, place_ref, route_ref,
               slab_ref, tile_ref, block_ref, owner_ref, defocus_ref, line_ref, pixel_ref, acc_ref, sems):
    count = images_ref.shape[0]
    part = count // CHUNKS
    small = [(defocus_hbm, defocus_ref), (block_hbm, block_ref), (noise_hbm, noise_ref)]
    small += [(slab_hbm, slab_ref), (tile_hbm, tile_ref), (owner_hbm, owner_ref)]
    large = [(images_hbm.at[pl.ds(n * part, part)], images_ref.at[pl.ds(n * part, part)]) for n in range(CHUNKS)]
    started = copies(small + large, sems)
    last = pltpu.make_async_copy(tiles_hbm, tiles_ref, sems.at[len(started)])
    height, pixels = noise_ref.shape
    batches = block_ref.shape[0]
    size = count // batches
    acc_ref[...] = jnp.zeros_like(acc_ref)
    for copy in started[: len(small)]:
        copy.wait()
    tables(defocus_ref, height, pixels, line_ref, pixel_ref)
    row_tables(shape, kinds, height, slab_ref[...], tile_ref[...], owner_ref[...], place_ref, route_ref)
    for b in range(batches):
        if b % (batches // CHUNKS) == 0:
            started[len(small) + b // (batches // CHUNKS)].wait()
        if b == 0:
            last.start()
        data = jnp.zeros((height, pixels), jnp.float32)
        weight = jnp.zeros((height, pixels), jnp.float32)
        for j in range(size):
            i = b * size + j
            wave = contrast_of(line_ref, pixel_ref, i)
            wave_ref[i] = wave
            data = data + wave * images_ref[i].astype(jnp.float32)
            weight = weight + wave * wave
        k = block_ref[b]
        acc_ref[k, 0] = acc_ref[k, 0] + data
        acc_ref[k, 1] = acc_ref[k, 1] + weight
    sums = (acc_ref[...] * noise_ref[...][None, None]).astype(jnp.bfloat16)
    sums_ref[...] = sums.reshape(sums_ref.shape)
    last.wait()


def fill(ref, start, place_ref, parts_ref, mate_ref=None):
    sides, height, length = ref.shape[1:]

    def step(slot, carry):
        acc = None
        for k in range(place_ref.shape[1]):
            at = pl.multiple_of(place_ref[start + slot, k], sides * height)
            part = parts_ref[pl.ds(at, sides * height), :]
            acc = part if acc is None else acc + part
        acc = acc.reshape(sides, height, length)
        if mate_ref is not None:
            acc = acc + mate_ref[slot].astype(jnp.float32)
        ref[slot] = acc.astype(ref.dtype)
        return carry

    lax.fori_loop(0, ref.shape[0], step, 0)


def insert_kernel(place_vmem, sums_ref, tiles_ref, send_ref, far_ref, parts_ref, place_ref, sems):
    (started,) = copies([(place_vmem, place_ref)], sems)
    kinds = tiles_ref.shape[0]
    rows = sums_ref.shape[0]
    zeros = parts_ref.shape[0] - kinds * rows
    parts_ref[kinds * rows :, :] = jnp.zeros((zeros, parts_ref.shape[1]), jnp.float32)
    for t in range(kinds):
        parts_ref[t * rows : (t + 1) * rows, :] = lax.dot_general(
            sums_ref[...], tiles_ref[t], (((1,), (1,)), ((), ())), preferred_element_type=jnp.float32
        )
    started.wait()
    fill(send_ref, 0, place_ref, parts_ref)
    devices = place_ref.shape[0]
    fill(far_ref, devices - far_ref.shape[0], place_ref, parts_ref)


def near_kernel(place_vmem, parts_ref, mate_ref, near_ref, place_ref, sems):
    (started,) = copies([(place_vmem, place_ref)], sems)
    started.wait()
    fill(near_ref, place_ref.shape[0] // 2, place_ref, parts_ref, mate_ref)


def project_kernel(places, route_vmem, tiles_ref, *refs):
    columns, refs = refs[: len(places)], refs[len(places) :]
    proj_ref, route_ref, lines_ref, flat_ref, sems = refs
    (started,) = copies([(route_vmem, route_ref)], sems)
    crossed, batches = route_ref.shape
    kinds = tiles_ref.shape[0]
    height = columns[0].shape[1]
    rows = lines_ref.shape[0]
    dense = rows // height * kinds <= crossed * batches
    for ref, aways in zip(columns, places):
        for n, away in enumerate(aways):
            lines_ref[away * height : (away + 1) * height, :] = ref[n]
    if dense:
        for t in range(kinds):
            flat_ref[t * rows : (t + 1) * rows, :] = jnp.dot(lines_ref[...], tiles_ref[t], preferred_element_type=jnp.float32)
    started.wait()

    def project(b, carry):
        acc = None
        for r in range(crossed):
            at = route_ref[r, b]
            if dense:
                part = flat_ref[pl.ds(pl.multiple_of(at, height), height), :]
            else:
                t, at = at // rows, pl.multiple_of(lax.rem(at, rows), height)
                part = jnp.dot(lines_ref[pl.ds(at, height), :], tiles_ref[t], preferred_element_type=jnp.float32)
            acc = part if acc is None else acc + part
        proj_ref[b] = acc
        return carry

    lax.fori_loop(0, batches, project, 0, unroll=dense)


def score_kernel(noise_ref, proj_ref, wave_ref, images_ref, score_ref, part_ref):
    height, pixels = noise_ref.shape
    count = images_ref.shape[0]
    size = count // proj_ref.shape[0]
    noise = noise_ref[...]
    for b in range(count // size):
        proj = proj_ref[b]
        for j in range(size):
            i = b * size + j
            residual = images_ref[i].astype(jnp.float32) - wave_ref[i] * proj
            power = residual * residual * noise
            power = sum(power[n * 8 : (n + 1) * 8] for n in range(height // 8))
            part_ref[i * 8 : (i + 1) * 8, :] = sum(power[:, n * LANES : (n + 1) * LANES] for n in range(pixels // LANES))
    total = sum(part_ref[pl.ds(n, count, 8), :] for n in range(8))
    total = jnp.sum(jnp.transpose(total), axis=0, keepdims=True)
    score_ref[...] = total * (1.0 / (height * pixels))


def on_device(volume, tiles, slab_ids, tile_ids, batch_block, images, defocus, inv_sigma2):
    blocks, crossed = slab_ids.shape
    height, length = volume.shape[1:]
    count, _, pixels = images.shape
    kinds = tiles.shape[0]
    devices = lax.axis_size("slab")
    shape = far, wide, cores = grid_of(devices)
    half = devices // 2
    rows = blocks * 2 * height
    slabs, kind_rows, row = slab_ids.T, tile_ids.T, defocus.reshape(1, count)

    def swap(array, offset):
        return lax.ppermute(array, "slab", [(i, i ^ offset) for i in range(devices)])

    vmem = pl.BlockSpec(memory_space=pltpu.VMEM)
    hbm = pl.BlockSpec(memory_space=pltpu.HBM)
    params = pltpu.CompilerParams(vmem_limit_bytes=VMEM_BYTES)
    f32, bf16 = jnp.float32, jnp.bfloat16
    i32 = jnp.int32

    def call(kernel, outs, inputs, operands, scratch, flops, moved, name):
        operands = [
            pltpu.with_memory_space_constraint(x, pltpu.HBM) if spec is hbm else x for x, spec in zip(operands, inputs)
        ]
        return pl.pallas_call(
            kernel,
            out_shape=tuple(jax.ShapeDtypeStruct(s, t) for s, t in outs),
            in_specs=inputs,
            out_specs=(vmem,) * len(outs),
            scratch_shapes=scratch,
            compiler_params=params,
            cost_estimate=pl.CostEstimate(flops=flops, bytes_accessed=moved, transcendentals=0),
            name=name,
        )(*operands)

    def hop(array, offset):
        return jnp.concatenate([array, swap(array, offset)], axis=0)

    along_z = [z * wide * cores for z in reversed(powers(far))]
    offsets = along_z[:1] + [x * cores for x in powers(wide)] + along_z[1:]
    away = [0]
    for offset in offsets[:-1]:
        away += [a ^ offset for a in away]
    gathered = hop(volume, offsets[0])

    batches = batch_block.shape[0]
    sums, wave, tiles_near, images_near, noise_near, place_rows, route_rows = call(
        functools.partial(sum_kernel, shape, kinds),
        [
            ((rows, pixels), bf16),
            (images.shape, f32),
            (tiles.shape, bf16),
            (images.shape, bf16),
            (inv_sigma2.shape, f32),
            ((devices, blocks), i32),
            ((crossed, batches), i32),
        ],
        [hbm] * 8,
        (slabs, kind_rows, batch_block, batch_block.reshape(1, batches), row, inv_sigma2, tiles, images),
        [
            pltpu.VMEM((crossed, blocks), i32),
            pltpu.VMEM((crossed, blocks), i32),
            pltpu.SMEM((batches,), i32),
            pltpu.VMEM((1, batches), i32),
            pltpu.VMEM((1, count), f32),
            pltpu.VMEM((2, height, count), f32),
            pltpu.VMEM((2, count, pixels), f32),
            pltpu.VMEM((blocks, 2, height, pixels), f32),
            pltpu.SemaphoreType.DMA((CHUNKS + 7,)),
        ],
        0,
        10 << 20,
        "sums",
    )

    place = (2, height, length)
    place_scratch = [pltpu.SMEM((devices, blocks), i32), pltpu.SemaphoreType.DMA((1,))]
    send, keep, parts = call(
        insert_kernel,
        [((half, *place), bf16), ((half - far, *place), f32), ((kinds * rows + 2 * height, length), f32)],
        [vmem] * 3,
        (place_rows, sums, tiles_near),
        place_scratch,
        2 * rows * pixels * kinds * length,
        8 << 20,
        "insert",
    )
    send, gathered = lax.optimization_barrier((send, gathered))
    mate = swap(send, 1)
    def along_x(start, stop):
        return (keep[start:stop] + mate[far + start : far + stop].astype(f32)).astype(bf16)

    cut = max(1, far // 2)
    main = [along_x(x * far + cut, (x + 1) * far) for x in range(wide - 1)]
    later = [along_x(x * far, x * far + cut) for x in range(wide - 1)]
    (near,) = call(
        near_kernel, [((far, *place), f32)], [vmem] * 3, (place_rows, parts, mate), place_scratch, 0, 0, "near"
    )
    for offset in offsets[1:-1]:
        came, _ = lax.optimization_barrier((swap(gathered, offset), near))
        gathered = jnp.concatenate([gathered, came], axis=0)
    mine = [near[z] for z in range(far)]
    for x in range(1, wide):
        came = swap(main[x - 1], x * cores)
        for z in range(cut, far):
            mine[z] = mine[z] + came[z - cut].astype(f32)
    outgoing = {z: mine[z].astype(bf16) for z in range(cut, far)}
    for x in range(1, wide):
        came, _ = lax.optimization_barrier((swap(later[x - 1], x * cores), outgoing[far - 1]))
        for z in range(cut):
            mine[z] = mine[z] + came[z].astype(f32)
    outgoing.update({z: mine[z].astype(bf16) for z in range(1, cut)})
    total = mine[0]

    held, _ = lax.optimization_barrier((gathered, later[0]))
    columns = [gathered, swap(held, offsets[-1])]
    columns += [swap(column, 1) for column in columns]
    _, *columns = lax.optimization_barrier((outgoing[1], *columns))
    places = [[a ^ last for a in away] for last in (0, offsets[-1], 1, offsets[-1] ^ 1)]
    if devices * kinds <= batches * crossed:
        flat = pltpu.VMEM((kinds * devices * height, pixels), f32)
    else:
        flat = pltpu.VMEM((8, LANES), f32)
    (proj,) = call(
        functools.partial(project_kernel, places),
        [((batches, height, pixels), f32)],
        [vmem] * (2 + len(columns)),
        (route_rows, tiles_near, *columns),
        [pltpu.SMEM((crossed, batches), i32), pltpu.VMEM((devices * height, length), bf16), flat, pltpu.SemaphoreType.DMA((1,))],
        0,
        0,
        "project",
    )

    (scores,) = call(
        score_kernel,
        [((1, count), f32)],
        [vmem] * 4,
        (noise_near, proj, wave, images_near),
        [pltpu.VMEM((count * 8, LANES), f32)],
        0,
        0,
        "scores",
    )
    for z in range(1, far):
        came = swap(outgoing[z], z * wide * cores)
        if z >= cut:
            came, scores = lax.optimization_barrier((came, scores))
        total = total + came.astype(f32)
    return scores.reshape(count), total[0:1], total[1:2]


def solution(mesh):
    placed = (
        P(("parts", "slab"), None, None),
        P(),
        P(("parts", "slab"), None),
        P(("parts", "slab"), None),
        P(("parts", "slab")),
        P(("parts", "slab"), None, None),
        P(("parts", "slab")),
        P("parts", None),
    )
    return jax.shard_map(
        on_device,
        mesh=mesh,
        in_specs=placed,
        out_specs=(
            P(("parts", "slab")),
            P(("parts", "slab"), None, None),
            P(("parts", "slab"), None, None),
        ),
        check_vma=False,
    )
```

```python
import functools

import jax
import jax.numpy as jnp
from jax import lax
from jax.experimental import pallas as pl
from jax.experimental.pallas import tpu as pltpu
from jax.sharding import PartitionSpec as P

LANES = 128
CHUNKS = 4
VMEM_BYTES = 24 * 1024 * 1024


def grid_of(devices):
    cores = 2 if devices % 2 == 0 else 1
    chips = devices // cores
    wide = 1
    while (2 * wide) ** 3 <= chips:
        wide *= 2
    return chips // wide, wide, cores


def powers(size):
    return [1 << n for n in range(size.bit_length() - 1)]


def sin_cos(angle):
    turns = jnp.floor(angle * 0.3183098861837907 + 0.5)
    rest = angle - turns * 3.140625
    rest = rest - turns * 9.675025939941406e-4
    rest = rest - turns * 1.5099580252808664e-7
    half = turns * 0.5
    sign = 1.0 - 4.0 * (half - jnp.floor(half))
    sq = rest * rest
    sin = rest * (1.0 + sq * (-1.0 / 6 + sq * (1.0 / 120 + sq * (-1.0 / 5040 + sq * (1.0 / 362880 + sq * (-1.0 / 39916800))))))
    cos = 1.0 + sq * (-0.5 + sq * (1.0 / 24 + sq * (-1.0 / 720 + sq * (1.0 / 40320 + sq * (-1.0 / 3628800 + sq * (1.0 / 479001600))))))
    return sign * sin, sign * cos


def tables(defocus_ref, height, pixels, line_ref, pixel_ref):
    images = defocus_ref.shape[1]
    defocus = defocus_ref[...]
    rows = lax.broadcasted_iota(jnp.int32, (height, images), 0)
    line = ((rows // 2 + 1).astype(jnp.float32) / (height // 2)) ** 2
    line_ref[0], line_ref[1] = sin_cos(defocus * line + 0.3)
    column = jnp.transpose(jnp.broadcast_to(defocus, (LANES, images)))
    part = 32
    lanes = lax.broadcasted_iota(jnp.int32, (part, LANES), 1)
    for n in range(images // part):
        rows = slice(n * part, (n + 1) * part)
        for m in range(pixels // LANES):
            pixel = ((lanes + (m * LANES + 1)).astype(jnp.float32) / pixels) ** 2
            at = slice(m * LANES, (m + 1) * LANES)
            pixel_ref[0, rows, at], pixel_ref[1, rows, at] = sin_cos(column[rows] * pixel)


def contrast_of(line_ref, pixel_ref, i):
    sin_line, cos_line = line_ref[0, :, i : i + 1], line_ref[1, :, i : i + 1]
    return sin_line * pixel_ref[1, i : i + 1, :] + cos_line * pixel_ref[0, i : i + 1, :]


def copies(pairs, sems):
    started = [pltpu.make_async_copy(source, target, sems.at[n]) for n, (source, target) in enumerate(pairs)]
    for copy in started:
        copy.start()
    return started


def row_tables(shape, kinds, height, bit, slab, tile, owner, place_ref, *route_refs):
    far, wide, cores = shape
    devices, blocks = place_ref.shape
    rows, half = blocks * 2 * height, devices // 2
    me = lax.axis_index("slab")
    slot = lax.broadcasted_iota(jnp.int32, (devices, blocks), 0)
    block = lax.broadcasted_iota(jnp.int32, (devices, blocks), 1)
    within = slot & (half - 1)
    core = jnp.where(slot < half, cores - 1, 0)
    named = me ^ (((within & (far - 1)) * wide + within // far) * cores + core)
    place = jnp.full((devices, blocks), kinds * rows, jnp.int32)
    for r in range(slab.shape[0]):
        row = tile[r : r + 1, :] * rows + block * (2 * height)
        place = jnp.where(slab[r : r + 1, :] == named, row, place)
    place_ref[...] = place
    away = me ^ slab
    row = (tile * half + (away & (bit - 1)) + away // (2 * bit) * bit) * height
    for side, route_ref in enumerate(route_refs):
        named = jnp.where((away // bit) & 1 == side, row, kinds * half * height)
        route = jnp.zeros(route_ref.shape, jnp.int32)
        for k in range(blocks):
            route = jnp.where(owner == k, named[:, k : k + 1], route)
        route_ref[...] = route


def sum_kernel(shape, kinds, bit, slab_hbm, tile_hbm, block_hbm, owner_hbm, defocus_hbm, noise_hbm, tiles_hbm, images_hbm,
               sums_ref, wave_ref, tiles_ref, images_ref, noise_ref, place_ref, first_ref, second_ref,
               slab_ref, tile_ref, block_ref, owner_ref, defocus_ref, line_ref, pixel_ref, acc_ref, sems):
    count = images_ref.shape[0]
    part = count // CHUNKS
    small = [(defocus_hbm, defocus_ref), (block_hbm, block_ref), (noise_hbm, noise_ref)]
    small += [(slab_hbm, slab_ref), (tile_hbm, tile_ref), (owner_hbm, owner_ref)]
    large = [(images_hbm.at[pl.ds(n * part, part)], images_ref.at[pl.ds(n * part, part)]) for n in range(CHUNKS)]
    started = copies(small + large, sems)
    last = pltpu.make_async_copy(tiles_hbm, tiles_ref, sems.at[len(started)])
    height, pixels = noise_ref.shape
    batches = block_ref.shape[0]
    size = count // batches
    acc_ref[...] = jnp.zeros_like(acc_ref)
    for copy in started[: len(small)]:
        copy.wait()
    tables(defocus_ref, height, pixels, line_ref, pixel_ref)
    row_tables(shape, kinds, height, bit, slab_ref[...], tile_ref[...], owner_ref[...], place_ref, first_ref, second_ref)
    for b in range(batches):
        if b % (batches // CHUNKS) == 0:
            started[len(small) + b // (batches // CHUNKS)].wait()
        if b == 0:
            last.start()
        data = jnp.zeros((height, pixels), jnp.float32)
        weight = jnp.zeros((height, pixels), jnp.float32)
        for j in range(size):
            i = b * size + j
            wave = contrast_of(line_ref, pixel_ref, i)
            wave_ref[i] = wave
            data = data + wave * images_ref[i].astype(jnp.float32)
            weight = weight + wave * wave
        k = block_ref[b]
        acc_ref[k, 0] = acc_ref[k, 0] + data
        acc_ref[k, 1] = acc_ref[k, 1] + weight
    sums = (acc_ref[...] * noise_ref[...][None, None]).astype(jnp.bfloat16)
    sums_ref[...] = sums.reshape(sums_ref.shape)
    last.wait()


def fill(ref, start, place_ref, parts_ref, mate_ref=None):
    sides, height, length = ref.shape[1:]

    def step(slot, carry):
        acc = None
        for k in range(place_ref.shape[1]):
            at = pl.multiple_of(place_ref[start + slot, k], sides * height)
            part = parts_ref[pl.ds(at, sides * height), :]
            acc = part if acc is None else acc + part
        acc = acc.reshape(sides, height, length)
        if mate_ref is not None:
            acc = acc + mate_ref[slot].astype(jnp.float32)
        ref[slot] = acc.astype(ref.dtype)
        return carry

    lax.fori_loop(0, ref.shape[0], step, 0)


def insert_kernel(place_vmem, sums_ref, tiles_ref, send_ref, far_ref, parts_ref, place_ref, sems):
    (started,) = copies([(place_vmem, place_ref)], sems)
    kinds = tiles_ref.shape[0]
    rows = sums_ref.shape[0]
    zeros = parts_ref.shape[0] - kinds * rows
    parts_ref[kinds * rows :, :] = jnp.zeros((zeros, parts_ref.shape[1]), jnp.float32)
    for t in range(kinds):
        parts_ref[t * rows : (t + 1) * rows, :] = lax.dot_general(
            sums_ref[...], tiles_ref[t], (((1,), (1,)), ((), ())), preferred_element_type=jnp.float32
        )
    started.wait()
    fill(send_ref, 0, place_ref, parts_ref)
    devices = place_ref.shape[0]
    fill(far_ref, devices - far_ref.shape[0], place_ref, parts_ref)


def near_kernel(place_vmem, parts_ref, mate_ref, near_ref, place_ref, sems):
    (started,) = copies([(place_vmem, place_ref)], sems)
    started.wait()
    fill(near_ref, place_ref.shape[0] // 2, place_ref, parts_ref, mate_ref)


def project_kernel(places, route_vmem, tiles_ref, *refs):
    columns, refs = refs[: len(places)], refs[len(places) :]
    *base, proj_ref, route_ref, lines_ref, flat_ref, sems = refs
    (started,) = copies([(route_vmem, route_ref)], sems)
    crossed, batches = route_ref.shape
    kinds = tiles_ref.shape[0]
    height = columns[0].shape[1]
    rows = lines_ref.shape[0]
    dense = flat_ref.shape[0] > kinds * rows
    for ref, slots in zip(columns, places):
        for n, slot in enumerate(slots):
            lines_ref[slot * height : (slot + 1) * height, :] = ref[n]
    if dense:
        for t in range(kinds):
            flat_ref[t * rows : (t + 1) * rows, :] = jnp.dot(lines_ref[...], tiles_ref[t], preferred_element_type=jnp.float32)
        flat_ref[kinds * rows :, :] = jnp.zeros((height, flat_ref.shape[1]), jnp.float32)
    started.wait()

    def project(b, carry):
        acc = base[0][b] if base else None
        for r in range(crossed):
            at = route_ref[r, b]
            if dense:
                part = flat_ref[pl.ds(pl.multiple_of(at, height), height), :]
            else:
                t, from_row = jnp.minimum(at // rows, kinds - 1), pl.multiple_of(lax.rem(at, rows), height)
                part = jnp.dot(lines_ref[pl.ds(from_row, height), :], tiles_ref[t], preferred_element_type=jnp.float32)
                part = part * jnp.where(at < kinds * rows, 1.0, 0.0)
            acc = part if acc is None else acc + part
        proj_ref[b] = acc
        return carry

    lax.fori_loop(0, batches, project, 0, unroll=dense)


def score_kernel(noise_ref, proj_ref, wave_ref, images_ref, score_ref, part_ref):
    height, pixels = noise_ref.shape
    count = images_ref.shape[0]
    size = count // proj_ref.shape[0]
    noise = noise_ref[...]
    for b in range(count // size):
        proj = proj_ref[b]
        for j in range(size):
            i = b * size + j
            residual = images_ref[i].astype(jnp.float32) - wave_ref[i] * proj
            power = residual * residual * noise
            power = sum(power[n * 8 : (n + 1) * 8] for n in range(height // 8))
            part_ref[i * 8 : (i + 1) * 8, :] = sum(power[:, n * LANES : (n + 1) * LANES] for n in range(pixels // LANES))
    total = sum(part_ref[pl.ds(n, count, 8), :] for n in range(8))
    total = jnp.sum(jnp.transpose(total), axis=0, keepdims=True)
    score_ref[...] = total * (1.0 / (height * pixels))


def on_device(volume, tiles, slab_ids, tile_ids, batch_block, images, defocus, inv_sigma2):
    blocks, crossed = slab_ids.shape
    height, length = volume.shape[1:]
    count, _, pixels = images.shape
    kinds = tiles.shape[0]
    devices = lax.axis_size("slab")
    shape = far, wide, cores = grid_of(devices)
    half = devices // 2
    rows = blocks * 2 * height
    slabs, kind_rows, row = slab_ids.T, tile_ids.T, defocus.reshape(1, count)

    def swap(array, offset):
        return lax.ppermute(array, "slab", [(i, i ^ offset) for i in range(devices)])

    vmem = pl.BlockSpec(memory_space=pltpu.VMEM)
    hbm = pl.BlockSpec(memory_space=pltpu.HBM)
    params = pltpu.CompilerParams(vmem_limit_bytes=VMEM_BYTES)
    f32, bf16 = jnp.float32, jnp.bfloat16
    i32 = jnp.int32

    def call(kernel, outs, inputs, operands, scratch, flops, moved, name):
        operands = [
            pltpu.with_memory_space_constraint(x, pltpu.HBM) if spec is hbm else x for x, spec in zip(operands, inputs)
        ]
        return pl.pallas_call(
            kernel,
            out_shape=tuple(jax.ShapeDtypeStruct(s, t) for s, t in outs),
            in_specs=inputs,
            out_specs=(vmem,) * len(outs),
            scratch_shapes=scratch,
            compiler_params=params,
            cost_estimate=pl.CostEstimate(flops=flops, bytes_accessed=moved, transcendentals=0),
            name=name,
        )(*operands)

    def hop(array, offset):
        return jnp.concatenate([array, swap(array, offset)], axis=0)

    along_z = [z * wide * cores for z in reversed(powers(far))]
    offsets = along_z[:1] + [x * cores for x in powers(wide)] + along_z[1:]
    away = [0]
    for offset in offsets[:-1]:
        away += [a ^ offset for a in away]
    gathered = hop(volume, offsets[0])

    batches = batch_block.shape[0]
    sums, wave, tiles_near, images_near, noise_near, place_rows, *route_rows = call(
        functools.partial(sum_kernel, shape, kinds, offsets[-1]),
        [
            ((rows, pixels), bf16),
            (images.shape, f32),
            (tiles.shape, bf16),
            (images.shape, bf16),
            (inv_sigma2.shape, f32),
            ((devices, blocks), i32),
            ((crossed, batches), i32),
            ((crossed, batches), i32),
        ],
        [hbm] * 8,
        (slabs, kind_rows, batch_block, batch_block.reshape(1, batches), row, inv_sigma2, tiles, images),
        [
            pltpu.VMEM((crossed, blocks), i32),
            pltpu.VMEM((crossed, blocks), i32),
            pltpu.SMEM((batches,), i32),
            pltpu.VMEM((1, batches), i32),
            pltpu.VMEM((1, count), f32),
            pltpu.VMEM((2, height, count), f32),
            pltpu.VMEM((2, count, pixels), f32),
            pltpu.VMEM((blocks, 2, height, pixels), f32),
            pltpu.SemaphoreType.DMA((CHUNKS + 7,)),
        ],
        0,
        10 << 20,
        "sums",
    )

    place = (2, height, length)
    place_scratch = [pltpu.SMEM((devices, blocks), i32), pltpu.SemaphoreType.DMA((1,))]
    send, keep, parts = call(
        insert_kernel,
        [((half, *place), bf16), ((half - far, *place), f32), ((kinds * rows + 2 * height, length), f32)],
        [vmem] * 3,
        (place_rows, sums, tiles_near),
        place_scratch,
        2 * rows * pixels * kinds * length,
        8 << 20,
        "insert",
    )
    send, gathered = lax.optimization_barrier((send, gathered))
    mate = swap(send, 1)
    def along_x(start, stop):
        return (keep[start:stop] + mate[far + start : far + stop].astype(f32)).astype(bf16)

    cut = max(1, far // 2)
    main = [along_x(x * far + cut, (x + 1) * far) for x in range(wide - 1)]
    later = [along_x(x * far, x * far + cut) for x in range(wide - 1)]
    (near,) = call(
        near_kernel, [((far, *place), f32)], [vmem] * 3, (place_rows, parts, mate), place_scratch, 0, 0, "near"
    )
    for offset in offsets[1:-1]:
        came, _ = lax.optimization_barrier((swap(gathered, offset), near))
        gathered = jnp.concatenate([gathered, came], axis=0)
    bit = offsets[-1]
    places = [[(a & (bit - 1)) + a // (2 * bit) * bit for a in [b ^ core for b in away]] for core in (0, 1)]
    flat_rows = kinds * half * height + height if devices * kinds <= batches * crossed else 8
    flat_columns = pixels if flat_rows > 8 else LANES

    def project(route, columns, *base):
        (proj,) = call(
            functools.partial(project_kernel, places),
            [((batches, height, pixels), f32)],
            [vmem] * (4 + len(base)),
            (route, tiles_near, *columns, *base),
            [
                pltpu.SMEM((crossed, batches), i32),
                pltpu.VMEM((half * height, length), bf16),
                pltpu.VMEM((flat_rows, flat_columns), f32),
                pltpu.SemaphoreType.DMA((1,)),
            ],
            0,
            0,
            "project",
        )
        return proj

    proj = project(route_rows[0], (gathered, swap(gathered, 1)))
    mine = [near[z] for z in range(far)]
    for x in range(1, wide):
        came = swap(main[x - 1], x * cores)
        for z in range(cut, far):
            mine[z] = mine[z] + came[z - cut].astype(f32)
    outgoing = {z: mine[z].astype(bf16) for z in range(cut, far)}
    for x in range(1, wide):
        came, _, _ = lax.optimization_barrier((swap(later[x - 1], x * cores), outgoing[far - 1], proj))
        for z in range(cut):
            mine[z] = mine[z] + came[z].astype(f32)
    outgoing.update({z: mine[z].astype(bf16) for z in range(1, cut)})
    total = mine[0]

    held, _ = lax.optimization_barrier((gathered, later[0]))
    column = swap(held, bit)
    _, column, mirror = lax.optimization_barrier((outgoing[1], column, swap(column, 1)))
    proj = project(route_rows[1], (column, mirror), proj)
    (scores,) = call(
        score_kernel,
        [((1, count), f32)],
        [vmem] * 4,
        (noise_near, proj, wave, images_near),
        [pltpu.VMEM((count * 8, LANES), f32)],
        0,
        0,
        "scores",
    )
    for z in range(1, far):
        came = swap(outgoing[z], z * wide * cores)
        if z >= cut:
            came, scores = lax.optimization_barrier((came, scores))
        total = total + came.astype(f32)
    return scores.reshape(count), total[0:1], total[1:2]


def solution(mesh):
    placed = (
        P(("parts", "slab"), None, None),
        P(),
        P(("parts", "slab"), None),
        P(("parts", "slab"), None),
        P(("parts", "slab")),
        P(("parts", "slab"), None, None),
        P(("parts", "slab")),
        P("parts", None),
    )
    return jax.shard_map(
        on_device,
        mesh=mesh,
        in_specs=placed,
        out_specs=(
            P(("parts", "slab")),
            P(("parts", "slab"), None, None),
            P(("parts", "slab"), None, None),
        ),
        check_vma=False,
    )
```

```python
import functools

import jax
import jax.numpy as jnp
from jax import lax
from jax.experimental import pallas as pl
from jax.experimental.pallas import tpu as pltpu
from jax.sharding import PartitionSpec as P

LANES = 128
CHUNKS = 4
VMEM_BYTES = 24 * 1024 * 1024


def grid_of(devices):
    cores = 2 if devices % 2 == 0 else 1
    chips = devices // cores
    wide = 1
    while (2 * wide) ** 3 <= chips:
        wide *= 2
    return chips // wide, wide, cores


def powers(size):
    return [1 << n for n in range(size.bit_length() - 1)]


def sin_cos(angle):
    turns = jnp.floor(angle * 0.3183098861837907 + 0.5)
    rest = angle - turns * 3.140625
    rest = rest - turns * 9.675025939941406e-4
    rest = rest - turns * 1.5099580252808664e-7
    half = turns * 0.5
    sign = 1.0 - 4.0 * (half - jnp.floor(half))
    sq = rest * rest
    sin = rest * (1.0 + sq * (-1.0 / 6 + sq * (1.0 / 120 + sq * (-1.0 / 5040 + sq * (1.0 / 362880 + sq * (-1.0 / 39916800))))))
    cos = 1.0 + sq * (-0.5 + sq * (1.0 / 24 + sq * (-1.0 / 720 + sq * (1.0 / 40320 + sq * (-1.0 / 3628800 + sq * (1.0 / 479001600))))))
    return sign * sin, sign * cos


def tables(defocus_ref, height, pixels, line_ref, pixel_ref):
    images = defocus_ref.shape[1]
    defocus = defocus_ref[...]
    rows = lax.broadcasted_iota(jnp.int32, (height, images), 0)
    line = ((rows // 2 + 1).astype(jnp.float32) / (height // 2)) ** 2
    line_ref[0], line_ref[1] = sin_cos(defocus * line + 0.3)
    column = jnp.transpose(jnp.broadcast_to(defocus, (LANES, images)))
    part = 32
    lanes = lax.broadcasted_iota(jnp.int32, (part, LANES), 1)
    for n in range(images // part):
        rows = slice(n * part, (n + 1) * part)
        for m in range(pixels // LANES):
            pixel = ((lanes + (m * LANES + 1)).astype(jnp.float32) / pixels) ** 2
            at = slice(m * LANES, (m + 1) * LANES)
            pixel_ref[0, rows, at], pixel_ref[1, rows, at] = sin_cos(column[rows] * pixel)


def contrast_of(line_ref, pixel_ref, i):
    sin_line, cos_line = line_ref[0, :, i : i + 1], line_ref[1, :, i : i + 1]
    return sin_line * pixel_ref[1, i : i + 1, :] + cos_line * pixel_ref[0, i : i + 1, :]


def copies(pairs, sems):
    started = [pltpu.make_async_copy(source, target, sems.at[n]) for n, (source, target) in enumerate(pairs)]
    for copy in started:
        copy.start()
    return started


def row_tables(shape, kinds, height, bit, slab, tile, owner, place_ref, *route_refs):
    far, wide, cores = shape
    devices, blocks = place_ref.shape
    rows, half = blocks * 2 * height, devices // 2
    me = lax.axis_index("slab")
    slot = lax.broadcasted_iota(jnp.int32, (devices, blocks), 0)
    block = lax.broadcasted_iota(jnp.int32, (devices, blocks), 1)
    within = slot & (half - 1)
    core = jnp.where(slot < half, cores - 1, 0)
    named = me ^ (((within & (far - 1)) * wide + within // far) * cores + core)
    place = jnp.full((devices, blocks), kinds * rows, jnp.int32)
    for r in range(slab.shape[0]):
        row = tile[r : r + 1, :] * rows + block * (2 * height)
        place = jnp.where(slab[r : r + 1, :] == named, row, place)
    place_ref[...] = place
    away = me ^ slab
    row = (tile * half + (away & (bit - 1)) + away // (2 * bit) * bit) * height
    for side, route_ref in enumerate(route_refs):
        named = jnp.where((away // bit) & 1 == side, row, kinds * half * height)
        route = jnp.zeros(route_ref.shape, jnp.int32)
        for k in range(blocks):
            route = jnp.where(owner == k, named[:, k : k + 1], route)
        route_ref[...] = route


def sum_kernel(shape, kinds, bit, slab_hbm, tile_hbm, block_hbm, owner_hbm, defocus_hbm, noise_hbm, images_hbm,
               sums_ref, wave_ref, images_ref, noise_ref, place_ref, first_ref, second_ref,
               slab_ref, tile_ref, block_ref, owner_ref, defocus_ref, line_ref, pixel_ref, acc_ref, sems):
    count = images_ref.shape[0]
    part = count // CHUNKS
    small = [(defocus_hbm, defocus_ref), (block_hbm, block_ref), (noise_hbm, noise_ref)]
    small += [(slab_hbm, slab_ref), (tile_hbm, tile_ref), (owner_hbm, owner_ref)]
    large = [(images_hbm.at[pl.ds(n * part, part)], images_ref.at[pl.ds(n * part, part)]) for n in range(CHUNKS)]
    started = copies(small + large, sems)
    height, pixels = noise_ref.shape
    batches = block_ref.shape[0]
    size = count // batches
    acc_ref[...] = jnp.zeros_like(acc_ref)
    started[0].wait()
    tables(defocus_ref, height, pixels, line_ref, pixel_ref)
    for copy in started[1 : len(small)]:
        copy.wait()
    row_tables(shape, kinds, height, bit, slab_ref[...], tile_ref[...], owner_ref[...], place_ref, first_ref, second_ref)
    for b in range(batches):
        if b % (batches // CHUNKS) == 0:
            started[len(small) + b // (batches // CHUNKS)].wait()
        data = jnp.zeros((height, pixels), jnp.float32)
        weight = jnp.zeros((height, pixels), jnp.float32)
        for j in range(size):
            i = b * size + j
            wave = contrast_of(line_ref, pixel_ref, i)
            wave_ref[i] = wave
            data = data + wave * images_ref[i].astype(jnp.float32)
            weight = weight + wave * wave
        k = block_ref[b]
        acc_ref[k, 0] = acc_ref[k, 0] + data
        acc_ref[k, 1] = acc_ref[k, 1] + weight
    sums = (acc_ref[...] * noise_ref[...][None, None]).astype(jnp.bfloat16)
    sums_ref[...] = sums.reshape(sums_ref.shape)


def fill(ref, start, place_ref, parts_ref, mate_ref=None):
    sides, height, length = ref.shape[1:]

    def step(slot, carry):
        acc = None
        for k in range(place_ref.shape[1]):
            at = pl.multiple_of(place_ref[start + slot, k], sides * height)
            part = parts_ref[pl.ds(at, sides * height), :]
            acc = part if acc is None else acc + part
        acc = acc.reshape(sides, height, length)
        if mate_ref is not None:
            acc = acc + mate_ref[slot].astype(jnp.float32)
        ref[slot] = acc.astype(ref.dtype)
        return carry

    lax.fori_loop(0, ref.shape[0], step, 0)


def insert_kernel(place_vmem, sums_ref, tiles_ref, send_ref, far_ref, parts_ref, place_ref, sems):
    (started,) = copies([(place_vmem, place_ref)], sems)
    kinds = tiles_ref.shape[0]
    rows = sums_ref.shape[0]
    zeros = parts_ref.shape[0] - kinds * rows
    parts_ref[kinds * rows :, :] = jnp.zeros((zeros, parts_ref.shape[1]), jnp.float32)
    for t in range(kinds):
        parts_ref[t * rows : (t + 1) * rows, :] = lax.dot_general(
            sums_ref[...], tiles_ref[t], (((1,), (1,)), ((), ())), preferred_element_type=jnp.float32
        )
    started.wait()
    fill(send_ref, 0, place_ref, parts_ref)
    devices = place_ref.shape[0]
    fill(far_ref, devices - far_ref.shape[0], place_ref, parts_ref)


def near_kernel(place_vmem, parts_ref, mate_ref, near_ref, place_ref, sems):
    (started,) = copies([(place_vmem, place_ref)], sems)
    started.wait()
    fill(near_ref, place_ref.shape[0] // 2, place_ref, parts_ref, mate_ref)


def project_kernel(places, route_vmem, tiles_ref, *refs):
    columns, refs = refs[: len(places)], refs[len(places) :]
    *base, proj_ref, route_ref, lines_ref, flat_ref, sems = refs
    (started,) = copies([(route_vmem, route_ref)], sems)
    crossed, batches = route_ref.shape
    kinds = tiles_ref.shape[0]
    height = columns[0].shape[1]
    rows = lines_ref.shape[0]
    dense = flat_ref.shape[0] > kinds * rows
    for ref, slots in zip(columns, places):
        for n, slot in enumerate(slots):
            lines_ref[slot * height : (slot + 1) * height, :] = ref[n]
    if dense:
        for t in range(kinds):
            flat_ref[t * rows : (t + 1) * rows, :] = jnp.dot(lines_ref[...], tiles_ref[t], preferred_element_type=jnp.float32)
        flat_ref[kinds * rows :, :] = jnp.zeros((height, flat_ref.shape[1]), jnp.float32)
    started.wait()

    def project(b, carry):
        acc = base[0][b] if base else None
        for r in range(crossed):
            at = route_ref[r, b]
            if dense:
                part = flat_ref[pl.ds(pl.multiple_of(at, height), height), :]
            else:
                t, from_row = jnp.minimum(at // rows, kinds - 1), pl.multiple_of(lax.rem(at, rows), height)
                part = jnp.dot(lines_ref[pl.ds(from_row, height), :], tiles_ref[t], preferred_element_type=jnp.float32)
                part = part * jnp.where(at < kinds * rows, 1.0, 0.0)
            acc = part if acc is None else acc + part
        proj_ref[b] = acc
        return carry

    lax.fori_loop(0, batches, project, 0, unroll=dense)


def score_kernel(noise_ref, proj_ref, wave_ref, images_ref, score_ref, part_ref):
    height, pixels = noise_ref.shape
    count = images_ref.shape[0]
    size = count // proj_ref.shape[0]
    noise = noise_ref[...]
    for b in range(count // size):
        proj = proj_ref[b]
        for j in range(size):
            i = b * size + j
            residual = images_ref[i].astype(jnp.float32) - wave_ref[i] * proj
            power = residual * residual * noise
            power = sum(power[n * 8 : (n + 1) * 8] for n in range(height // 8))
            part_ref[i * 8 : (i + 1) * 8, :] = sum(power[:, n * LANES : (n + 1) * LANES] for n in range(pixels // LANES))
    total = sum(part_ref[pl.ds(n, count, 8), :] for n in range(8))
    total = jnp.sum(jnp.transpose(total), axis=0, keepdims=True)
    score_ref[...] = total * (1.0 / (height * pixels))


def on_device(volume, tiles, slab_ids, tile_ids, batch_block, images, defocus, inv_sigma2):
    blocks, crossed = slab_ids.shape
    height, length = volume.shape[1:]
    count, _, pixels = images.shape
    kinds = tiles.shape[0]
    devices = lax.axis_size("slab")
    shape = far, wide, cores = grid_of(devices)
    half = devices // 2
    rows = blocks * 2 * height
    slabs, kind_rows, row = slab_ids.T, tile_ids.T, defocus.reshape(1, count)

    def swap(array, offset):
        return lax.ppermute(array, "slab", [(i, i ^ offset) for i in range(devices)])

    vmem = pl.BlockSpec(memory_space=pltpu.VMEM)
    hbm = pl.BlockSpec(memory_space=pltpu.HBM)
    params = pltpu.CompilerParams(vmem_limit_bytes=VMEM_BYTES)
    f32, bf16 = jnp.float32, jnp.bfloat16
    i32 = jnp.int32

    def call(kernel, outs, inputs, operands, scratch, flops, moved, name):
        operands = [
            pltpu.with_memory_space_constraint(x, pltpu.HBM) if spec is hbm else x for x, spec in zip(operands, inputs)
        ]
        return pl.pallas_call(
            kernel,
            out_shape=tuple(jax.ShapeDtypeStruct(s, t) for s, t in outs),
            in_specs=inputs,
            out_specs=(vmem,) * len(outs),
            scratch_shapes=scratch,
            compiler_params=params,
            cost_estimate=pl.CostEstimate(flops=flops, bytes_accessed=moved, transcendentals=0),
            name=name,
        )(*operands)

    def hop(array, offset):
        return jnp.concatenate([array, swap(array, offset)], axis=0)

    along_z = [z * wide * cores for z in reversed(powers(far))]
    offsets = along_z[:1] + [x * cores for x in powers(wide)] + along_z[1:]
    away = [0]
    for offset in offsets[:-1]:
        away += [a ^ offset for a in away]
    gathered = hop(volume, offsets[0])

    batches = batch_block.shape[0]
    sums, wave, images_near, noise_near, place_rows, *route_rows = call(
        functools.partial(sum_kernel, shape, kinds, offsets[-1]),
        [
            ((rows, pixels), bf16),
            (images.shape, f32),
            (images.shape, bf16),
            (inv_sigma2.shape, f32),
            ((devices, blocks), i32),
            ((crossed, batches), i32),
            ((crossed, batches), i32),
        ],
        [hbm] * 7,
        (slabs, kind_rows, batch_block, batch_block.reshape(1, batches), row, inv_sigma2, images),
        [
            pltpu.VMEM((crossed, blocks), i32),
            pltpu.VMEM((crossed, blocks), i32),
            pltpu.SMEM((batches,), i32),
            pltpu.VMEM((1, batches), i32),
            pltpu.VMEM((1, count), f32),
            pltpu.VMEM((2, height, count), f32),
            pltpu.VMEM((2, count, pixels), f32),
            pltpu.VMEM((blocks, 2, height, pixels), f32),
            pltpu.SemaphoreType.DMA((CHUNKS + 6,)),
        ],
        0,
        10 << 20,
        "sums",
    )

    place = (2, height, length)
    place_scratch = [pltpu.SMEM((devices, blocks), i32), pltpu.SemaphoreType.DMA((1,))]
    send, keep, parts = call(
        insert_kernel,
        [((half, *place), bf16), ((half - far, *place), f32), ((kinds * rows + 2 * height, length), f32)],
        [vmem] * 3,
        (place_rows, sums, tiles),
        place_scratch,
        2 * rows * pixels * kinds * length,
        8 << 20,
        "insert",
    )
    send, gathered = lax.optimization_barrier((send, gathered))
    mate = swap(send, 1)
    def along_x(start, stop):
        return (keep[start:stop] + mate[far + start : far + stop].astype(f32)).astype(bf16)

    cut = max(1, far // 2)
    main = [along_x(x * far + cut, (x + 1) * far) for x in range(wide - 1)]
    later = [along_x(x * far, x * far + cut) for x in range(wide - 1)]
    (near,) = call(
        near_kernel, [((far, *place), f32)], [vmem] * 3, (place_rows, parts, mate), place_scratch, 0, 0, "near"
    )
    for offset in offsets[1:-1]:
        came, _ = lax.optimization_barrier((swap(gathered, offset), near))
        gathered = jnp.concatenate([gathered, came], axis=0)
    bit = offsets[-1]
    places = [[(a & (bit - 1)) + a // (2 * bit) * bit for a in [b ^ core for b in away]] for core in (0, 1)]
    flat_rows = kinds * half * height + height if devices * kinds <= batches * crossed else 8
    flat_columns = pixels if flat_rows > 8 else LANES

    def project(route, columns, *base):
        (proj,) = call(
            functools.partial(project_kernel, places),
            [((batches, height, pixels), f32)],
            [vmem] * (4 + len(base)),
            (route, tiles, *columns, *base),
            [
                pltpu.SMEM((crossed, batches), i32),
                pltpu.VMEM((half * height, length), bf16),
                pltpu.VMEM((flat_rows, flat_columns), f32),
                pltpu.SemaphoreType.DMA((1,)),
            ],
            0,
            0,
            "project",
        )
        return proj

    proj = project(route_rows[0], (gathered, swap(gathered, 1)))
    mine = [near[z] for z in range(far)]
    for x in range(1, wide):
        came = swap(main[x - 1], x * cores)
        for z in range(cut, far):
            mine[z] = mine[z] + came[z - cut].astype(f32)
    outgoing = {z: mine[z].astype(bf16) for z in range(cut, far)}
    for x in range(1, wide):
        came, _, _ = lax.optimization_barrier((swap(later[x - 1], x * cores), outgoing[far - 1], proj))
        for z in range(cut):
            mine[z] = mine[z] + came[z].astype(f32)
    outgoing.update({z: mine[z].astype(bf16) for z in range(1, cut)})
    total = mine[0]

    held, _ = lax.optimization_barrier((gathered, later[0]))
    column = swap(held, bit)
    _, column, mirror = lax.optimization_barrier((outgoing[1], column, swap(column, 1)))
    proj = project(route_rows[1], (column, mirror), proj)
    (scores,) = call(
        score_kernel,
        [((1, count), f32)],
        [vmem] * 4,
        (noise_near, proj, wave, images_near),
        [pltpu.VMEM((count * 8, LANES), f32)],
        0,
        0,
        "scores",
    )
    for z in range(1, far):
        came = swap(outgoing[z], z * wide * cores)
        if z >= cut:
            came, scores = lax.optimization_barrier((came, scores))
        total = total + came.astype(f32)
    return scores.reshape(count), total[0:1], total[1:2]


def solution(mesh):
    placed = (
        P(("parts", "slab"), None, None),
        P(),
        P(("parts", "slab"), None),
        P(("parts", "slab"), None),
        P(("parts", "slab")),
        P(("parts", "slab"), None, None),
        P(("parts", "slab")),
        P("parts", None),
    )
    return jax.shard_map(
        on_device,
        mesh=mesh,
        in_specs=placed,
        out_specs=(
            P(("parts", "slab")),
            P(("parts", "slab"), None, None),
            P(("parts", "slab"), None, None),
        ),
        check_vma=False,
    )
```

```python
import functools

import jax
import jax.numpy as jnp
from jax import lax
from jax.experimental import pallas as pl
from jax.experimental.pallas import tpu as pltpu
from jax.sharding import PartitionSpec as P

LANES = 128
CHUNKS = 4
VMEM_BYTES = 24 * 1024 * 1024


def grid_of(devices):
    cores = 2 if devices % 2 == 0 else 1
    chips = devices // cores
    wide = 1
    while (2 * wide) ** 3 <= chips:
        wide *= 2
    return chips // wide, wide, cores


def powers(size):
    return [1 << n for n in range(size.bit_length() - 1)]


def sin_cos(angle):
    turns = jnp.floor(angle * 0.3183098861837907 + 0.5)
    rest = angle - turns * 3.140625
    rest = rest - turns * 9.675025939941406e-4
    rest = rest - turns * 1.5099580252808664e-7
    half = turns * 0.5
    sign = 1.0 - 4.0 * (half - jnp.floor(half))
    sq = rest * rest
    sin = rest * (1.0 + sq * (-1.0 / 6 + sq * (1.0 / 120 + sq * (-1.0 / 5040 + sq * (1.0 / 362880 + sq * (-1.0 / 39916800))))))
    cos = 1.0 + sq * (-0.5 + sq * (1.0 / 24 + sq * (-1.0 / 720 + sq * (1.0 / 40320 + sq * (-1.0 / 3628800 + sq * (1.0 / 479001600))))))
    return sign * sin, sign * cos


def tables(defocus_ref, height, pixels, line_ref, pixel_ref):
    images = defocus_ref.shape[1]
    defocus = defocus_ref[...]
    rows = lax.broadcasted_iota(jnp.int32, (height, images), 0)
    line = ((rows // 2 + 1).astype(jnp.float32) / (height // 2)) ** 2
    line_ref[0], line_ref[1] = sin_cos(defocus * line + 0.3)
    column = jnp.transpose(jnp.broadcast_to(defocus, (LANES, images)))
    part = 32
    lanes = lax.broadcasted_iota(jnp.int32, (part, LANES), 1)
    for n in range(images // part):
        rows = slice(n * part, (n + 1) * part)
        for m in range(pixels // LANES):
            pixel = ((lanes + (m * LANES + 1)).astype(jnp.float32) / pixels) ** 2
            at = slice(m * LANES, (m + 1) * LANES)
            pixel_ref[0, rows, at], pixel_ref[1, rows, at] = sin_cos(column[rows] * pixel)


def contrast_of(line_ref, pixel_ref, i):
    sin_line, cos_line = line_ref[0, :, i : i + 1], line_ref[1, :, i : i + 1]
    return sin_line * pixel_ref[1, i : i + 1, :] + cos_line * pixel_ref[0, i : i + 1, :]


def copies(pairs, sems):
    started = [pltpu.make_async_copy(source, target, sems.at[n]) for n, (source, target) in enumerate(pairs)]
    for copy in started:
        copy.start()
    return started


def row_tables(shape, kinds, height, bit, slab, tile, owner, place_ref, *route_refs):
    far, wide, cores = shape
    devices, blocks = place_ref.shape
    rows, half = blocks * 2 * height, devices // 2
    me = lax.axis_index("slab")
    slot = lax.broadcasted_iota(jnp.int32, (devices, blocks), 0)
    block = lax.broadcasted_iota(jnp.int32, (devices, blocks), 1)
    within = slot & (half - 1)
    core = jnp.where(slot < half, cores - 1, 0)
    named = me ^ (((within & (far - 1)) * wide + within // far) * cores + core)
    place = jnp.full((devices, blocks), kinds * rows, jnp.int32)
    for r in range(slab.shape[0]):
        row = tile[r : r + 1, :] * rows + block * (2 * height)
        place = jnp.where(slab[r : r + 1, :] == named, row, place)
    place_ref[...] = place
    away = me ^ slab
    row = (tile * half + (away & (bit - 1)) + away // (2 * bit) * bit) * height
    for side, route_ref in enumerate(route_refs):
        named = jnp.where((away // bit) & 1 == side, row, kinds * half * height)
        route = jnp.zeros(route_ref.shape, jnp.int32)
        for k in range(blocks):
            route = jnp.where(owner == k, named[:, k : k + 1], route)
        route_ref[...] = route


def sum_kernel(shape, kinds, bit, slab_hbm, tile_hbm, block_hbm, owner_hbm, defocus_hbm, noise_hbm, tiles_hbm, images_hbm,
               sums_ref, wave_ref, tiles_ref, images_ref, noise_ref, place_ref, first_ref, second_ref,
               slab_ref, tile_ref, block_ref, owner_ref, defocus_ref, line_ref, pixel_ref, acc_ref, sems):
    count = images_ref.shape[0]
    part = count // CHUNKS
    small = [(defocus_hbm, defocus_ref), (block_hbm, block_ref), (noise_hbm, noise_ref)]
    small += [(slab_hbm, slab_ref), (tile_hbm, tile_ref), (owner_hbm, owner_ref)]
    large = [(images_hbm.at[pl.ds(n * part, part)], images_ref.at[pl.ds(n * part, part)]) for n in range(CHUNKS)]
    started = copies(small + large, sems)
    last = pltpu.make_async_copy(tiles_hbm, tiles_ref, sems.at[len(started)])
    height, pixels = noise_ref.shape
    batches = block_ref.shape[0]
    size = count // batches
    acc_ref[...] = jnp.zeros_like(acc_ref)
    for copy in started[: len(small)]:
        copy.wait()
    tables(defocus_ref, height, pixels, line_ref, pixel_ref)
    row_tables(shape, kinds, height, bit, slab_ref[...], tile_ref[...], owner_ref[...], place_ref, first_ref, second_ref)
    for b in range(batches):
        if b % (batches // CHUNKS) == 0:
            started[len(small) + b // (batches // CHUNKS)].wait()
        if b == 0:
            last.start()
        data = jnp.zeros((height, pixels), jnp.float32)
        weight = jnp.zeros((height, pixels), jnp.float32)
        for j in range(size):
            i = b * size + j
            wave = contrast_of(line_ref, pixel_ref, i)
            wave_ref[i] = wave
            data = data + wave * images_ref[i].astype(jnp.float32)
            weight = weight + wave * wave
        k = block_ref[b]
        acc_ref[k, 0] = acc_ref[k, 0] + data
        acc_ref[k, 1] = acc_ref[k, 1] + weight
    sums = (acc_ref[...] * noise_ref[...][None, None]).astype(jnp.bfloat16)
    sums_ref[...] = sums.reshape(sums_ref.shape)
    last.wait()


def fill(ref, start, place_ref, parts_ref, mate_ref=None):
    sides, height, length = ref.shape[1:]

    def step(slot, carry):
        acc = None
        for k in range(place_ref.shape[1]):
            at = pl.multiple_of(place_ref[start + slot, k], sides * height)
            part = parts_ref[pl.ds(at, sides * height), :]
            acc = part if acc is None else acc + part
        acc = acc.reshape(sides, height, length)
        if mate_ref is not None:
            acc = acc + mate_ref[slot].astype(jnp.float32)
        ref[slot] = acc.astype(ref.dtype)
        return carry

    lax.fori_loop(0, ref.shape[0], step, 0)


def insert_kernel(far, cut, place_vmem, sums_ref, tiles_ref, send_ref, far_ref, parts_ref, place_ref, sems):
    (started,) = copies([(place_vmem, place_ref)], sems)
    kinds = tiles_ref.shape[0]
    rows = sums_ref.shape[0]
    zeros = parts_ref.shape[0] - kinds * rows
    parts_ref[kinds * rows :, :] = jnp.zeros((zeros, parts_ref.shape[1]), jnp.float32)
    for t in range(kinds):
        parts_ref[t * rows : (t + 1) * rows, :] = lax.dot_general(
            sums_ref[...], tiles_ref[t], (((1,), (1,)), ((), ())), preferred_element_type=jnp.float32
        )
    started.wait()
    fill(send_ref, 0, place_ref, parts_ref)
    half, size = place_ref.shape[0] // 2, far - cut
    for x in range(far_ref.shape[0] // size):
        fill(far_ref.at[pl.ds(x * size, size)], half + (x + 1) * far + cut, place_ref, parts_ref)


def near_kernel(cut, place_vmem, parts_ref, mate_ref, later_ref, near_ref, place_ref, sems):
    (started,) = copies([(place_vmem, place_ref)], sems)
    started.wait()
    half, far = place_ref.shape[0] // 2, near_ref.shape[0]
    for x in range(later_ref.shape[0] // cut):
        mates = mate_ref.at[pl.ds((x + 1) * far, cut)]
        fill(later_ref.at[pl.ds(x * cut, cut)], half + (x + 1) * far, place_ref, parts_ref, mates)
    fill(near_ref, half, place_ref, parts_ref, mate_ref)


def project_kernel(places, route_vmem, tiles_ref, *refs):
    columns, refs = refs[: len(places)], refs[len(places) :]
    *base, proj_ref, route_ref, lines_ref, flat_ref, sems = refs
    (started,) = copies([(route_vmem, route_ref)], sems)
    crossed, batches = route_ref.shape
    kinds = tiles_ref.shape[0]
    height = columns[0].shape[1]
    rows = lines_ref.shape[0]
    dense = flat_ref.shape[0] > kinds * rows
    for ref, slots in zip(columns, places):
        for n, slot in enumerate(slots):
            lines_ref[slot * height : (slot + 1) * height, :] = ref[n]
    if dense:
        for t in range(kinds):
            flat_ref[t * rows : (t + 1) * rows, :] = jnp.dot(lines_ref[...], tiles_ref[t], preferred_element_type=jnp.float32)
        flat_ref[kinds * rows :, :] = jnp.zeros((height, flat_ref.shape[1]), jnp.float32)
    started.wait()

    def project(b, carry):
        acc = base[0][b] if base else None
        for r in range(crossed):
            at = route_ref[r, b]
            if dense:
                part = flat_ref[pl.ds(pl.multiple_of(at, height), height), :]
            else:
                t, from_row = jnp.minimum(at // rows, kinds - 1), pl.multiple_of(lax.rem(at, rows), height)
                part = jnp.dot(lines_ref[pl.ds(from_row, height), :], tiles_ref[t], preferred_element_type=jnp.float32)
                part = part * jnp.where(at < kinds * rows, 1.0, 0.0)
            acc = part if acc is None else acc + part
        proj_ref[b] = acc
        return carry

    lax.fori_loop(0, batches, project, 0, unroll=dense)


def score_kernel(noise_ref, proj_ref, wave_ref, images_ref, score_ref, part_ref):
    height, pixels = noise_ref.shape
    count = images_ref.shape[0]
    size = count // proj_ref.shape[0]
    noise = noise_ref[...]
    for b in range(count // size):
        proj = proj_ref[b]
        for j in range(size):
            i = b * size + j
            residual = images_ref[i].astype(jnp.float32) - wave_ref[i] * proj
            power = residual * residual * noise
            power = sum(power[n * 8 : (n + 1) * 8] for n in range(height // 8))
            part_ref[i * 8 : (i + 1) * 8, :] = sum(power[:, n * LANES : (n + 1) * LANES] for n in range(pixels // LANES))
    total = sum(part_ref[pl.ds(n, count, 8), :] for n in range(8))
    total = jnp.sum(jnp.transpose(total), axis=0, keepdims=True)
    score_ref[...] = total * (1.0 / (height * pixels))


def on_device(volume, tiles, slab_ids, tile_ids, batch_block, images, defocus, inv_sigma2):
    blocks, crossed = slab_ids.shape
    height, length = volume.shape[1:]
    count, _, pixels = images.shape
    kinds = tiles.shape[0]
    devices = lax.axis_size("slab")
    shape = far, wide, cores = grid_of(devices)
    half = devices // 2
    rows = blocks * 2 * height
    slabs, kind_rows, row = slab_ids.T, tile_ids.T, defocus.reshape(1, count)

    def swap(array, offset):
        return lax.ppermute(array, "slab", [(i, i ^ offset) for i in range(devices)])

    vmem = pl.BlockSpec(memory_space=pltpu.VMEM)
    hbm = pl.BlockSpec(memory_space=pltpu.HBM)
    params = pltpu.CompilerParams(vmem_limit_bytes=VMEM_BYTES)
    f32, bf16 = jnp.float32, jnp.bfloat16
    i32 = jnp.int32

    def call(kernel, outs, inputs, operands, scratch, flops, moved, name):
        operands = [
            pltpu.with_memory_space_constraint(x, pltpu.HBM) if spec is hbm else x for x, spec in zip(operands, inputs)
        ]
        return pl.pallas_call(
            kernel,
            out_shape=tuple(jax.ShapeDtypeStruct(s, t) for s, t in outs),
            in_specs=inputs,
            out_specs=(vmem,) * len(outs),
            scratch_shapes=scratch,
            compiler_params=params,
            cost_estimate=pl.CostEstimate(flops=flops, bytes_accessed=moved, transcendentals=0),
            name=name,
        )(*operands)

    def hop(array, offset):
        return jnp.concatenate([array, swap(array, offset)], axis=0)

    along_z = [z * wide * cores for z in reversed(powers(far))]
    offsets = along_z[:1] + [x * cores for x in powers(wide)] + along_z[1:]
    away = [0]
    for offset in offsets[:-1]:
        away += [a ^ offset for a in away]
    gathered = hop(volume, offsets[0])

    batches = batch_block.shape[0]
    sums, wave, tiles_near, images_near, noise_near, place_rows, *route_rows = call(
        functools.partial(sum_kernel, shape, kinds, offsets[-1]),
        [
            ((rows, pixels), bf16),
            (images.shape, f32),
            (tiles.shape, bf16),
            (images.shape, bf16),
            (inv_sigma2.shape, f32),
            ((devices, blocks), i32),
            ((crossed, batches), i32),
            ((crossed, batches), i32),
        ],
        [hbm] * 8,
        (slabs, kind_rows, batch_block, batch_block.reshape(1, batches), row, inv_sigma2, tiles, images),
        [
            pltpu.VMEM((crossed, blocks), i32),
            pltpu.VMEM((crossed, blocks), i32),
            pltpu.SMEM((batches,), i32),
            pltpu.VMEM((1, batches), i32),
            pltpu.VMEM((1, count), f32),
            pltpu.VMEM((2, height, count), f32),
            pltpu.VMEM((2, count, pixels), f32),
            pltpu.VMEM((blocks, 2, height, pixels), f32),
            pltpu.SemaphoreType.DMA((CHUNKS + 7,)),
        ],
        0,
        10 << 20,
        "sums",
    )

    place = (2, height, length)
    place_scratch = [pltpu.SMEM((devices, blocks), i32), pltpu.SemaphoreType.DMA((1,))]
    cut = max(1, far // 2)
    send, keep, parts = call(
        functools.partial(insert_kernel, far, cut),
        [((half, *place), bf16), (((wide - 1) * (far - cut), *place), f32), ((kinds * rows + 2 * height, length), f32)],
        [vmem] * 3,
        (place_rows, sums, tiles_near),
        place_scratch,
        2 * rows * pixels * kinds * length,
        8 << 20,
        "insert",
    )
    send, gathered = lax.optimization_barrier((send, gathered))
    mate = swap(send, 1)
    main = []
    for x in range(wide - 1):
        came = mate[(x + 1) * far + cut : (x + 2) * far].astype(f32)
        main.append((keep[x * (far - cut) : (x + 1) * (far - cut)] + came).astype(bf16))
    later, near = call(
        functools.partial(near_kernel, cut),
        [(((wide - 1) * cut, *place), bf16), ((far, *place), f32)],
        [vmem] * 3,
        (place_rows, parts, mate),
        place_scratch,
        0,
        0,
        "near",
    )
    later = [later[x * cut : (x + 1) * cut] for x in range(wide - 1)]
    for offset in offsets[1:-1]:
        came, _ = lax.optimization_barrier((swap(gathered, offset), near))
        gathered = jnp.concatenate([gathered, came], axis=0)
    bit = offsets[-1]
    places = [[(a & (bit - 1)) + a // (2 * bit) * bit for a in [b ^ core for b in away]] for core in (0, 1)]
    flat_rows = kinds * half * height + height if devices * kinds <= batches * crossed else 8
    flat_columns = pixels if flat_rows > 8 else LANES

    def project(route, columns, *base):
        (proj,) = call(
            functools.partial(project_kernel, places),
            [((batches, height, pixels), f32)],
            [vmem] * (4 + len(base)),
            (route, tiles_near, *columns, *base),
            [
                pltpu.SMEM((crossed, batches), i32),
                pltpu.VMEM((half * height, length), bf16),
                pltpu.VMEM((flat_rows, flat_columns), f32),
                pltpu.SemaphoreType.DMA((1,)),
            ],
            0,
            0,
            "project",
        )
        return proj

    proj = project(route_rows[0], (gathered, swap(gathered, 1)))
    mine = [near[z] for z in range(far)]
    for x in range(1, wide):
        came = swap(main[x - 1], x * cores)
        for z in range(cut, far):
            mine[z] = mine[z] + came[z - cut].astype(f32)
    outgoing = {z: mine[z].astype(bf16) for z in range(cut, far)}
    for x in range(1, wide):
        came, _, _ = lax.optimization_barrier((swap(later[x - 1], x * cores), outgoing[far - 1], proj))
        for z in range(cut):
            mine[z] = mine[z] + came[z].astype(f32)
    outgoing.update({z: mine[z].astype(bf16) for z in range(1, cut)})
    total = mine[0]

    held, _ = lax.optimization_barrier((gathered, later[0]))
    column = swap(held, bit)
    _, column, mirror = lax.optimization_barrier((outgoing[1], column, swap(column, 1)))
    proj = project(route_rows[1], (column, mirror), proj)
    (scores,) = call(
        score_kernel,
        [((1, count), f32)],
        [vmem] * 4,
        (noise_near, proj, wave, images_near),
        [pltpu.VMEM((count * 8, LANES), f32)],
        0,
        0,
        "scores",
    )
    for z in range(1, far):
        came = swap(outgoing[z], z * wide * cores)
        if z >= cut:
            came, scores = lax.optimization_barrier((came, scores))
        total = total + came.astype(f32)
    return scores.reshape(count), total[0:1], total[1:2]


def solution(mesh):
    placed = (
        P(("parts", "slab"), None, None),
        P(),
        P(("parts", "slab"), None),
        P(("parts", "slab"), None),
        P(("parts", "slab")),
        P(("parts", "slab"), None, None),
        P(("parts", "slab")),
        P("parts", None),
    )
    return jax.shard_map(
        on_device,
        mesh=mesh,
        in_specs=placed,
        out_specs=(
            P(("parts", "slab")),
            P(("parts", "slab"), None, None),
            P(("parts", "slab"), None, None),
        ),
        check_vma=False,
    )
```

```python
import functools

import jax
import jax.numpy as jnp
from jax import lax
from jax.experimental import pallas as pl
from jax.experimental.pallas import tpu as pltpu
from jax.sharding import PartitionSpec as P

LANES = 128
CHUNKS = 4
VMEM_BYTES = 24 * 1024 * 1024


def grid_of(devices):
    cores = 2 if devices % 2 == 0 else 1
    chips = devices // cores
    wide = 1
    while (2 * wide) ** 3 <= chips:
        wide *= 2
    return chips // wide, wide, cores


def powers(size):
    return [1 << n for n in range(size.bit_length() - 1)]


def sin_cos(angle):
    turns = jnp.floor(angle * 0.3183098861837907 + 0.5)
    rest = angle - turns * 3.140625
    rest = rest - turns * 9.675025939941406e-4
    rest = rest - turns * 1.5099580252808664e-7
    half = turns * 0.5
    sign = 1.0 - 4.0 * (half - jnp.floor(half))
    sq = rest * rest
    sin = rest * (1.0 + sq * (-1.0 / 6 + sq * (1.0 / 120 + sq * (-1.0 / 5040 + sq * (1.0 / 362880 + sq * (-1.0 / 39916800))))))
    cos = 1.0 + sq * (-0.5 + sq * (1.0 / 24 + sq * (-1.0 / 720 + sq * (1.0 / 40320 + sq * (-1.0 / 3628800 + sq * (1.0 / 479001600))))))
    return sign * sin, sign * cos


def tables(defocus_ref, height, pixels, line_ref, pixel_ref):
    images = defocus_ref.shape[1]
    defocus = defocus_ref[...]
    rows = lax.broadcasted_iota(jnp.int32, (height, images), 0)
    line = ((rows // 2 + 1).astype(jnp.float32) / (height // 2)) ** 2
    line_ref[0], line_ref[1] = sin_cos(defocus * line + 0.3)
    column = jnp.transpose(jnp.broadcast_to(defocus, (LANES, images)))
    part = 32
    lanes = lax.broadcasted_iota(jnp.int32, (part, LANES), 1)
    for n in range(images // part):
        rows = slice(n * part, (n + 1) * part)
        for m in range(pixels // LANES):
            pixel = ((lanes + (m * LANES + 1)).astype(jnp.float32) / pixels) ** 2
            at = slice(m * LANES, (m + 1) * LANES)
            pixel_ref[0, rows, at], pixel_ref[1, rows, at] = sin_cos(column[rows] * pixel)


def contrast_of(line_ref, pixel_ref, i):
    sin_line, cos_line = line_ref[0, :, i : i + 1], line_ref[1, :, i : i + 1]
    return sin_line * pixel_ref[1, i : i + 1, :] + cos_line * pixel_ref[0, i : i + 1, :]


def copies(pairs, sems):
    started = [pltpu.make_async_copy(source, target, sems.at[n]) for n, (source, target) in enumerate(pairs)]
    for copy in started:
        copy.start()
    return started


def row_tables(shape, kinds, height, bit, slab, tile, owner, place_ref, *route_refs):
    far, wide, cores = shape
    devices, blocks = place_ref.shape
    rows, half = blocks * 2 * height, devices // 2
    me = lax.axis_index("slab")
    slot = lax.broadcasted_iota(jnp.int32, (devices, blocks), 0)
    block = lax.broadcasted_iota(jnp.int32, (devices, blocks), 1)
    within = slot & (half - 1)
    core = jnp.where(slot < half, cores - 1, 0)
    named = me ^ (((within & (far - 1)) * wide + within // far) * cores + core)
    place = jnp.full((devices, blocks), kinds * rows, jnp.int32)
    for r in range(slab.shape[0]):
        row = tile[r : r + 1, :] * rows + block * (2 * height)
        place = jnp.where(slab[r : r + 1, :] == named, row, place)
    place_ref[...] = place
    away = me ^ slab
    row = (tile * half + (away & (bit - 1)) + away // (2 * bit) * bit) * height
    for side, route_ref in enumerate(route_refs):
        named = jnp.where((away // bit) & 1 == side, row, kinds * half * height)
        route = jnp.zeros(route_ref.shape, jnp.int32)
        for k in range(blocks):
            route = jnp.where(owner == k, named[:, k : k + 1], route)
        route_ref[...] = route


def sum_kernel(shape, kinds, bit, slab_hbm, tile_hbm, block_hbm, owner_hbm, defocus_hbm, noise_hbm, tiles_hbm, images_hbm,
               sums_ref, wave_ref, tiles_ref, images_ref, noise_ref, place_ref, first_ref, second_ref,
               slab_ref, tile_ref, block_ref, owner_ref, defocus_ref, line_ref, pixel_ref, acc_ref, sems):
    count = images_ref.shape[0]
    part = count // CHUNKS
    small = [(defocus_hbm, defocus_ref), (block_hbm, block_ref), (noise_hbm, noise_ref)]
    small += [(slab_hbm, slab_ref), (tile_hbm, tile_ref), (owner_hbm, owner_ref)]
    large = [(images_hbm.at[pl.ds(n * part, part)], images_ref.at[pl.ds(n * part, part)]) for n in range(CHUNKS)]
    started = copies(small + large, sems)
    last = pltpu.make_async_copy(tiles_hbm, tiles_ref, sems.at[len(started)])
    height, pixels = noise_ref.shape
    batches = block_ref.shape[0]
    size = count // batches
    acc_ref[...] = jnp.zeros_like(acc_ref)
    for copy in started[: len(small)]:
        copy.wait()
    tables(defocus_ref, height, pixels, line_ref, pixel_ref)
    row_tables(shape, kinds, height, bit, slab_ref[...], tile_ref[...], owner_ref[...], place_ref, first_ref, second_ref)
    for b in range(batches):
        if b % (batches // CHUNKS) == 0:
            started[len(small) + b // (batches // CHUNKS)].wait()
        if b == 0:
            last.start()
        data = jnp.zeros((height, pixels), jnp.float32)
        weight = jnp.zeros((height, pixels), jnp.float32)
        for j in range(size):
            i = b * size + j
            wave = contrast_of(line_ref, pixel_ref, i)
            wave_ref[i] = wave
            data = data + wave * images_ref[i].astype(jnp.float32)
            weight = weight + wave * wave
        k = block_ref[b]
        acc_ref[k, 0] = acc_ref[k, 0] + data
        acc_ref[k, 1] = acc_ref[k, 1] + weight
    sums = (acc_ref[...] * noise_ref[...][None, None]).astype(jnp.bfloat16)
    sums_ref[...] = sums.reshape(sums_ref.shape)
    last.wait()


def fill(ref, start, place_ref, parts_ref, mate_ref=None):
    sides, height, length = ref.shape[1:]

    def step(slot, carry):
        acc = None
        for k in range(place_ref.shape[1]):
            at = pl.multiple_of(place_ref[start + slot, k], sides * height)
            part = parts_ref[pl.ds(at, sides * height), :]
            acc = part if acc is None else acc + part
        acc = acc.reshape(sides, height, length)
        if mate_ref is not None:
            acc = acc + mate_ref[slot].astype(jnp.float32)
        ref[slot] = acc.astype(ref.dtype)
        return carry

    lax.fori_loop(0, ref.shape[0], step, 0, unroll=2)


def insert_kernel(place_vmem, sums_ref, tiles_ref, send_ref, far_ref, parts_ref, place_ref, sems):
    (started,) = copies([(place_vmem, place_ref)], sems)
    kinds = tiles_ref.shape[0]
    rows = sums_ref.shape[0]
    zeros = parts_ref.shape[0] - kinds * rows
    parts_ref[kinds * rows :, :] = jnp.zeros((zeros, parts_ref.shape[1]), jnp.float32)
    for t in range(kinds):
        parts_ref[t * rows : (t + 1) * rows, :] = lax.dot_general(
            sums_ref[...], tiles_ref[t], (((1,), (1,)), ((), ())), preferred_element_type=jnp.float32
        )
    started.wait()
    fill(send_ref, 0, place_ref, parts_ref)
    devices = place_ref.shape[0]
    fill(far_ref, devices - far_ref.shape[0], place_ref, parts_ref)


def near_kernel(place_vmem, parts_ref, mate_ref, near_ref, place_ref, sems):
    (started,) = copies([(place_vmem, place_ref)], sems)
    started.wait()
    fill(near_ref, place_ref.shape[0] // 2, place_ref, parts_ref, mate_ref)


def project_kernel(places, route_vmem, tiles_ref, *refs):
    columns, refs = refs[: len(places)], refs[len(places) :]
    *base, proj_ref, route_ref, lines_ref, flat_ref, sems = refs
    (started,) = copies([(route_vmem, route_ref)], sems)
    crossed, batches = route_ref.shape
    kinds = tiles_ref.shape[0]
    height = columns[0].shape[1]
    rows = lines_ref.shape[0]
    dense = flat_ref.shape[0] > kinds * rows
    for ref, slots in zip(columns, places):
        for n, slot in enumerate(slots):
            lines_ref[slot * height : (slot + 1) * height, :] = ref[n]
    if dense:
        for t in range(kinds):
            flat_ref[t * rows : (t + 1) * rows, :] = jnp.dot(lines_ref[...], tiles_ref[t], preferred_element_type=jnp.float32)
        flat_ref[kinds * rows :, :] = jnp.zeros((height, flat_ref.shape[1]), jnp.float32)
    started.wait()

    def project(b, carry):
        acc = base[0][b] if base else None
        for r in range(crossed):
            at = route_ref[r, b]
            if dense:
                part = flat_ref[pl.ds(pl.multiple_of(at, height), height), :]
            else:
                t, from_row = jnp.minimum(at // rows, kinds - 1), pl.multiple_of(lax.rem(at, rows), height)
                part = jnp.dot(lines_ref[pl.ds(from_row, height), :], tiles_ref[t], preferred_element_type=jnp.float32)
                part = part * jnp.where(at < kinds * rows, 1.0, 0.0)
            acc = part if acc is None else acc + part
        proj_ref[b] = acc
        return carry

    lax.fori_loop(0, batches, project, 0, unroll=dense)


def score_kernel(noise_ref, proj_ref, wave_ref, images_ref, score_ref, part_ref):
    height, pixels = noise_ref.shape
    count = images_ref.shape[0]
    size = count // proj_ref.shape[0]
    noise = noise_ref[...]
    for b in range(count // size):
        proj = proj_ref[b]
        for j in range(size):
            i = b * size + j
            residual = images_ref[i].astype(jnp.float32) - wave_ref[i] * proj
            power = residual * residual * noise
            power = sum(power[n * 8 : (n + 1) * 8] for n in range(height // 8))
            part_ref[i * 8 : (i + 1) * 8, :] = sum(power[:, n * LANES : (n + 1) * LANES] for n in range(pixels // LANES))
    total = sum(part_ref[pl.ds(n, count, 8), :] for n in range(8))
    total = jnp.sum(jnp.transpose(total), axis=0, keepdims=True)
    score_ref[...] = total * (1.0 / (height * pixels))


def on_device(volume, tiles, slab_ids, tile_ids, batch_block, images, defocus, inv_sigma2):
    blocks, crossed = slab_ids.shape
    height, length = volume.shape[1:]
    count, _, pixels = images.shape
    kinds = tiles.shape[0]
    devices = lax.axis_size("slab")
    shape = far, wide, cores = grid_of(devices)
    half = devices // 2
    rows = blocks * 2 * height
    slabs, kind_rows, row = slab_ids.T, tile_ids.T, defocus.reshape(1, count)

    def swap(array, offset):
        return lax.ppermute(array, "slab", [(i, i ^ offset) for i in range(devices)])

    vmem = pl.BlockSpec(memory_space=pltpu.VMEM)
    hbm = pl.BlockSpec(memory_space=pltpu.HBM)
    params = pltpu.CompilerParams(vmem_limit_bytes=VMEM_BYTES)
    f32, bf16 = jnp.float32, jnp.bfloat16
    i32 = jnp.int32

    def call(kernel, outs, inputs, operands, scratch, flops, moved, name):
        operands = [
            pltpu.with_memory_space_constraint(x, pltpu.HBM) if spec is hbm else x for x, spec in zip(operands, inputs)
        ]
        return pl.pallas_call(
            kernel,
            out_shape=tuple(jax.ShapeDtypeStruct(s, t) for s, t in outs),
            in_specs=inputs,
            out_specs=(vmem,) * len(outs),
            scratch_shapes=scratch,
            compiler_params=params,
            cost_estimate=pl.CostEstimate(flops=flops, bytes_accessed=moved, transcendentals=0),
            name=name,
        )(*operands)

    def hop(array, offset):
        return jnp.concatenate([array, swap(array, offset)], axis=0)

    along_z = [z * wide * cores for z in reversed(powers(far))]
    offsets = along_z[:1] + [x * cores for x in powers(wide)] + along_z[1:]
    away = [0]
    for offset in offsets[:-1]:
        away += [a ^ offset for a in away]
    gathered = hop(volume, offsets[0])

    batches = batch_block.shape[0]
    sums, wave, tiles_near, images_near, noise_near, place_rows, *route_rows = call(
        functools.partial(sum_kernel, shape, kinds, offsets[-1]),
        [
            ((rows, pixels), bf16),
            (images.shape, f32),
            (tiles.shape, bf16),
            (images.shape, bf16),
            (inv_sigma2.shape, f32),
            ((devices, blocks), i32),
            ((crossed, batches), i32),
            ((crossed, batches), i32),
        ],
        [hbm] * 8,
        (slabs, kind_rows, batch_block, batch_block.reshape(1, batches), row, inv_sigma2, tiles, images),
        [
            pltpu.VMEM((crossed, blocks), i32),
            pltpu.VMEM((crossed, blocks), i32),
            pltpu.SMEM((batches,), i32),
            pltpu.VMEM((1, batches), i32),
            pltpu.VMEM((1, count), f32),
            pltpu.VMEM((2, height, count), f32),
            pltpu.VMEM((2, count, pixels), f32),
            pltpu.VMEM((blocks, 2, height, pixels), f32),
            pltpu.SemaphoreType.DMA((CHUNKS + 7,)),
        ],
        0,
        10 << 20,
        "sums",
    )

    place = (2, height, length)
    place_scratch = [pltpu.SMEM((devices, blocks), i32), pltpu.SemaphoreType.DMA((1,))]
    send, keep, parts = call(
        insert_kernel,
        [((half, *place), bf16), ((half - far, *place), f32), ((kinds * rows + 2 * height, length), f32)],
        [vmem] * 3,
        (place_rows, sums, tiles_near),
        place_scratch,
        2 * rows * pixels * kinds * length,
        8 << 20,
        "insert",
    )
    send, gathered = lax.optimization_barrier((send, gathered))
    mate = swap(send, 1)
    def along_x(start, stop):
        return (keep[start:stop] + mate[far + start : far + stop].astype(f32)).astype(bf16)

    cut = max(1, far // 2)
    main = [along_x(x * far + cut, (x + 1) * far) for x in range(wide - 1)]
    later = [along_x(x * far, x * far + cut) for x in range(wide - 1)]
    (near,) = call(
        near_kernel, [((far, *place), f32)], [vmem] * 3, (place_rows, parts, mate), place_scratch, 0, 0, "near"
    )
    for offset in offsets[1:-1]:
        came, _ = lax.optimization_barrier((swap(gathered, offset), near))
        gathered = jnp.concatenate([gathered, came], axis=0)
    bit = offsets[-1]
    places = [[(a & (bit - 1)) + a // (2 * bit) * bit for a in [b ^ core for b in away]] for core in (0, 1)]
    flat_rows = kinds * half * height + height if devices * kinds <= batches * crossed else 8
    flat_columns = pixels if flat_rows > 8 else LANES

    def project(route, columns, *base):
        (proj,) = call(
            functools.partial(project_kernel, places),
            [((batches, height, pixels), f32)],
            [vmem] * (4 + len(base)),
            (route, tiles_near, *columns, *base),
            [
                pltpu.SMEM((crossed, batches), i32),
                pltpu.VMEM((half * height, length), bf16),
                pltpu.VMEM((flat_rows, flat_columns), f32),
                pltpu.SemaphoreType.DMA((1,)),
            ],
            0,
            0,
            "project",
        )
        return proj

    proj = project(route_rows[0], (gathered, swap(gathered, 1)))
    mine = [near[z] for z in range(far)]
    for x in range(1, wide):
        came = swap(main[x - 1], x * cores)
        for z in range(cut, far):
            mine[z] = mine[z] + came[z - cut].astype(f32)
    outgoing = {z: mine[z].astype(bf16) for z in range(cut, far)}
    for x in range(1, wide):
        came, _, _ = lax.optimization_barrier((swap(later[x - 1], x * cores), outgoing[far - 1], proj))
        for z in range(cut):
            mine[z] = mine[z] + came[z].astype(f32)
    outgoing.update({z: mine[z].astype(bf16) for z in range(1, cut)})
    total = mine[0]

    held, _ = lax.optimization_barrier((gathered, later[0]))
    column = swap(held, bit)
    _, column, mirror = lax.optimization_barrier((outgoing[1], column, swap(column, 1)))
    proj = project(route_rows[1], (column, mirror), proj)
    (scores,) = call(
        score_kernel,
        [((1, count), f32)],
        [vmem] * 4,
        (noise_near, proj, wave, images_near),
        [pltpu.VMEM((count * 8, LANES), f32)],
        0,
        0,
        "scores",
    )
    for z in range(1, far):
        came = swap(outgoing[z], z * wide * cores)
        if z >= cut:
            came, scores = lax.optimization_barrier((came, scores))
        total = total + came.astype(f32)
    return scores.reshape(count), total[0:1], total[1:2]


def solution(mesh):
    placed = (
        P(("parts", "slab"), None, None),
        P(),
        P(("parts", "slab"), None),
        P(("parts", "slab"), None),
        P(("parts", "slab")),
        P(("parts", "slab"), None, None),
        P(("parts", "slab")),
        P("parts", None),
    )
    return jax.shard_map(
        on_device,
        mesh=mesh,
        in_specs=placed,
        out_specs=(
            P(("parts", "slab")),
            P(("parts", "slab"), None, None),
            P(("parts", "slab"), None, None),
        ),
        check_vma=False,
    )
```
